32 devices in a mesh: dp: 4 (over z), seq: 4 (over x, core), blk: 2 (over y).
Axes of the slice: x: 2, y: 2, z: 4, core: 2. Of those that a mesh axis runs over, the one named last changes fastest.
Arguments:
- tokens: bfloat16 [4096, 768], P(('dp', 'seq', 'blk')), may hold values from -6 to 6
- cotangent: bfloat16 [4096, 768], P(('dp', 'seq', 'blk')), may hold values from -6 to 6
- qkv_weight: float32 [768, 2304], P(('dp', 'seq', 'blk')), may hold values from -0.21875 to 0.21875
- proj_weight: float32 [768, 768], P(('dp', 'seq', 'blk')), may hold values from -0.625 to 0.625
- expand_weight: float32 [768, 3072], P(('dp', 'seq', 'blk')), may hold values from -0.21875 to 0.21875
- shrink_weight: float32 [3072, 768], P(('dp', 'seq', 'blk')), may hold values from -0.109375 to 0.109375
- small_params: float32 [12, 768], P(None, ('dp', 'seq', 'blk')), may hold values from -0.6 to 1.5, as said below
- qkv_first: float32 [768, 2304], P(('dp', 'seq', 'blk')), may hold values from -12 to 12
- proj_first: float32 [768, 768], P(('dp', 'seq', 'blk')), may hold values from -12 to 12
- expand_first: float32 [768, 3072], P(('dp', 'seq', 'blk')), may hold values from -16 to 16
- shrink_first: float32 [3072, 768], P(('dp', 'seq', 'blk')), may hold values from -24 to 24
- small_first: float32 [12, 768], P(None, ('dp', 'seq', 'blk')), may hold values from -20 to 20
- qkv_second: float32 [768, 2304], P(('dp', 'seq', 'blk')), may hold values from 19.6608 to 77.824
- proj_second: float32 [768, 768], P(('dp', 'seq', 'blk')), may hold values from 19.6608 to 77.824
- expand_second: float32 [768, 3072], P(('dp', 'seq', 'blk')), may hold values from 26.624 to 106.496
- shrink_second: float32 [3072, 768], P(('dp', 'seq', 'blk')), may hold values from 77.824 to 311.296
- small_second: float32 [12, 768], P(None, ('dp', 'seq', 'blk')), may hold values from 53.248 to 217.088
Outputs:
- block_out: float32 [4096, 768], P(('dp', 'seq', 'blk'))
- token_grad: float32 [4096, 768], P(('dp', 'seq', 'blk'))
- qkv_moment: float32 [768, 2304], P(('dp', 'seq', 'blk'))
- qkv_variance: float32 [768, 2304], P(('dp', 'seq', 'blk'))
- qkv_updated: float32 [768, 2304], P(('dp', 'seq', 'blk'))
- proj_moment: float32 [768, 768], P(('dp', 'seq', 'blk'))
- proj_variance: float32 [768, 768], P(('dp', 'seq', 'blk'))
- proj_updated: float32 [768, 768], P(('dp', 'seq', 'blk'))
- expand_moment: float32 [768, 3072], P(('dp', 'seq', 'blk'))
- expand_variance: float32 [768, 3072], P(('dp', 'seq', 'blk'))
- expand_updated: float32 [768, 3072], P(('dp', 'seq', 'blk'))
- shrink_moment: float32 [3072, 768], P(('dp', 'seq', 'blk'))
- shrink_variance: float32 [3072, 768], P(('dp', 'seq', 'blk'))
- shrink_updated: float32 [3072, 768], P(('dp', 'seq', 'blk'))
- small_moment: float32 [12, 768], P(None, ('dp', 'seq', 'blk'))
- small_variance: float32 [12, 768], P(None, ('dp', 'seq', 'blk'))
- small_updated: float32 [12, 768], P(None, ('dp', 'seq', 'blk'))
The draws below stay inside these ranges and needn't reach their ends.
Inputs may be any that keep to these rules, and one draw needn't show every extreme that they name: `small_params`: rows 0 and 5 are gains near one, every other row a bias of moderate size.
All inputs are finite; a program needn't handle non-finite values.
Results may differ from the reference program's by a relative error of at most 0.011.
Values may be sent and summed in bfloat16 or wider, within the bound.
No kernel may reach another device: no remote copies, remote signals or barrier semaphores. Data moves between devices by JAX's collectives and lax.ppermute only.
A program may use at most 192 MiB of HBM per device.

```python
import math
import jax
import jax.numpy as jnp
from jax import lax

D = 768
HEADS = 12
HEAD = 64
FF = 3072
STEP = 10
LEN = 1024
SEQS = 4
TOKENS = 4096


def draw_small_params(key, part):
    key = jax.random.fold_in(key, 7)
    row_count = 8 + FF // D
    gain_key, bias_key = jax.random.split(key)
    gains = jnp.clip(1.0 + 0.15 * jax.random.normal(gain_key, (row_count, D), jnp.float32), 0.5, 1.5)
    biases = jnp.clip(0.2 * jax.random.normal(bias_key, (row_count, D), jnp.float32), -0.6, 0.6)
    row_index = jnp.arange(row_count)[:, None]
    gain_rows = (row_index == 0) | (row_index == 5)
    return jnp.where(gain_rows, gains, biases)


def block_scale(own_key, dims, cuts, smallest, high):
    factor_of, own = 1.0, jax.random.fold_in(own_key, 6)
    for axis_at, blocks in cuts:
        steps = jnp.exp(jax.random.uniform(jax.random.fold_in(own, axis_at), (blocks,), jnp.float32, smallest / len(cuts), high / len(cuts)))
        factor_of = factor_of * jnp.repeat(steps, dims[axis_at] // blocks).reshape([-1 if axis == axis_at else 1 for axis in range(len(dims))])
    return factor_of


def centred(key, dims, scale, reach, pieces=(), held_as=jnp.bfloat16):
    entries = jax.random.normal(key, dims, jnp.float32) * scale
    if len(pieces) > 0:
        entries = block_scale(key, dims, pieces, -0.22, 0.18) * entries
    return jnp.clip(entries, min=-reach, max=reach).astype(held_as)


def setup_inputs(seed: int = 0) -> dict:
    seeds = jax.random.split(jax.random.key(seed), 18)
    return {
        "tokens": centred(seeds[0], (TOKENS, D), 1.0, 6.0, ((0, 32),)),
        "cotangent": centred(seeds[1], (TOKENS, D), 1.0, 6.0, ((0, 32),)),
        "qkv_weight": centred(seeds[2], (D, 3 * D), D ** -0.5, 0.21875, ((0, 32),), jnp.float32),
        "proj_weight": centred(seeds[3], (D, D), (D // 8) ** -0.5, 0.625, ((0, 32),), jnp.float32),
        "expand_weight": centred(seeds[4], (D, FF), D ** -0.5, 0.21875, ((0, 32),), jnp.float32),
        "shrink_weight": centred(seeds[5], (FF, D), FF ** -0.5, 0.109375, ((0, 32),), jnp.float32),
        "small_params": draw_small_params(jax.random.fold_in(seeds[17], 71), 0),
        "qkv_first": centred(seeds[7], (D, 3 * D), (0.033 * TOKENS ** 0.5), 12.0, ((0, 32),), jnp.float32),
        "proj_first": centred(seeds[8], (D, D), (0.033 * TOKENS ** 0.5), 12.0, ((0, 32),), jnp.float32),
        "expand_first": centred(seeds[9], (D, FF), (0.0385 * TOKENS ** 0.5), 16.0, ((0, 32),), jnp.float32),
        "shrink_first": centred(seeds[10], (FF, D), (0.066 * TOKENS ** 0.5), 24.0, ((0, 32),), jnp.float32),
        "small_first": centred(seeds[11], (8 + FF // D, D), (0.055 * TOKENS ** 0.5), 20.0, ((1, 32),), jnp.float32),
        "qkv_second": jnp.clip(jnp.exp(math.log(77.824) - 1.375823 * jax.random.uniform(seeds[12], (D, 3 * D), jnp.float32) ** block_scale(seeds[12], (D, 3 * D), ((0, 32),), -0.2, 0.2)), 19.6608, 77.824),
        "proj_second": jnp.clip(jnp.exp(math.log(77.824) - 1.375823 * jax.random.uniform(seeds[13], (D, D), jnp.float32) ** block_scale(seeds[13], (D, D), ((0, 32),), -0.2, 0.2)), 19.6608, 77.824),
        "expand_second": jnp.clip(jnp.exp(math.log(106.496) - 1.3862944 * jax.random.uniform(seeds[14], (D, FF), jnp.float32) ** block_scale(seeds[14], (D, FF), ((0, 32),), -0.2, 0.2)), 26.624, 106.496),
        "shrink_second": jnp.clip(jnp.exp(math.log(311.296) - 1.3862944 * jax.random.uniform(seeds[15], (FF, D), jnp.float32) ** block_scale(seeds[15], (FF, D), ((0, 32),), -0.2, 0.2)), 77.824, 311.296),
        "small_second": jnp.clip(jnp.exp(math.log(217.088) - 1.40534252 * jax.random.uniform(seeds[16], (8 + FF // D, D), jnp.float32) ** block_scale(seeds[16], (8 + FF // D, D), ((1, 32),), -0.2, 0.2)), 53.248, 217.088),
    }


@jax.custom_vjp
def low(v):
    return lax.optimization_barrier(v.astype(jnp.bfloat16)).astype(jnp.float32)

@jax.custom_vjp
def low_back(v):
    return v

def low_keep(v):
    return (low(v), None)

def low_pass(kept, grad):
    return (grad,)

def back_keep(v):
    return (v, None)

def back_low(kept, grad):
    return (low(grad),)
low.defvjp(low_keep, low_pass)
low_back.defvjp(back_keep, back_low)
highest = lax.Precision.HIGHEST
norm_eps = 1e-05
beta_one = 0.9
beta_two = 0.95
adam_eps = 1e-08
matrix_rate = 0.05
matrix_decay = 0.1
small_rate = 0.5
masked_score = -1e+30

def layer_norm(values, norm_gain, norm_shift):
    center = lax.optimization_barrier(jnp.mean(values, -1, keepdims=True))
    spread = values - center
    square_mean = lax.optimization_barrier(jnp.mean(spread * spread, -1, keepdims=True))
    return spread * lax.rsqrt(square_mean + norm_eps) * norm_gain + norm_shift

def unpack(small, model_width, hidden):
    extra_rows = hidden // model_width
    return (small[0], small[1], small[2], small[3], small[4], small[5], small[6], small[7:7 + extra_rows].reshape(hidden), small[7 + extra_rows])

def adam_update(weight, first_state, second, gradient, step_rate, decay_rate):
    moment = beta_one * first_state + (1.0 - beta_one) * gradient
    variance = beta_two * second + (1.0 - beta_two) * gradient * gradient
    mean_fixed = moment / (1.0 - beta_one ** STEP)
    var_fixed = variance / (1.0 - beta_two ** STEP)
    updated = weight - step_rate * (mean_fixed / (jnp.sqrt(var_fixed) + adam_eps) + decay_rate * weight)
    return (moment, variance, updated)

def attend_head(head_item):
    queries, key_rows, values = head_item
    scores = jnp.dot(queries, key_rows.T, precision=highest) * (1.0 / math.sqrt(HEAD))
    places = jnp.arange(LEN)
    scores = jnp.where(places[:, None] >= places[None, :], scores, masked_score)
    scores = low_back(scores)
    soft_probs = low(jax.nn.softmax(scores, axis=-1))
    return jnp.dot(soft_probs, values, precision=highest)

def forward(inputs, qkv_weight, proj_weight, expand_weight, shrink_weight, small_params):
    qkv_low = low(qkv_weight)
    proj_low = low(proj_weight)
    expand_low = low(expand_weight)
    shrink_low = low(shrink_weight)
    small_low = low(small_params)
    gain_one, shift_one, bias_query, bias_value, bias_proj, gain_two, shift_two, bias_expand, bias_shrink = unpack(small_low, D, FF)
    normed_one = low(layer_norm(inputs, gain_one, shift_one))
    bias_all = jnp.concatenate([bias_query, jnp.zeros((D,), jnp.float32), bias_value])
    qkv_all = low_back(low(jnp.dot(normed_one, qkv_low, precision=highest) + bias_all))
    split_heads = qkv_all.reshape(LEN, 3, HEADS, HEAD).transpose(1, 2, 0, 3)
    attended = lax.map(jax.checkpoint(attend_head), (split_heads[0], split_heads[1], split_heads[2]))
    attended = attended.transpose(1, 0, 2).reshape(LEN, D)
    attended = low_back(low(attended))
    mixed = inputs + low_back(jnp.dot(attended, proj_low, precision=highest) + bias_proj)
    normed_two = low(layer_norm(mixed, gain_two, shift_two))
    pre_act = low_back(jnp.dot(normed_two, expand_low, precision=highest) + bias_expand)
    activated = low(jax.nn.gelu(pre_act, approximate=True))
    return mixed + jnp.dot(activated, shrink_low, precision=highest) + bias_shrink

def reference(tokens, cotangent, qkv_weight, proj_weight, expand_weight, shrink_weight, small_params, qkv_first, proj_first, expand_first, shrink_first, small_first, qkv_second, proj_second, expand_second, shrink_second, small_second):
    params = (qkv_weight, proj_weight, expand_weight, shrink_weight, small_params)
    inputs = tokens.astype(jnp.float32).reshape(SEQS, LEN, D)
    cot_rows = cotangent.astype(jnp.float32).reshape(SEQS, LEN, D)

    def one_sequence(running, seq_item):
        seq_inputs, seq_cot = seq_item
        layer_out, pull_back = jax.vjp(forward, seq_inputs, params[0], params[1], params[2], params[3], params[4])
        pulled = pull_back(seq_cot)
        running = tuple((total_one + fresh for total_one, fresh in zip(running, pulled[1:])))
        return (running, (layer_out, pulled[0]))
    zero_sums = tuple((jnp.zeros_like(array_one) for array_one in params))
    grad_sums, (layer_outs, input_grads) = lax.scan(one_sequence, zero_sums, (inputs, cot_rows))
    block_out = layer_outs.reshape(TOKENS, D)
    token_grad = input_grads.reshape(TOKENS, D)
    qkv_moment, qkv_variance, qkv_updated = adam_update(qkv_weight, qkv_first, qkv_second, grad_sums[0], matrix_rate, matrix_decay)
    proj_moment, proj_variance, proj_updated = adam_update(proj_weight, proj_first, proj_second, grad_sums[1], matrix_rate, matrix_decay)
    expand_moment, expand_variance, expand_updated = adam_update(expand_weight, expand_first, expand_second, grad_sums[2], matrix_rate, matrix_decay)
    shrink_moment, shrink_variance, shrink_updated = adam_update(shrink_weight, shrink_first, shrink_second, grad_sums[3], matrix_rate, matrix_decay)
    small_moment, small_variance, small_updated = adam_update(small_params, small_first, small_second, grad_sums[4], small_rate, 0.0)
    return (block_out, token_grad, qkv_moment, qkv_variance, qkv_updated, proj_moment, proj_variance, proj_updated, expand_moment, expand_variance, expand_updated, shrink_moment, shrink_variance, shrink_updated, small_moment, small_variance, small_updated)
```

```python
import math

import jax
import jax.numpy as jnp
from jax import lax
from jax.experimental import pallas as pl
from jax.experimental.pallas import tpu as pltpu
from jax.sharding import PartitionSpec as P

HEAD = 64
STEP = 10

norm_eps = 1e-05
beta_one = 0.9
beta_two = 0.95
adam_eps = 1e-08
matrix_rate = 0.05
matrix_decay = 0.1
small_rate = 0.5
masked_score = -1e30
score_scale = 1.0 / math.sqrt(HEAD)

F32 = jnp.float32
BF16 = jnp.bfloat16
ALL = ("dp", "seq", "blk")
PLANE = ("seq", "blk")
VMEM_LIMIT = 56 * 1024 * 1024
NT = (((1,), (1,)), ((), ()))
TN = (((0,), (0,)), ((), ()))


def dot(a, b, dims=None):
    if dims is None:
        return jnp.dot(a, b, preferred_element_type=F32)
    return lax.dot_general(a, b, dims, preferred_element_type=F32)


def adam_update(weight, first_state, second, gradient, step_rate, decay_rate):
    moment = beta_one * first_state + (1.0 - beta_one) * gradient
    variance = beta_two * second + (1.0 - beta_two) * gradient * gradient
    mean_fixed = moment / (1.0 - beta_one**STEP)
    var_fixed = variance / (1.0 - beta_two**STEP)
    updated = weight - step_rate * (
        mean_fixed / (jnp.sqrt(var_fixed) + adam_eps) + decay_rate * weight
    )
    return (moment, variance, updated)


def norm_parts(values):
    center = jnp.mean(values, -1, keepdims=True)
    spread = values - center
    inverse = lax.rsqrt(jnp.mean(spread * spread, -1, keepdims=True) + norm_eps)
    return spread * inverse, inverse


def norm_pull(unit, inverse, gain, grad):
    scaled = grad * gain
    first = jnp.mean(scaled, -1, keepdims=True)
    second = jnp.mean(scaled * unit, -1, keepdims=True)
    return inverse * (scaled - first - unit * second)


def swap(value, seq_bits, blk_bits):
    seq_count, blk_count = lax.axis_size("seq"), lax.axis_size("blk")
    pairs = [
        (i * blk_count + j, (i ^ seq_bits) * blk_count + (j ^ blk_bits))
        for i in range(seq_count)
        for j in range(blk_count)
    ]
    return lax.ppermute(value, PLANE, pairs)


def shift(value, step):
    count = lax.axis_size("dp")
    return lax.ppermute(value, "dp", [(i, (i + step) % count) for i in range(count)])


def gather_plane(value):
    near = jnp.stack([value, swap(value, 0, 1), swap(value, 2, 0), swap(value, 2, 1)])
    return near, swap(near, 1, 0)


def scatter_plane(near, far):
    both = (near.astype(F32) + swap(far, 1, 0).astype(F32)).astype(BF16)
    return (
        both[0].astype(F32)
        + swap(both[1], 0, 1).astype(F32)
        + swap(both[2], 2, 0).astype(F32)
        + swap(both[3], 2, 1).astype(F32)
    )


def gather_dp(value):
    count = lax.axis_size("dp")
    if count != 4:
        return lax.all_gather(value, "dp", axis=0, tiled=False)
    me = lax.axis_index("dp")
    parts = [value, shift(value, 1), shift(value, 2), shift(value, 3)]
    ordered = []
    for j in range(count):
        picked = parts[3]
        for k in (2, 1, 0):
            picked = jnp.where(me == (j + k) % count, parts[k], picked)
        ordered.append(picked)
    return jnp.stack(ordered)


def scatter_dp(value):
    count = lax.axis_size("dp")
    if count != 4:
        return lax.psum_scatter(value, "dp", scatter_dimension=0, tiled=False).astype(F32)
    me = lax.axis_index("dp")
    total = lax.dynamic_index_in_dim(value, me, 0, keepdims=False).astype(F32)
    for k in range(1, count):
        chunk = lax.dynamic_index_in_dim(value, (me + k) % count, 0, keepdims=False)
        total = total + shift(chunk, k).astype(F32)
    return total


def head_masks(width):
    lane = lax.broadcasted_iota(jnp.int32, (1, width), 1)
    return [(lane >= h * HEAD) & (lane < (h + 1) * HEAD) for h in range(width // HEAD)]


def spread_heads(block, masks):
    return jnp.concatenate([jnp.where(m, block, jnp.zeros_like(block)) for m in masks], 0)


def join_heads(stacked, masks):
    rows = stacked.shape[0] // len(masks)
    out = jnp.where(masks[0], stacked[:rows], 0.0)
    for h in range(1, len(masks)):
        out = out + jnp.where(masks[h], stacked[h * rows : (h + 1) * rows], 0.0)
    return out


def visible(heads, rows, keys, first_row):
    row = lax.broadcasted_iota(jnp.int32, (heads, rows, keys), 1).reshape(heads * rows, keys)
    key = lax.broadcasted_iota(jnp.int32, (heads * rows, keys), 1)
    return key <= row + first_row


def forward_kernel(place, tok_a, tok_b, w_ref, vec_ref, bias_ref, qkv_ref, n1_ref, att_ref, lse_ref):
    me, half = place[0], place[1]
    rows = tok_a.shape[1]
    gain, lift = vec_ref[0:1, :], vec_ref[1:2, :]
    for bit in range(2):
        tok = (tok_a, tok_b)[bit]
        for far in range(2):
            at = me ^ (2 * far + bit)
            two = tok[2 * far : 2 * far + 2].reshape(2 * rows, -1).astype(F32)
            unit, _ = norm_parts(two)
            n1 = (unit * gain + lift).astype(BF16)
            outs = [(dot(n1, w_ref[j]) + bias_ref[j]).astype(BF16) for j in range(3)]
            for other in range(2):
                where = pl.ds(pl.multiple_of((2 * at + (half ^ other)) * rows, rows), rows)
                n1_ref[where, :] = n1[other * rows : (other + 1) * rows]
                for j in range(3):
                    qkv_ref[j, where, :] = outs[j][other * rows : (other + 1) * rows]
    masks = head_masks(qkv_ref.shape[2])
    heads = len(masks)
    for i in range(4):
        keys = 2 * rows * (i + 1)
        where = pl.ds(pl.multiple_of((2 * i + half) * rows, rows), rows)
        queries = spread_heads(qkv_ref[0, where, :], masks)
        scores = dot(queries, qkv_ref[1, 0:keys, :], NT) * score_scale
        seen = visible(heads, rows, keys, (2 * i + half) * rows)
        scores = jnp.where(seen, scores, masked_score)
        top = jnp.max(scores, -1, keepdims=True)
        raised = jnp.exp(scores - top)
        total = jnp.sum(raised, -1, keepdims=True)
        probs = (raised / total).astype(BF16)
        result = join_heads(dot(probs, qkv_ref[2, 0:keys, :]), masks)
        att_ref[:, i * rows : (i + 1) * rows] = result.T.astype(BF16)
        lse_ref[i] = top + jnp.log(total)


def hidden_kernel(
    place, tok_a, tok_b, cot_a, cot_b, att_a, att_b, proj_ref, we_ref, ws_ref, vec_ref, be_ref,
    out_a, out_b, dn_a, dn_b, mixed_ref, gs_ref, ge_ref, sums_ref, gb_ref,
    att_all, gs_sum, ge_sum,
):
    me = place[0]
    rows = tok_a.shape[1]
    span = 4 * rows
    group = att_a.shape[1]
    for bit in range(2):
        att = (att_a, att_b)[bit]
        for far in range(2):
            at = me ^ (2 * far + bit)
            where = pl.ds(pl.multiple_of(at * group, 64), group)
            for other in range(2):
                att_all[where, other * span : (other + 1) * span] = att[2 * far + other]
    bias_proj, gain, lift = vec_ref[0:1, :], vec_ref[1:2, :], vec_ref[2:3, :]
    sums_ref[...] = jnp.zeros_like(sums_ref)
    gb_ref[...] = jnp.zeros_like(gb_ref)
    for bit in range(2):
        tok, cot, out, dn = (tok_a, tok_b)[bit], (cot_a, cot_b)[bit], (out_a, out_b)[bit], (dn_a, dn_b)[bit]
        for far in range(2):
            start = pl.multiple_of((me ^ (2 * far + bit)) * rows, rows)
            att = jnp.concatenate(
                [
                    att_all[:, pl.ds(start, rows)],
                    att_all[:, pl.ds(pl.multiple_of(span + start, rows), rows)],
                ],
                1,
            )
            two = tok[2 * far : 2 * far + 2].reshape(2 * rows, -1).astype(F32)
            mixed = two + (dot(att, proj_ref[...], TN) + bias_proj)
            if bit == 0 and far == 0:
                mixed_ref[...] = mixed[:rows]
            unit, _ = norm_parts(mixed)
            n2 = (unit * gain + lift).astype(BF16)
            pre = dot(n2, we_ref[...]) + be_ref[...]
            cots = cot[2 * far : 2 * far + 2].reshape(2 * rows, -1)
            factor = math.sqrt(2.0 / math.pi)
            square = pre * pre
            bent = jnp.tanh(factor * pre * (1.0 + 0.044715 * square))
            act = (0.5 * pre * (1.0 + bent)).astype(BF16)
            slope = 0.5 * (1.0 + bent) + 0.5 * pre * (1.0 - bent * bent) * (
                factor * (1.0 + 3.0 * 0.044715 * square)
            )
            d_act = dot(cots, ws_ref[...], NT)
            d_pre32 = d_act * slope
            d_pre = d_pre32.astype(BF16)
            d_n2 = dot(d_pre, we_ref[...], NT)
            dn[2 * far : 2 * far + 2] = d_n2.astype(BF16).reshape(2, rows, -1)
            out[2 * far : 2 * far + 2] = dot(act, ws_ref[...]).astype(BF16).reshape(2, rows, -1)
            gs = dot(act, cots, TN)
            ge = dot(n2, d_pre, TN)
            if bit == 0 and far == 0:
                gs_sum[...] = gs
                ge_sum[...] = ge
            else:
                gs_sum[...] += gs
                ge_sum[...] += ge
            sums_ref[0:1, :] += jnp.sum(d_n2 * unit, 0, keepdims=True)
            sums_ref[1:2, :] += jnp.sum(d_n2, 0, keepdims=True)
            gb_ref[0:1, :] += jnp.sum(d_pre.astype(F32), 0, keepdims=True)
    gs_ref[...] = gs_sum[...].astype(BF16)
    ge_ref[...] = ge_sum[...].astype(BF16)


def backward_kernel(
    place, db_a, db_b, qkv_ref, lse_ref, n1_ref, tok_a, tok_b, att_a, att_b, proj_ref, w_ref,
    dn_a, dn_b, g_ref, gp_ref, sums_ref, gb_ref,
    db_all, dq, dk, dv,
):
    me, half = place[0], place[1]
    rows = tok_a.shape[1]
    group = qkv_ref.shape[2]
    masks = head_masks(group)
    heads = len(masks)
    for bit in range(2):
        for far in range(2):
            at = me ^ (2 * far + bit)
            db_all[pl.ds(pl.multiple_of(at * rows, rows), rows), :] = (db_a, db_b)[bit][far]
    own_proj = proj_ref[pl.ds(pl.multiple_of(me * group, 64), group), :]
    dq[...] = jnp.zeros_like(dq)
    dk[...] = jnp.zeros_like(dk)
    dv[...] = jnp.zeros_like(dv)
    for i in range(4):
        keys = 2 * rows * (i + 1)
        where = pl.ds(pl.multiple_of((2 * i + half) * rows, rows), rows)
        queries = spread_heads(qkv_ref[0, where, :], masks)
        d_att = dot(db_all[i * rows : (i + 1) * rows, :], own_proj, NT).astype(BF16)
        grads = spread_heads(d_att, masks)
        key_rows, values = qkv_ref[1, 0:keys, :], qkv_ref[2, 0:keys, :]
        scores = dot(queries, key_rows, NT) * score_scale
        seen = visible(heads, rows, keys, (2 * i + half) * rows)
        probs = jnp.where(seen, jnp.exp(scores - lse_ref[i]), 0.0)
        weighed = probs * dot(grads, values, NT)
        d_scores = (weighed - probs * jnp.sum(weighed, -1, keepdims=True)).astype(BF16)
        dq[where, :] = join_heads(dot(d_scores, key_rows), masks) * score_scale
        dk[0:keys, :] += dot(d_scores, queries, TN) * score_scale
        dv[0:keys, :] += dot(probs.astype(BF16), grads, TN)
    for bit in range(2):
        for far in range(2):
            at = me ^ (2 * far + bit)
            gp_ref[pl.ds(pl.multiple_of(at * group, 64), group), :] = dot(
                (att_a, att_b)[bit][2 * far], db_all[...]
            ).astype(BF16)
    sums_ref[...] = jnp.zeros_like(sums_ref)
    parts = [dq[...].astype(BF16), dk[...].astype(BF16), dv[...].astype(BF16)]
    for j in range(3):
        g_ref[j] = dot(n1_ref[...], parts[j], TN).astype(BF16)
        gb_ref[j] = jnp.sum(parts[j].astype(F32), 0, keepdims=True)
    for bit in range(2):
        tok, dn = (tok_a, tok_b)[bit], (dn_a, dn_b)[bit]
        for far in range(2):
            for other in range(2):
                at = (me ^ (2 * far + bit)) * 2 + (half ^ other)
                where = pl.ds(pl.multiple_of(at * rows, rows), rows)
                d_n1 = (
                    dot(dk[where, :].astype(BF16), w_ref[1], NT)
                    + dot(dv[where, :].astype(BF16), w_ref[2], NT)
                )
                if other == 0:
                    d_n1 = d_n1 + dot(dq[where, :].astype(BF16), w_ref[0], NT)
                unit, _ = norm_parts(tok[2 * far + other].astype(F32))
                dn[2 * far + other] = d_n1.astype(BF16)
                sums_ref[0:1, :] += jnp.sum(d_n1 * unit, 0, keepdims=True)
                sums_ref[1:2, :] += jnp.sum(d_n1, 0, keepdims=True)


def call(kernel, outs, scratch, flops, *args):
    whole = pl.BlockSpec(memory_space=pltpu.VMEM)
    specs = [pl.BlockSpec(memory_space=pltpu.SMEM)] + [whole] * (len(args) - 1)
    moved = sum(math.prod(a.shape) * a.dtype.itemsize for a in args)
    return pl.pallas_call(
        kernel,
        out_shape=[jax.ShapeDtypeStruct(shape, kind) for shape, kind in outs],
        in_specs=specs,
        out_specs=[whole] * len(outs),
        scratch_shapes=[pltpu.VMEM(shape, kind) for shape, kind in scratch],
        compiler_params=pltpu.CompilerParams(vmem_limit_bytes=VMEM_LIMIT),
        cost_estimate=pl.CostEstimate(flops=flops, bytes_accessed=moved, transcendentals=10**6),
    )(*args)


def shards(
    tokens,
    cotangent,
    qkv_weight,
    proj_weight,
    expand_weight,
    shrink_weight,
    small_params,
    qkv_first,
    proj_first,
    expand_first,
    shrink_first,
    small_first,
    qkv_second,
    proj_second,
    expand_second,
    shrink_second,
    small_second,
):
    rows, width = tokens.shape
    hidden = expand_weight.shape[1]
    own_rows = qkv_weight.shape[0]
    own_hidden = shrink_weight.shape[0]
    dp_count, seq_count, blk_count = (lax.axis_size(a) for a in ALL)
    plane = seq_count * blk_count
    assert (seq_count, blk_count) == (4, 2)
    dp, seq, blk = (lax.axis_index(a) for a in ALL)
    spot = seq * blk_count + blk
    group = width // seq_count
    slots = hidden // plane
    length = plane * rows
    half_length = length // blk_count
    small_rows = small_params.shape[0]
    place = jnp.stack([seq, blk]).astype(jnp.int32)

    tok_a, tok_b = gather_plane(tokens)

    qkv_parts = qkv_weight.astype(BF16).reshape(own_rows, 3, seq_count, group)
    qkv_parts = jnp.transpose(qkv_parts, (2, 0, 1, 3)).reshape(seq_count, own_rows, 3 * group)
    qkv_parts = lax.all_to_all(qkv_parts, "seq", split_axis=0, concat_axis=0, tiled=True)
    own = gather_dp(qkv_parts)
    other = swap(own, 0, 1)
    w_qkv = jnp.stack([jnp.where(blk == 0, own, other), jnp.where(blk == 0, other, own)], 2)
    w_qkv = jnp.transpose(w_qkv.reshape(width, 3, group), (1, 0, 2))

    proj_ext = jnp.concatenate([proj_weight, small_params.T], 1).astype(BF16)
    own = gather_dp(proj_ext)
    other = swap(own, 0, 1)
    pair = jnp.stack([jnp.where(blk == 0, own, other), jnp.where(blk == 0, other, own)], 1)
    two = jnp.stack([pair, swap(pair, 2, 0)])
    four = jnp.concatenate([two, swap(two, 1, 0)], 0)
    ordered = []
    for s in range(seq_count):
        apart = seq ^ s
        at = (apart & 1) * 2 + (apart >> 1)
        ordered.append(lax.dynamic_index_in_dim(four, at, 0, keepdims=False))
    proj_ext = jnp.stack(ordered, 1).reshape(width, width + small_rows)
    proj_full = proj_ext[:, :width]
    small_full = proj_ext[:, width:].T.astype(F32)

    expand_parts = expand_weight.astype(BF16).reshape(own_rows, dp_count, plane, own_hidden)
    expand_parts = jnp.transpose(expand_parts, (2, 0, 1, 3)).reshape(plane, own_rows, slots)
    expand_parts = lax.all_to_all(expand_parts, PLANE, split_axis=0, concat_axis=0, tiled=True)
    w_expand = gather_dp(expand_parts).reshape(width, slots)
    w_shrink = gather_dp(shrink_weight.astype(BF16)).reshape(slots, width)

    cot_a, cot_b = gather_plane(cotangent)

    extra = hidden // width
    zero = jnp.zeros((width,), F32)
    bias_all = jnp.stack([small_full[2], zero, small_full[3]]).reshape(3, seq_count, group)
    bias_own = lax.dynamic_index_in_dim(bias_all, seq, 1)
    bias_expand = small_full[7 : 7 + extra].reshape(dp_count, plane, own_hidden)
    bias_expand = lax.dynamic_index_in_dim(bias_expand, spot, 1, keepdims=False).reshape(1, slots)
    bias_shrink = small_full[7 + extra]

    qkv, n1, att, lse = call(
        forward_kernel,
        [
            ((3, length, group), BF16),
            ((length, width), BF16),
            ((group, half_length), BF16),
            ((4, 3 * rows, 1), F32),
        ],
        [],
        2 * 10**9,
        place, tok_a, tok_b, w_qkv, small_full, bias_own,
    )
    att_a, att_b = gather_plane(att)

    big = ((4, rows, width), BF16)
    out_a, out_b, dn_a, dn_b, mixed, g_shrink, g_expand, sums_two, gb_expand = call(
        hidden_kernel,
        [
            big, big, big, big,
            ((rows, width), F32),
            ((slots, width), BF16),
            ((width, slots), BF16),
            ((8, width), F32),
            ((8, slots), F32),
        ],
        [((width, length), BF16), ((slots, width), F32), ((width, slots), F32)],
        6 * 10**9,
        place, tok_a, tok_b, cot_a, cot_b, att_a, att_b, proj_full, w_expand, w_shrink,
        small_full[4:7], bias_expand,
    )

    cot_wide = cotangent.astype(F32)
    d_normed_two = scatter_plane(dn_a, dn_b)
    unit, inverse = norm_parts(mixed)
    d_mixed = cot_wide + norm_pull(unit, inverse, small_full[5], d_normed_two)
    d_branch = d_mixed.astype(BF16)
    db_a = jnp.stack([d_branch, swap(d_branch, 2, 0)])
    db_b = swap(db_a, 1, 0)

    block_out = mixed + scatter_plane(out_a, out_b) + bias_shrink

    sum_shrink = lax.psum_scatter(g_shrink, "dp", scatter_dimension=0, tiled=True).astype(F32)
    sum_expand = lax.psum_scatter(g_expand, "dp", scatter_dimension=0, tiled=True)
    sum_expand = lax.all_to_all(
        sum_expand.reshape(plane, own_rows, slots), PLANE, split_axis=0, concat_axis=0, tiled=True
    )
    sum_expand = jnp.transpose(
        sum_expand.reshape(plane, own_rows, dp_count, own_hidden), (1, 2, 0, 3)
    ).reshape(own_rows, hidden).astype(F32)

    dn_a, dn_b, g_qkv, g_proj, sums_one, gb_qkv = call(
        backward_kernel,
        [
            big, big,
            ((3, width, group), BF16),
            ((width, width), BF16),
            ((8, width), F32),
            ((3, 1, group), F32),
        ],
        [
            ((half_length, width), BF16),
            ((length, group), F32),
            ((length, group), F32),
            ((length, group), F32),
        ],
        6 * 10**9,
        place, db_a, db_b, qkv, lse, n1, tok_a, tok_b, att_a, att_b, proj_full, w_qkv,
    )

    g_proj = g_proj.reshape(dp_count, seq_count, blk_count, own_rows, width)
    g_proj = lax.dynamic_index_in_dim(g_proj, seq, 1, keepdims=False)
    keep = lax.dynamic_index_in_dim(g_proj, blk, 1, keepdims=False)
    send = lax.dynamic_index_in_dim(g_proj, 1 - blk, 1, keepdims=False)
    g_proj = (keep.astype(F32) + swap(send, 0, 1).astype(F32)).astype(BF16)
    sum_proj = scatter_dp(g_proj)

    def at_heads(row):
        return lax.dynamic_update_slice(zero, row.reshape(group), (seq * group,))

    gb_full = jnp.zeros((dp_count, plane, own_hidden), F32)
    gb_full = lax.dynamic_update_slice(
        gb_full, gb_expand[0].reshape(dp_count, 1, own_hidden), (0, spot, 0)
    ).reshape(extra, width)
    g_small = jnp.concatenate(
        [
            jnp.stack(
                [
                    sums_one[0],
                    sums_one[1],
                    at_heads(gb_qkv[0]),
                    at_heads(gb_qkv[2]),
                    jnp.sum(d_branch.astype(F32), 0),
                    sums_two[0],
                    sums_two[1],
                ]
            ),
            gb_full,
            jnp.sum(cot_wide, 0)[None],
        ],
        0,
    )

    g_all = jnp.concatenate(
        [jnp.transpose(g_qkv, (1, 0, 2)).reshape(width, 3 * group), g_small.T.astype(BF16)], 1
    )
    g_all = g_all.reshape(dp_count, seq_count, blk_count, own_rows, 3 * group + small_rows)
    keep = lax.dynamic_index_in_dim(g_all, blk, 2, keepdims=False)
    send = lax.dynamic_index_in_dim(g_all, 1 - blk, 2, keepdims=False)
    g_all = (keep.astype(F32) + swap(send, 0, 1).astype(F32)).astype(BF16)
    g_all = scatter_dp(g_all).astype(BF16)
    g_all = lax.all_to_all(g_all, "seq", split_axis=0, concat_axis=0, tiled=True).astype(F32)
    sum_small = jnp.sum(g_all[:, :, 3 * group :], 0).T
    sum_qkv = jnp.transpose(
        g_all[:, :, : 3 * group].reshape(seq_count, own_rows, 3, group), (1, 2, 0, 3)
    ).reshape(own_rows, 3 * width)

    d_normed_one = scatter_plane(dn_a, dn_b)
    unit, inverse = norm_parts(tokens.astype(F32))
    token_grad = d_mixed + norm_pull(unit, inverse, small_full[0], d_normed_one)

    qkv_out = adam_update(
        qkv_weight, qkv_first, qkv_second, sum_qkv, matrix_rate, matrix_decay
    )
    proj_out = adam_update(
        proj_weight, proj_first, proj_second, sum_proj, matrix_rate, matrix_decay
    )
    expand_out = adam_update(
        expand_weight, expand_first, expand_second, sum_expand, matrix_rate, matrix_decay
    )
    shrink_out = adam_update(
        shrink_weight, shrink_first, shrink_second, sum_shrink, matrix_rate, matrix_decay
    )
    small_out = adam_update(
        small_params, small_first, small_second, sum_small, small_rate, 0.0
    )
    return (block_out, token_grad, *qkv_out, *proj_out, *expand_out, *shrink_out, *small_out)


def solution(mesh):
    by_rows = P(ALL, None)
    by_columns = P(None, ALL)
    state = (by_rows,) * 4 + (by_columns,)
    return jax.shard_map(
        shards,
        mesh=mesh,
        in_specs=(by_rows, by_rows) + state * 3,
        out_specs=(by_rows,) * 14 + (by_columns,) * 3,
        check_vma=False,
    )
```

```python
from functools import partial
import math

import jax
import jax.numpy as jnp
from jax import lax
from jax.experimental import pallas as pl
from jax.experimental.pallas import tpu as pltpu
from jax.sharding import PartitionSpec as P

HEAD = 64
STEP = 10

norm_eps = 1e-05
beta_one = 0.9
beta_two = 0.95
adam_eps = 1e-08
matrix_rate = 0.05
matrix_decay = 0.1
small_rate = 0.5
masked_score = -1e30
score_scale = 1.0 / math.sqrt(HEAD)

F32 = jnp.float32
BF16 = jnp.bfloat16
ALL = ("dp", "seq", "blk")
PLANE = ("seq", "blk")
VMEM_LIMIT = 56 * 1024 * 1024
NT = (((1,), (1,)), ((), ()))
TN = (((0,), (0,)), ((), ()))


def dot(a, b, dims=None):
    if dims is None:
        return jnp.dot(a, b, preferred_element_type=F32)
    return lax.dot_general(a, b, dims, preferred_element_type=F32)


def adam_update(weight, first_state, second, gradient, step_rate, decay_rate):
    moment = beta_one * first_state + (1.0 - beta_one) * gradient
    variance = beta_two * second + (1.0 - beta_two) * gradient * gradient
    mean_fixed = moment / (1.0 - beta_one**STEP)
    var_fixed = variance / (1.0 - beta_two**STEP)
    updated = weight - step_rate * (
        mean_fixed / (jnp.sqrt(var_fixed) + adam_eps) + decay_rate * weight
    )
    return (moment, variance, updated)


def norm_parts(values):
    center = jnp.mean(values, -1, keepdims=True)
    spread = values - center
    inverse = lax.rsqrt(jnp.mean(spread * spread, -1, keepdims=True) + norm_eps)
    return spread * inverse, inverse


def norm_pull(unit, inverse, gain, grad):
    scaled = grad * gain
    first = jnp.mean(scaled, -1, keepdims=True)
    second = jnp.mean(scaled * unit, -1, keepdims=True)
    return inverse * (scaled - first - unit * second)


def swap(value, seq_bits, blk_bits):
    seq_count, blk_count = lax.axis_size("seq"), lax.axis_size("blk")
    pairs = [
        (i * blk_count + j, (i ^ seq_bits) * blk_count + (j ^ blk_bits))
        for i in range(seq_count)
        for j in range(blk_count)
    ]
    return lax.ppermute(value, PLANE, pairs)


def shift(value, step):
    count = lax.axis_size("dp")
    return lax.ppermute(value, "dp", [(i, (i + step) % count) for i in range(count)])


def gather_near(value):
    return jnp.stack([value, swap(value, 0, 1), swap(value, 2, 0), swap(value, 2, 1)])


def after(value, *others):
    return lax.optimization_barrier((value, *others))[0]


def gather_steps(value):
    two = jnp.stack([value, swap(value, 0, 1)])
    return jnp.concatenate([two, swap(two, 2, 0)], 0)


def add_low(a, b):
    return (a.astype(F32) + b.astype(F32)).astype(BF16)


def spread_near(both):
    return both[0], swap(both[1], 0, 1), swap(both[2], 2, 0), swap(both[3], 2, 1)


def add_all(parts):
    total = parts[0].astype(F32)
    for part in parts[1:]:
        total = total + part.astype(F32)
    return total


def scatter_dp(value, *others):
    count = lax.axis_size("dp")
    if count != 4:
        return lax.psum_scatter(value, "dp", scatter_dimension=0, tiled=False).astype(F32)
    me = lax.axis_index("dp")
    parts = [lax.dynamic_index_in_dim(value, me, 0, keepdims=False)]
    for k in range(1, count):
        chunk = lax.dynamic_index_in_dim(value, (me + k) % count, 0, keepdims=False)
        parts.append(shift(chunk, k))
    if others:
        parts = lax.optimization_barrier((*parts, *others))[:count]
    return add_all(parts)


def head_masks(first, group):
    lane = lax.broadcasted_iota(jnp.int32, (1, 256), 1) - first
    return [(lane >= h * HEAD) & (lane < (h + 1) * HEAD) for h in range(group // HEAD)]


def turned(block):
    return pltpu.roll(block.astype(F32), 64, 1).astype(BF16)


def spread_heads(block, masks):
    return jnp.concatenate([jnp.where(m, block, jnp.zeros_like(block)) for m in masks], 0)


def join_heads(stacked, masks):
    rows = stacked.shape[0] // len(masks)
    out = jnp.where(masks[0], stacked[:rows], 0.0)
    for h in range(1, len(masks)):
        out = out + jnp.where(masks[h], stacked[h * rows : (h + 1) * rows], 0.0)
    return out


def visible(heads, rows, keys, first_row):
    row = lax.broadcasted_iota(jnp.int32, (heads, rows, keys), 1).reshape(heads * rows, keys)
    key = lax.broadcasted_iota(jnp.int32, (heads * rows, keys), 1)
    return key <= row + first_row


def forward_kernel(pieces, place, *refs):
    me, half, layer = place[0], place[1], place[2]
    w_parts, refs = refs[: max(1, 2 * pieces)], refs[max(1, 2 * pieces) :]
    tok_a, tok_b, qkv_ref, n1_ref, att_ref, lse_ref, w_ref, small_ref, w32 = refs
    rows = tok_a.shape[1]
    group = att_ref.shape[0]
    wide = w32.shape[1]
    tail = wide - 128
    w32[:, tail:wide] = jnp.zeros((w32.shape[0], 128), F32)
    if pieces == 0:
        w32[:, : w_parts[0].shape[1]] = w_parts[0][...].astype(F32)
    for k in range(pieces):
        own_layer = lax.rem(layer + (pieces - k), pieces)
        for other in range(2):
            part = w_parts[2 * k + other]
            for j in range(4):
                owner = (own_layer * 4 + (me ^ j)) * 2 + (half ^ other)
                count = part.shape[1]
                where = pl.ds(pl.multiple_of(owner * count, 8), count)
                w32[where, : part.shape[2]] = part[j].astype(F32)
    w_ref[...] = w32[...].astype(BF16)
    first = 3 * group - tail
    small = w32[:, tail:wide].T
    small_ref[...] = small[first : first + small_ref.shape[0]]
    heads_small = w32[pl.ds(pl.multiple_of(me * group, 64), group), tail:wide].T
    heads_small = heads_small[first : first + 8].astype(BF16)
    row = lax.broadcasted_iota(jnp.int32, (group, wide), 0)
    lane = lax.broadcasted_iota(jnp.int32, (group, wide), 1)
    bias = (
        dot(heads_small, (lane == row).astype(F32).astype(BF16))[2:3]
        + dot(heads_small, (lane == row + 2 * group).astype(F32).astype(BF16))[3:4]
    )
    gain, lift = small_ref[0:1, :], small_ref[1:2, :]
    for bit in range(2):
        tok = (tok_a, tok_b)[bit]
        for far in range(2):
            at = me ^ (2 * far + bit)
            two = tok[2 * far : 2 * far + 2].reshape(2 * rows, -1).astype(F32)
            unit, _ = norm_parts(two)
            n1 = (unit * gain + lift).astype(BF16)
            out = (dot(n1, w_ref[...]) + bias).astype(BF16)
            for other in range(2):
                where = pl.ds(pl.multiple_of((2 * at + (half ^ other)) * rows, rows), rows)
                n1_ref[where, :] = n1[other * rows : (other + 1) * rows]
                qkv_ref[where, :] = out[other * rows : (other + 1) * rows]
    shifted, plain = head_masks(64, group), head_masks(0, group)
    heads = len(plain)
    for i in range(4):
        keys = 2 * rows * (i + 1)
        where = pl.ds(pl.multiple_of((2 * i + half) * rows, rows), rows)
        queries = spread_heads(turned(qkv_ref[where, 0:256]), shifted)
        scores = dot(queries, qkv_ref[0:keys, 128:384], NT) * score_scale
        seen = visible(heads, rows, keys, (2 * i + half) * rows)
        scores = jnp.where(seen, scores, masked_score)
        top = jnp.max(scores, -1, keepdims=True)
        raised = jnp.exp(scores - top)
        total = jnp.sum(raised, -1, keepdims=True)
        probs = (raised / total).astype(BF16)
        result = join_heads(dot(probs, qkv_ref[0:keys, 384:640]), plain)
        att_ref[:, i * rows : (i + 1) * rows] = result.T[:group].astype(BF16)
        lse_ref[i] = top + jnp.log(total)


def hidden_kernel(
    pieces, place, tok_a, tok_b, cot_a, cot_b, att_a, att_b, vec_ref, be_ref, *refs
):
    given, refs = refs[:3], refs[3:]
    out_a, out_b, dn_a, dn_b, mixed_ref, unit_ref, inverse_ref, sums_ref, gb_ref, own_ref = refs[:10]
    g_outs, refs = refs[10:-7], refs[-7:]
    att_all, gs_sum, ge_sum, p32, proj_ref, we_ref, ws_ref = refs
    me, half, layer = place[0], place[1], place[2]
    if pieces == 0:
        p32[...] = given[0][...].astype(F32)
        we_ref[...] = given[1][...]
        ws_ref[...] = given[2][...]
    else:
        p_parts, ff_ref = given[:2], given[2]
        slots, part = ws_ref.shape[0], ws_ref.shape[0] // pieces
        for k in range(pieces):
            ws_ref[k * part : (k + 1) * part, :] = ff_ref[k, 0:part, :]
            for side in range(2):
                we_ref[(2 * k + side) * part : (2 * k + side + 1) * part, :] = ff_ref[
                    k, part:, side * slots : (side + 1) * slots
                ]
        for bit in range(2):
            for j in range(4):
                for k in range(pieces):
                    own_layer = lax.rem(layer + (pieces - k), pieces)
                    owner = (own_layer * 4 + (me ^ ((j & 2) + bit))) * 2 + (half ^ (j & 1))
                    count = p_parts[bit].shape[2]
                    where = pl.ds(pl.multiple_of(owner * count, 8), count)
                    p32[where, :] = p_parts[bit][j, k].astype(F32)
    proj_ref[...] = p32[...].astype(BF16)
    rows = tok_a.shape[1]
    span = 4 * rows
    group = att_a.shape[1]
    for bit in range(2):
        att = (att_a, att_b)[bit]
        for far in range(2):
            at = me ^ (2 * far + bit)
            where = pl.ds(pl.multiple_of(at * group, 64), group)
            if bit == 0 and far == 0:
                own_ref[...] = p32[where, :].astype(BF16)
            for other in range(2):
                att_all[where, other * span : (other + 1) * span] = att[2 * far + other]
    bias_proj, gain, lift = vec_ref[4:5, :], vec_ref[5:6, :], vec_ref[6:7, :]
    sums = [jnp.zeros((1, gain.shape[1]), F32)] * 2
    gb = jnp.zeros((1, gb_ref.shape[1]), F32)
    sums_ref[2:3, :] = jnp.sum(cot_a[0].astype(F32), 0, keepdims=True)
    for bit in range(2):
        tok, cot, out, dn = (tok_a, tok_b)[bit], (cot_a, cot_b)[bit], (out_a, out_b)[bit], (dn_a, dn_b)[bit]
        for far in range(2):
            start = pl.multiple_of((me ^ (2 * far + bit)) * rows, rows)
            att = jnp.concatenate(
                [
                    att_all[:, pl.ds(start, rows)],
                    att_all[:, pl.ds(pl.multiple_of(span + start, rows), rows)],
                ],
                1,
            )
            two = tok[2 * far : 2 * far + 2].reshape(2 * rows, -1).astype(F32)
            mixed = two + (dot(att, proj_ref[...], TN) + bias_proj)
            if bit == 0 and far == 0:
                mixed_ref[...] = mixed[:rows]
            unit, inverse = norm_parts(mixed)
            if bit == 0 and far == 0:
                unit_ref[...] = unit[:rows]
                inverse_ref[...] = inverse[:rows]
            n2 = (unit * gain + lift).astype(BF16)
            pre = dot(n2, we_ref[...]) + be_ref[...]
            cots = cot[2 * far : 2 * far + 2].reshape(2 * rows, -1)
            factor = math.sqrt(2.0 / math.pi)
            square = pre * pre
            bent = jnp.tanh(factor * pre * (1.0 + 0.044715 * square))
            act = (0.5 * pre * (1.0 + bent)).astype(BF16)
            slope = 0.5 * (1.0 + bent) + 0.5 * pre * (1.0 - bent * bent) * (
                factor * (1.0 + 3.0 * 0.044715 * square)
            )
            d_act = dot(cots, ws_ref[...], NT)
            d_pre32 = d_act * slope
            d_pre = d_pre32.astype(BF16)
            d_n2 = dot(d_pre, we_ref[...], NT)
            dn[2 * far : 2 * far + 2] = d_n2.astype(BF16).reshape(2, rows, -1)
            out[2 * far : 2 * far + 2] = dot(act, ws_ref[...]).astype(BF16).reshape(2, rows, -1)
            gs = dot(act, cots, TN)
            ge = dot(n2, d_pre, TN)
            if bit == 0 and far == 0:
                gs_sum[...] = gs
                ge_sum[...] = ge
            else:
                gs_sum[...] += gs
                ge_sum[...] += ge
            sums[0] = sums[0] + jnp.sum(d_n2 * unit, 0, keepdims=True)
            sums[1] = sums[1] + jnp.sum(d_n2, 0, keepdims=True)
            gb = gb + jnp.sum(d_pre.astype(F32), 0, keepdims=True)
    sums_ref[0:1, :] = sums[0]
    sums_ref[1:2, :] = sums[1]
    gb_ref[...] = gb
    if pieces == 0:
        g_outs[0][...] = ge_sum[...].astype(BF16)
        g_outs[1][...] = gs_sum[...].astype(BF16)
        return
    pack = g_outs[0]
    for k in range(pieces):
        pack[k, 0:part, :] = gs_sum[k * part : (k + 1) * part, :].astype(BF16)
        for side in range(2):
            pack[k, part:, side * slots : (side + 1) * slots] = ge_sum[
                (2 * k + side) * part : (2 * k + side + 1) * part, :
            ].astype(BF16)


def split_halves(table, keep, send, half, row_of, lanes, at=0):
    layers, four, count, _ = keep.shape
    for k in range(layers):
        for j in range(four):
            base = row_of(k, j) * 2
            for out, owner in ((keep, base + half), (send, base + 1 - half)):
                where = pl.ds(pl.multiple_of(owner * count, 8), count)
                out[k, j, :, at : at + lanes] = table(where, j).astype(BF16)


def attention_back_kernel(
    pieces, place, db_own, db_far, db_near, db_cross, qkv_ref, lse_ref, n1_ref, own_proj, *refs
):
    d_ref, db_all, outs, (d_all, g_all) = refs[0], refs[1], refs[2:-2], refs[-2:]
    me, half = place[0], place[1]
    rows = db_own.shape[0]
    group = own_proj.shape[0]
    shifted, plain = head_masks(64, group), head_masks(0, group)
    heads = len(plain)
    for bits, db in ((0, db_own), (2, db_far), (1, db_near), (3, db_cross)):
        db_all[pl.ds(pl.multiple_of((me ^ bits) * rows, rows), rows), :] = db[...]
    d_all[...] = jnp.zeros_like(d_all)
    row = lax.broadcasted_iota(jnp.int32, (group, 256), 0)
    lane = lax.broadcasted_iota(jnp.int32, (group, 256), 1)
    widen = (row == lane).astype(F32).astype(BF16)
    for i in range(4):
        keys = 2 * rows * (i + 1)
        where = pl.ds(pl.multiple_of((2 * i + half) * rows, rows), rows)
        queries = spread_heads(turned(qkv_ref[where, 0:256]), shifted)
        d_att = dot(db_all[i * rows : (i + 1) * rows, :], own_proj[...], NT).astype(BF16)
        grads = spread_heads(dot(d_att, widen).astype(BF16), plain)
        key_rows, values = qkv_ref[0:keys, 128:384], qkv_ref[0:keys, 384:640]
        scores = dot(queries, key_rows, NT) * score_scale
        seen = visible(heads, rows, keys, (2 * i + half) * rows)
        probs = jnp.where(seen, jnp.exp(scores - lse_ref[i]), 0.0)
        weighed = probs * dot(grads, values, NT)
        d_scores = (weighed - probs * jnp.sum(weighed, -1, keepdims=True)).astype(BF16)
        dq = join_heads(dot(d_scores, key_rows), shifted) * score_scale
        d_all[where, 0:256] += pltpu.roll(dq, 192, 1)
        d_all[0:keys, 128:384] += dot(d_scores, queries, TN) * score_scale
        d_all[0:keys, 384:640] += dot(probs.astype(BF16), grads, TN)
    d_ref[...] = d_all[...].astype(BF16)
    g_all[...] = dot(n1_ref[...], d_ref[:, 0 : 2 * group], TN)
    if pieces == 0:
        outs[0][...] = g_all[...].astype(BF16)
    else:
        split_halves(
            lambda where, j: g_all[where, :], outs[0], outs[1], half, lambda k, j: k * 4 + j, 2 * group
        )


def norm_back_kernel(
    pieces, place, d_ref, db_all, n1_ref, tok_a, tok_b, att_a, att_b, w_ref, two_ref, gb_ref, spot_ref,
    dn_a, dn_b, *refs
):
    outs, (g_all, gp_all) = refs[:-2], refs[-2:]
    me, half = place[0], place[1]
    rows = tok_a.shape[1]
    group = att_a.shape[1]
    wide, width = d_ref.shape[1], n1_ref.shape[1]
    sums = [jnp.zeros((1, width), F32)] * 2
    for bit in range(2):
        tok, dn = (tok_a, tok_b)[bit], (dn_a, dn_b)[bit]
        for far in range(2):
            at = me ^ (2 * far + bit)
            gp_all[pl.ds(pl.multiple_of(at * group, 64), group), :] = dot(
                (att_a, att_b)[bit][2 * far], db_all[...]
            )
            for other in range(2):
                where = pl.ds(pl.multiple_of((2 * at + (half ^ other)) * rows, rows), rows)
                d_n1 = dot(d_ref[where, :], w_ref[...], NT)
                unit, _ = norm_parts(tok[2 * far + other].astype(F32))
                dn[2 * far + other] = d_n1.astype(BF16)
                sums[0] = sums[0] + jnp.sum(d_n1 * unit, 0, keepdims=True)
                sums[1] = sums[1] + jnp.sum(d_n1, 0, keepdims=True)
    heads_sum = jnp.sum(d_ref[...].astype(F32), 0, keepdims=True).astype(BF16)
    heads_sum = jnp.broadcast_to(heads_sum, (16, wide))
    row = lax.broadcasted_iota(jnp.int32, (wide, width), 0)
    lane = lax.broadcasted_iota(jnp.int32, (wide, width), 1)
    head_q = dot(heads_sum, ((row < group) & (lane == row + me * group)).astype(F32).astype(BF16))
    row = row - 2 * group
    head_v = dot(
        heads_sum,
        ((row >= 0) & (row < group) & (lane == row + me * group)).astype(F32).astype(BF16),
    )
    index = lax.broadcasted_iota(jnp.int32, (16, width), 0)
    small = jnp.where(index == 0, sums[0], 0.0)
    small = jnp.where(index == 1, sums[1], small)
    own = db_all[pl.ds(pl.multiple_of(me * rows, rows), rows), :].astype(F32)
    small = jnp.where(index == 4, jnp.sum(own, 0, keepdims=True), small)
    slots = gb_ref.shape[1]
    block = lax.broadcasted_iota(jnp.int32, (16, slots), 1) - 96 * (
        lax.broadcasted_iota(jnp.int32, (16, slots), 0) - 7
    )
    hidden_rows = jnp.where((block >= 0) & (block < 96), gb_ref[...], 0.0).astype(BF16)
    small = small + dot(hidden_rows, spot_ref[...])
    small = jnp.where(index == 5, two_ref[0:1, :], small)
    small = jnp.where(index == 6, two_ref[1:2, :], small)
    small = jnp.where(index == 7 + slots // 96, two_ref[2:3, :], small)
    small = jnp.where(index == 2, head_q, small)
    small = jnp.where(index == 3, head_v, small).astype(BF16)
    row = lax.broadcasted_iota(jnp.int32, (16, 256), 0)
    lane = lax.broadcasted_iota(jnp.int32, (16, 256), 1)
    spread = (lane == row + group).astype(F32).astype(BF16)
    g_all[...] = dot(n1_ref[...], d_ref[:, 2 * group :], TN) + dot(small, spread, TN)
    if pieces == 0:
        outs[0][...] = g_all[...].astype(BF16)
        outs[1][...] = gp_all[...].astype(BF16)
        return
    split_halves(
        lambda where, j: g_all[where, :], outs[0], outs[1], half, lambda k, j: k * 4 + j, 256
    )

    def chunk(where, j):
        start = j * group
        block = gp_all[where, start // 128 * 128 : start // 128 * 128 + 256]
        if start % 128:
            block = pltpu.roll(block, 256 - start % 128, 1)
        return block[:, :group]

    split_halves(chunk, outs[0], outs[1], half, lambda k, j: k * 4 + me, group, 256)


def call(kernel, outs, scratch, flops, *args):
    whole = pl.BlockSpec(memory_space=pltpu.VMEM)
    specs = [pl.BlockSpec(memory_space=pltpu.SMEM)] + [whole] * (len(args) - 1)
    moved = sum(math.prod(a.shape) * a.dtype.itemsize for a in args)
    return pl.pallas_call(
        kernel,
        out_shape=[jax.ShapeDtypeStruct(shape, kind) for shape, kind in outs],
        in_specs=specs,
        out_specs=[whole] * len(outs),
        scratch_shapes=[pltpu.VMEM(shape, kind) for shape, kind in scratch],
        compiler_params=pltpu.CompilerParams(vmem_limit_bytes=VMEM_LIMIT),
        cost_estimate=pl.CostEstimate(flops=flops, bytes_accessed=moved, transcendentals=10**6),
    )(*args)


def shards(
    tokens,
    cotangent,
    qkv_weight,
    proj_weight,
    expand_weight,
    shrink_weight,
    small_params,
    qkv_first,
    proj_first,
    expand_first,
    shrink_first,
    small_first,
    qkv_second,
    proj_second,
    expand_second,
    shrink_second,
    small_second,
):
    rows, width = tokens.shape
    hidden = expand_weight.shape[1]
    own_rows = qkv_weight.shape[0]
    own_hidden = shrink_weight.shape[0]
    dp_count, seq_count, blk_count = (lax.axis_size(a) for a in ALL)
    plane = seq_count * blk_count
    assert (seq_count, blk_count) == (4, 2)
    dp, seq, blk = (lax.axis_index(a) for a in ALL)
    spot = seq * blk_count + blk
    group = width // seq_count
    slots = hidden // plane
    length = plane * rows
    half_length = length // blk_count
    small_rows = small_params.shape[0]
    place = jnp.stack([seq, blk, dp]).astype(jnp.int32)

    w_lanes = 3 * group + small_rows
    parts = qkv_weight.astype(BF16).reshape(own_rows, 3, seq_count, group)
    parts = jnp.transpose(parts, (2, 0, 1, 3)).reshape(seq_count, own_rows, 3 * group)
    small_part = jnp.broadcast_to(
        small_params.T.astype(BF16), (seq_count, own_rows, small_rows)
    )
    parts = jnp.concatenate([parts, small_part], 2)
    pieces = 4 if dp_count == 4 and own_rows % 8 == 0 else 0
    if pieces:
        picked = [lax.dynamic_index_in_dim(parts, seq ^ k, 0, keepdims=False) for k in range(4)]
        near = jnp.stack([picked[0]] + [swap(picked[k], k, 0) for k in range(1, 4)])
        layers = [near] + [shift(near, k) for k in range(1, 4)]
        w_parts = []
        for part in layers:
            w_parts += [part, swap(part, 0, 1)]
    else:
        parts = lax.all_to_all(parts, "seq", split_axis=0, concat_axis=0, tiled=True)
        both = lax.all_gather(parts, ("dp", "blk"), axis=0, tiled=False)
        both = both.reshape(dp_count, blk_count, seq_count, own_rows, w_lanes)
        layers = [parts]
        w_parts = [jnp.transpose(both, (0, 2, 1, 3, 4)).reshape(width, w_lanes)]

    tok_a = gather_near(after(tokens, layers[0]))
    tok_b = swap(tok_a, 1, 0)

    expand_parts = after(expand_weight, layers[0]).astype(BF16)
    expand_parts = expand_parts.reshape(own_rows, dp_count, plane, own_hidden)
    expand_parts = jnp.transpose(expand_parts, (2, 0, 1, 3)).reshape(plane, own_rows, slots)
    expand_parts = lax.all_to_all(expand_parts, PLANE, split_axis=0, concat_axis=0, tiled=True)
    proj_low = after(proj_weight, layers[0]).astype(BF16)
    if pieces:
        proj_moved = [proj_low] + [shift(proj_low, k) for k in range(1, 4)]
    else:
        proj_moved = [proj_low]
    expand_parts = after(expand_parts, *layers, *proj_moved, w_parts[min(1, pieces)], tok_a)
    expand_parts = expand_parts.reshape(2, own_hidden, slots)
    ff_own = jnp.concatenate(
        [
            shrink_weight.astype(BF16),
            jnp.concatenate([expand_parts[0], expand_parts[1]], 1),
        ],
        0,
    )
    ff_all = lax.all_gather(ff_own, "dp", axis=0, tiled=False)

    cot_near = gather_steps(after(cotangent, tok_a))
    cot_a, cot_b = cot_near, swap(cot_near, 1, 0)

    if pieces:
        p_near = gather_steps(jnp.stack(proj_moved))
        hidden_weights = (p_near, swap(p_near, 1, 0), ff_all)
    else:
        w_shrink = ff_all[:, :own_hidden].reshape(slots, width)
        w_expand = jnp.stack([ff_all[:, own_hidden:, :slots], ff_all[:, own_hidden:, slots:]], 1)
        proj_whole = lax.all_gather(proj_low, ALL, axis=0, tiled=True)
        hidden_weights = (proj_whole, w_expand.reshape(width, slots), w_shrink)

    w_parts[0] = after(w_parts[0], ff_own)

    unit_at = jnp.arange(slots) % (width // plane)
    unit_at = unit_at // own_hidden * (plane * own_hidden) + spot * own_hidden + unit_at % own_hidden
    spot_table = (unit_at[:, None] == jnp.arange(width)[None]).astype(BF16)

    wide = 640
    qkv, n1, att, lse, w_qkv, small_full = call(
        partial(forward_kernel, pieces),
        [
            ((length, wide), BF16),
            ((length, width), BF16),
            ((group, half_length), BF16),
            ((4, 3 * rows, 1), F32),
            ((width, wide), BF16),
            ((small_rows, width), F32),
        ],
        [((width, wide), F32)],
        2 * 10**9,
        place, *w_parts, tok_a, tok_b,
    )
    extra = hidden // width
    zero = jnp.zeros((width,), F32)
    bias_expand = small_full[7 : 7 + extra].reshape(dp_count, plane, own_hidden)
    bias_expand = lax.dynamic_index_in_dim(bias_expand, spot, 1, keepdims=False).reshape(1, slots)
    bias_shrink = small_full[7 + extra]
    att_a = after(gather_near(att), bias_expand)
    att_b = swap(att_a, 1, 0)

    big = ((4, rows, width), BF16)
    if pieces:
        hidden_grads = [((dp_count, 2 * own_hidden, width), BF16)]
    else:
        hidden_grads = [((width, slots), BF16), ((slots, width), BF16)]
    out_a, out_b, dn_a, dn_b, mixed, unit, inverse, sums_two, gb_expand, own_proj, *ff_grad = call(
        partial(hidden_kernel, pieces),
        [
            big, big, big, big,
            ((rows, width), F32),
            ((rows, width), F32),
            ((rows, 1), F32),
            ((3, width), F32),
            ((1, slots), F32),
            ((group, width), BF16),
            *hidden_grads,
        ],
        [
            ((width, length), BF16),
            ((slots, width), F32),
            ((width, slots), F32),
            ((width, width), F32),
            ((width, width), BF16),
            ((width, slots), BF16),
            ((slots, width), BF16),
        ],
        6 * 10**9,
        place, tok_a, tok_b, cot_a, cot_b, att_a, att_b, small_full, bias_expand, *hidden_weights,
    )

    dn_both = add_low(dn_a, swap(dn_b, 1, 0))

    cot_wide = cotangent.astype(F32)
    if pieces:
        ff_grad = ff_grad[0]
    else:
        ge = ff_grad[0].reshape(dp_count, 2, own_hidden, slots)
        ff_grad = jnp.concatenate(
            [
                ff_grad[1].reshape(dp_count, own_hidden, width),
                jnp.concatenate([ge[:, 0], ge[:, 1]], 2),
            ],
            1,
        )
    ff_sum = lax.psum_scatter(
        ff_grad.reshape(-1, width), "dp", scatter_dimension=0, tiled=True
    )
    out_both = add_low(out_a, swap(after(out_b, dn_both), 1, 0))

    dn_parts = lax.optimization_barrier((*spread_near(dn_both), out_both))
    d_normed_two = add_all(dn_parts[:4])
    out_both = dn_parts[4]
    d_mixed = cot_wide + norm_pull(unit, inverse, small_full[5], d_normed_two)
    d_branch = d_mixed.astype(BF16)
    db_near = swap(d_branch, 1, 0)
    db_far = swap(d_branch, 2, 0)
    db_cross = swap(db_far, 1, 0)
    out_half = swap(after(out_both[1::2], d_branch), 0, 1)

    if pieces:
        first = ((4, 4, own_rows, 2 * group), BF16)
        second = ((4, 4, own_rows, 256 + group), BF16)
        first, second = [first] * 2, [second] * 2
    else:
        first = [((width, 2 * group), BF16)]
        second = [((width, 256), BF16), ((width, width), BF16)]
    d_low, db_all, *grads = call(
        partial(attention_back_kernel, pieces),
        [((length, wide), BF16), ((half_length, width), BF16), *first],
        [((length, wide), F32), ((width, 2 * group), F32)],
        10 * 10**9,
        place, d_branch, db_far, db_near, db_cross, qkv, lse, n1, own_proj,
    )
    grads = list(lax.optimization_barrier((*grads, out_half)))[:-1]

    def halves(table, lanes):
        table = table.reshape(dp_count, -1, blk_count, own_rows, lanes)
        keep = lax.dynamic_index_in_dim(table, blk, 2, keepdims=False)
        return keep, lax.dynamic_index_in_dim(table, 1 - blk, 2, keepdims=False)

    keep, send = grads if pieces else halves(grads[0], 2 * group)
    g_first = add_low(keep, swap(send, 0, 1))
    out_two = add_low(out_both[0::2], out_half)
    out_last = swap(out_two[1], 2, 0)

    dn_a, dn_b, *grads = call(
        partial(norm_back_kernel, pieces),
        [big, big, *second],
        [((width, 256), F32), ((width, width), F32)],
        6 * 10**9,
        place, after(d_low, out_two), db_all, n1, tok_a, tok_b, att_a, att_b, w_qkv,
        sums_two, gb_expand, spot_table,
    )
    dn_b = after(dn_b, out_last)
    g_first = scatter_dp(g_first)

    if pieces:
        keep, send = grads
    else:
        v_keep, v_send = halves(grads[0], 256)
        gp = grads[1].reshape(dp_count, seq_count, blk_count, own_rows, seq_count, group)
        gp = lax.dynamic_index_in_dim(gp, seq, 1, keepdims=False)
        gp = jnp.transpose(gp, (0, 3, 1, 2, 4))
        p_keep, p_send = halves(gp, group)
        keep = jnp.concatenate([v_keep, p_keep], -1)
        send = jnp.concatenate([v_send, p_send], -1)
    g_got = swap(send, 0, 1)

    dn_both = add_low(dn_a, swap(dn_b, 1, 0))
    dn_two = add_low(dn_both[:2], swap(dn_both[2:], 2, 0))

    ff_sum = after(ff_sum, dn_both)
    sum_shrink = ff_sum[:own_hidden].astype(F32)
    sum_expand = ff_sum[own_hidden:]
    sum_expand = jnp.stack([sum_expand[:, :slots], sum_expand[:, slots:]])
    sum_expand = sum_expand.reshape(plane, own_rows, slots)
    sum_expand = lax.all_to_all(sum_expand, PLANE, split_axis=0, concat_axis=0, tiled=True)

    g_rest = add_low(keep, after(g_got, sum_expand))
    g_rest = scatter_dp(g_rest, dn_two)
    block_out = mixed + (out_two[0].astype(F32) + out_last.astype(F32)) + bias_shrink

    g_all = jnp.concatenate([g_first, g_rest[:, :, : group + small_rows]], -1).astype(BF16)
    g_all = lax.all_to_all(g_all, "seq", split_axis=0, concat_axis=0, tiled=True).astype(F32)
    sum_proj = jnp.transpose(g_rest[:, :, 256:], (1, 0, 2)).reshape(own_rows, width)
    sum_small = jnp.sum(g_all[:, :, 3 * group :], 0).T
    sum_qkv = jnp.transpose(
        g_all[:, :, : 3 * group].reshape(seq_count, own_rows, 3, group), (1, 2, 0, 3)
    ).reshape(own_rows, 3 * width)
    sum_expand = jnp.transpose(
        sum_expand.reshape(plane, own_rows, dp_count, own_hidden), (1, 2, 0, 3)
    ).reshape(own_rows, hidden).astype(F32)

    d_normed_one = dn_two[0].astype(F32) + swap(dn_two[1], 0, 1).astype(F32)
    unit, inverse = norm_parts(tokens.astype(F32))
    token_grad = d_mixed + norm_pull(unit, inverse, small_full[0], d_normed_one)

    qkv_out = adam_update(
        qkv_weight, qkv_first, qkv_second, sum_qkv, matrix_rate, matrix_decay
    )
    proj_out = adam_update(
        proj_weight, proj_first, proj_second, sum_proj, matrix_rate, matrix_decay
    )
    expand_out = adam_update(
        expand_weight, expand_first, expand_second, sum_expand, matrix_rate, matrix_decay
    )
    shrink_out = adam_update(
        shrink_weight, shrink_first, shrink_second, sum_shrink, matrix_rate, matrix_decay
    )
    small_out = adam_update(
        small_params, small_first, small_second, sum_small, small_rate, 0.0
    )
    return (block_out, token_grad, *qkv_out, *proj_out, *expand_out, *shrink_out, *small_out)


def solution(mesh):
    by_rows = P(ALL, None)
    by_columns = P(None, ALL)
    state = (by_rows,) * 4 + (by_columns,)
    return jax.shard_map(
        shards,
        mesh=mesh,
        in_specs=(by_rows, by_rows) + state * 3,
        out_specs=(by_rows,) * 14 + (by_columns,) * 3,
        check_vma=False,
    )
```

```python
from functools import partial
import math

import jax
import jax.numpy as jnp
from jax import lax
from jax.experimental import pallas as pl
from jax.experimental.pallas import tpu as pltpu
from jax.sharding import PartitionSpec as P

HEAD = 64
STEP = 10

norm_eps = 1e-05
beta_one = 0.9
beta_two = 0.95
adam_eps = 1e-08
matrix_rate = 0.05
matrix_decay = 0.1
small_rate = 0.5
masked_score = -1e30
score_scale = 1.0 / math.sqrt(HEAD)

F32 = jnp.float32
BF16 = jnp.bfloat16
ALL = ("dp", "seq", "blk")
PLANE = ("seq", "blk")
VMEM_LIMIT = 56 * 1024 * 1024
NT = (((1,), (1,)), ((), ()))
TN = (((0,), (0,)), ((), ()))


def dot(a, b, dims=None):
    if dims is None:
        return jnp.dot(a, b, preferred_element_type=F32)
    return lax.dot_general(a, b, dims, preferred_element_type=F32)


def adam_update(weight, first_state, second, gradient, step_rate, decay_rate):
    moment = beta_one * first_state + (1.0 - beta_one) * gradient
    variance = beta_two * second + (1.0 - beta_two) * gradient * gradient
    mean_fixed = moment / (1.0 - beta_one**STEP)
    var_fixed = variance / (1.0 - beta_two**STEP)
    updated = weight - step_rate * (
        mean_fixed / (jnp.sqrt(var_fixed) + adam_eps) + decay_rate * weight
    )
    return (moment, variance, updated)


def norm_parts(values):
    center = jnp.mean(values, -1, keepdims=True)
    spread = values - center
    inverse = lax.rsqrt(jnp.mean(spread * spread, -1, keepdims=True) + norm_eps)
    return spread * inverse, inverse


def norm_pull(unit, inverse, gain, grad):
    scaled = grad * gain
    first = jnp.mean(scaled, -1, keepdims=True)
    second = jnp.mean(scaled * unit, -1, keepdims=True)
    return inverse * (scaled - first - unit * second)


def swap(value, seq_bits, blk_bits):
    seq_count, blk_count = lax.axis_size("seq"), lax.axis_size("blk")
    pairs = [
        (i * blk_count + j, (i ^ seq_bits) * blk_count + (j ^ blk_bits))
        for i in range(seq_count)
        for j in range(blk_count)
    ]
    return lax.ppermute(value, PLANE, pairs)


def shift(value, step):
    count = lax.axis_size("dp")
    return lax.ppermute(value, "dp", [(i, (i + step) % count) for i in range(count)])


def gather_near(value):
    return jnp.stack([value, swap(value, 0, 1), swap(value, 2, 0), swap(value, 2, 1)])


def after(value, *others):
    return lax.optimization_barrier((value, *others))[0]


def together(*values):
    return lax.optimization_barrier(values)


def gather_steps(value):
    two = jnp.stack([value, swap(value, 0, 1)])
    return jnp.concatenate([two, swap(two, 2, 0)], 0)


def add_low(a, b):
    return (a.astype(F32) + b.astype(F32)).astype(BF16)


def spread_near(both):
    return both[0], swap(both[1], 0, 1), swap(both[2], 2, 0), swap(both[3], 2, 1)


def add_all(parts):
    total = parts[0].astype(F32)
    for part in parts[1:]:
        total = total + part.astype(F32)
    return total


def spread_dp(value):
    count = lax.axis_size("dp")
    if count != 4:
        return [lax.psum_scatter(value, "dp", scatter_dimension=0, tiled=False)]
    me = lax.axis_index("dp")
    parts = [lax.dynamic_index_in_dim(value, me, 0, keepdims=False)]
    for k in range(1, count):
        chunk = lax.dynamic_index_in_dim(value, (me + k) % count, 0, keepdims=False)
        parts.append(shift(chunk, k))
    return parts


def head_masks(first, group):
    lane = lax.broadcasted_iota(jnp.int32, (1, 256), 1) - first
    return [(lane >= h * HEAD) & (lane < (h + 1) * HEAD) for h in range(group // HEAD)]


def turned(block):
    return pltpu.roll(block.astype(F32), 64, 1).astype(BF16)


def spread_heads(block, masks):
    return jnp.concatenate([jnp.where(m, block, jnp.zeros_like(block)) for m in masks], 0)


def join_heads(stacked, masks):
    rows = stacked.shape[0] // len(masks)
    out = jnp.where(masks[0], stacked[:rows], 0.0)
    for h in range(1, len(masks)):
        out = out + jnp.where(masks[h], stacked[h * rows : (h + 1) * rows], 0.0)
    return out


def visible(heads, rows, keys, first_row):
    row = lax.broadcasted_iota(jnp.int32, (heads, rows, keys), 1).reshape(heads * rows, keys)
    key = lax.broadcasted_iota(jnp.int32, (heads * rows, keys), 1)
    return key <= row + first_row


def both_rows(tok_all, at, half):
    rows = [tok_all[2 * at + half], tok_all[2 * at + 1 - half]]
    return jnp.concatenate(rows, 0).astype(F32)


def forward_kernel(pieces, place, *refs):
    me, half, layer = place[0], place[1], place[2]
    w_parts, refs = refs[: max(1, 2 * pieces)], refs[max(1, 2 * pieces) :]
    tok_all, qkv_ref, n1_ref, att_ref, lse_ref, w_ref, small_ref, w32 = refs
    rows = tok_all.shape[1]
    group = att_ref.shape[0]
    wide = w32.shape[1]
    tail = wide - 128
    w32[:, tail:wide] = jnp.zeros((w32.shape[0], 128), F32)
    if pieces == 0:
        w32[:, : w_parts[0].shape[1]] = w_parts[0][...].astype(F32)
    for k in range(pieces):
        own_layer = lax.rem(layer + (pieces - k), pieces)
        for other in range(2):
            part = w_parts[2 * k + other]
            for j in range(4):
                owner = (own_layer * 4 + (me ^ j)) * 2 + (half ^ other)
                count = part.shape[1]
                where = pl.ds(pl.multiple_of(owner * count, 8), count)
                w32[where, : part.shape[2]] = part[j].astype(F32)
    w_low = w32[...].astype(BF16)
    w_ref[...] = w_low
    first = 3 * group - tail
    small = w32[:, tail:wide].T
    small_ref[...] = small[first : first + small_ref.shape[0]]
    width = small_ref.shape[1]
    turned_small = pltpu.roll(small[first : first + 8], width - me * group, 1)
    bias = jnp.concatenate(
        [
            turned_small[2:3, :group],
            jnp.zeros((1, group), F32),
            turned_small[3:4, :group],
            jnp.zeros((1, wide - 3 * group), F32),
        ],
        1,
    )
    gain, lift = small_ref[0:1, :], small_ref[1:2, :]
    for bit in range(2):
        for far in range(2):
            at = me ^ (2 * far + bit)
            unit, _ = norm_parts(both_rows(tok_all, at, half))
            n1 = (unit * gain + lift).astype(BF16)
            out = (dot(n1, w_low) + bias).astype(BF16)
            for other in range(2):
                where = pl.ds(pl.multiple_of((2 * at + (half ^ other)) * rows, rows), rows)
                n1_ref[where, :] = n1[other * rows : (other + 1) * rows]
                qkv_ref[where, :] = out[other * rows : (other + 1) * rows]
    shifted, plain = head_masks(64, group), head_masks(0, group)
    heads = len(plain)
    for i in range(4):
        keys = 2 * rows * (i + 1)
        where = pl.ds(pl.multiple_of((2 * i + half) * rows, rows), rows)
        queries = spread_heads(turned(qkv_ref[where, 0:256]), shifted)
        scores = dot(queries, qkv_ref[0:keys, 128:384], NT) * score_scale
        seen = visible(heads, rows, keys, (2 * i + half) * rows)
        scores = jnp.where(seen, scores, masked_score)
        top = jnp.max(scores, -1, keepdims=True)
        raised = jnp.exp(scores - top)
        total = jnp.sum(raised, -1, keepdims=True)
        probs = (raised / total).astype(BF16)
        result = join_heads(dot(probs, qkv_ref[0:keys, 384:640]), plain)
        att_ref[:, i * rows : (i + 1) * rows] = result.T[:group].astype(BF16)
        lse_ref[i] = top + jnp.log(total)


def hidden_kernel(
    pieces, place, tok_all, cot_a, cot_b, att_a, att_b, vec_ref, be_ref, *refs
):
    given, refs = refs[:3], refs[3:]
    out_a, out_b, dn_a, dn_b, mixed_ref, unit_ref, inverse_ref, sums_ref, gb_ref, own_ref = refs[:10]
    g_outs, refs = refs[10:-11], refs[-11:]
    att_all, gs_sum, ge_sum, p32, proj_ref, we_ref, ws_ref, act_all, pre_all, n2_all, cot_all = refs
    me, half, layer = place[0], place[1], place[2]
    if pieces == 0:
        p32[...] = given[0][...].astype(F32)
        we_ref[...] = given[1][...]
        ws_ref[...] = given[2][...]
    else:
        p_parts, ff_ref = given[:2], given[2]
        slots, part = ws_ref.shape[0], ws_ref.shape[0] // pieces
        for k in range(pieces):
            ws_ref[k * part : (k + 1) * part, :] = ff_ref[k, 0:part, :]
            for side in range(2):
                we_ref[(2 * k + side) * part : (2 * k + side + 1) * part, :] = ff_ref[
                    k, part:, side * slots : (side + 1) * slots
                ]
        for bit in range(2):
            for j in range(4):
                for k in range(pieces):
                    own_layer = lax.rem(layer + (pieces - k), pieces)
                    owner = (own_layer * 4 + (me ^ ((j & 2) + bit))) * 2 + (half ^ (j & 1))
                    count = p_parts[bit].shape[2]
                    where = pl.ds(pl.multiple_of(owner * count, 8), count)
                    p32[where, :] = p_parts[bit][j, k].astype(F32)
    proj_ref[...] = p32[...].astype(BF16)
    rows = tok_all.shape[1]
    span = 4 * rows
    group = att_a.shape[1]
    for bit in range(2):
        att = (att_a, att_b)[bit]
        for far in range(2):
            at = me ^ (2 * far + bit)
            where = pl.ds(pl.multiple_of(at * group, 64), group)
            if bit == 0 and far == 0:
                own_ref[0:group, :] = p32[where, :].astype(BF16)
                own_ref[group:, :] = jnp.zeros((own_ref.shape[0] - group, own_ref.shape[1]), BF16)
            for other in range(2):
                att_all[where, other * span : (other + 1) * span] = att[2 * far + other]
    bias_proj, gain, lift = vec_ref[4:5, :], vec_ref[5:6, :], vec_ref[6:7, :]
    sums = [jnp.zeros((1, gain.shape[1]), F32)] * 2
    gb = jnp.zeros((1, gb_ref.shape[1]), F32)
    sums_ref[2:3, :] = jnp.sum(cot_a[0].astype(F32), 0, keepdims=True)
    for bit in range(2):
        cot, out, dn = (cot_a, cot_b)[bit], (out_a, out_b)[bit], (dn_a, dn_b)[bit]
        for far in range(2):
            start = pl.multiple_of((me ^ (2 * far + bit)) * rows, rows)
            att = jnp.concatenate(
                [
                    att_all[:, pl.ds(start, rows)],
                    att_all[:, pl.ds(pl.multiple_of(span + start, rows), rows)],
                ],
                1,
            )
            two = both_rows(tok_all, me ^ (2 * far + bit), half)
            mixed = two + (dot(att, proj_ref[...], TN) + bias_proj)
            if bit == 0 and far == 0:
                mixed_ref[...] = mixed[:rows]
            unit, inverse = norm_parts(mixed)
            if bit == 0 and far == 0:
                unit_ref[...] = unit[:rows]
                inverse_ref[...] = inverse[:rows]
            n2 = (unit * gain + lift).astype(BF16)
            pre = dot(n2, we_ref[...]) + be_ref[...]
            cots = cot[2 * far : 2 * far + 2].reshape(2 * rows, -1)
            factor = math.sqrt(2.0 / math.pi)
            square = pre * pre
            bent = jnp.tanh(factor * pre * (1.0 + 0.044715 * square))
            act = (0.5 * pre * (1.0 + bent)).astype(BF16)
            slope = 0.5 * (1.0 + bent) + 0.5 * pre * (1.0 - bent * bent) * (
                factor * (1.0 + 3.0 * 0.044715 * square)
            )
            d_act = dot(cots, ws_ref[...], NT)
            d_pre32 = d_act * slope
            d_pre = d_pre32.astype(BF16)
            d_n2 = dot(d_pre, we_ref[...], NT)
            dn[2 * far : 2 * far + 2] = d_n2.astype(BF16).reshape(2, rows, -1)
            out[2 * far : 2 * far + 2] = dot(act, ws_ref[...]).astype(BF16).reshape(2, rows, -1)
            step = pl.ds((2 * bit + far) * 2 * rows, 2 * rows)
            act_all[step, :] = act
            pre_all[step, :] = d_pre
            n2_all[step, :] = n2
            cot_all[step, :] = cots
            sums[0] = sums[0] + jnp.sum(d_n2 * unit, 0, keepdims=True)
            sums[1] = sums[1] + jnp.sum(d_n2, 0, keepdims=True)
            gb = gb + jnp.sum(d_pre.astype(F32), 0, keepdims=True)
    gs_sum[...] = dot(act_all[...], cot_all[...], TN)
    ge_sum[...] = dot(n2_all[...], pre_all[...], TN)
    sums_ref[0:1, :] = sums[0]
    sums_ref[1:2, :] = sums[1]
    gb_ref[...] = gb
    if pieces == 0:
        g_outs[0][...] = ge_sum[...].astype(BF16)
        g_outs[1][...] = gs_sum[...].astype(BF16)
        return
    pack = g_outs[0]
    for k in range(pieces):
        pack[k, 0:part, :] = gs_sum[k * part : (k + 1) * part, :].astype(BF16)
        for side in range(2):
            pack[k, part:, side * slots : (side + 1) * slots] = ge_sum[
                (2 * k + side) * part : (2 * k + side + 1) * part, :
            ].astype(BF16)


def split_halves(table, keep, send, half, row_of, lanes, at=0):
    layers, four, count, _ = keep.shape
    for k in range(layers):
        for j in range(four):
            base = row_of(k, j) * 2
            for out, owner in ((keep, base + half), (send, base + 1 - half)):
                where = pl.ds(pl.multiple_of(owner * count, 8), count)
                out[k, j, :, at : at + lanes] = table(where, j).astype(BF16)


def attention_back_kernel(
    pieces, place, db_own, db_far, db_near, db_cross, qkv_ref, lse_ref, n1_ref, own_proj, *refs
):
    d_ref, db_all, outs, (d_all, g_all) = refs[0], refs[1], refs[2:-2], refs[-2:]
    me, half = place[0], place[1]
    rows = db_own.shape[0]
    group = 3 * HEAD
    shifted, plain = head_masks(64, group), head_masks(0, group)
    heads = len(plain)
    for bits, db in ((0, db_own), (2, db_far), (1, db_near), (3, db_cross)):
        db_all[pl.ds(pl.multiple_of((me ^ bits) * rows, rows), rows), :] = db[...]
    d_all[...] = jnp.zeros_like(d_all)
    for i in range(4):
        keys = 2 * rows * (i + 1)
        where = pl.ds(pl.multiple_of((2 * i + half) * rows, rows), rows)
        queries = spread_heads(turned(qkv_ref[where, 0:256]), shifted)
        d_att = dot(db_all[i * rows : (i + 1) * rows, :], own_proj[...], NT).astype(BF16)
        grads = spread_heads(d_att, plain)
        key_rows, values = qkv_ref[0:keys, 128:384], qkv_ref[0:keys, 384:640]
        scores = dot(queries, key_rows, NT) * score_scale
        seen = visible(heads, rows, keys, (2 * i + half) * rows)
        probs = jnp.where(seen, jnp.exp(scores - lse_ref[i]), 0.0)
        weighed = probs * dot(grads, values, NT)
        d_scores = (weighed - probs * jnp.sum(weighed, -1, keepdims=True)).astype(BF16)
        dq = join_heads(dot(d_scores, key_rows), shifted) * score_scale
        d_all[where, 0:256] += pltpu.roll(dq, 192, 1)
        d_all[0:keys, 128:384] += dot(d_scores, queries, TN) * score_scale
        d_all[0:keys, 384:640] += dot(probs.astype(BF16), grads, TN)
    d_ref[...] = d_all[...].astype(BF16)
    g_all[...] = dot(n1_ref[...], d_ref[:, 0 : 2 * group], TN)
    if pieces == 0:
        outs[0][...] = g_all[...].astype(BF16)
    else:
        split_halves(
            lambda where, j: g_all[where, :], outs[0], outs[1], half, lambda k, j: k * 4 + j, 2 * group
        )


def norm_back_kernel(
    pieces, place, d_ref, db_all, n1_ref, tok_all, att_a, att_b, w_ref, two_ref, gb_ref, spot_ref,
    dn_a, dn_b, *refs
):
    outs, (g_all, gp_all) = refs[:-2], refs[-2:]
    me, half = place[0], place[1]
    rows = tok_all.shape[1]
    group = att_a.shape[1]
    wide, width = d_ref.shape[1], n1_ref.shape[1]
    sums = [jnp.zeros((1, width), F32)] * 2
    for bit in range(2):
        dn = (dn_a, dn_b)[bit]
        for far in range(2):
            at = me ^ (2 * far + bit)
            gp_all[pl.ds(pl.multiple_of(at * group, 64), group), :] = dot(
                (att_a, att_b)[bit][2 * far], db_all[...]
            )
            for other in range(2):
                where = pl.ds(pl.multiple_of((2 * at + (half ^ other)) * rows, rows), rows)
                d_n1 = dot(d_ref[where, :], w_ref[...], NT)
                unit, _ = norm_parts(tok_all[2 * at + (half ^ other)].astype(F32))
                dn[2 * far + other] = d_n1.astype(BF16)
                sums[0] = sums[0] + jnp.sum(d_n1 * unit, 0, keepdims=True)
                sums[1] = sums[1] + jnp.sum(d_n1, 0, keepdims=True)
    heads_sum = jnp.sum(d_ref[...].astype(F32), 0, keepdims=True)

    def at_heads(row):
        row = jnp.concatenate([row, jnp.zeros((1, width - group), F32)], 1)
        return pltpu.roll(jnp.broadcast_to(row, (8, width)), me * group, 1)[0:1]

    head_q, head_v = at_heads(heads_sum[:, :group]), at_heads(heads_sum[:, 2 * group : 3 * group])
    index = lax.broadcasted_iota(jnp.int32, (16, width), 0)
    small = jnp.where(index == 0, sums[0], 0.0)
    small = jnp.where(index == 1, sums[1], small)
    own = db_all[pl.ds(pl.multiple_of(me * rows, rows), rows), :].astype(F32)
    small = jnp.where(index == 4, jnp.sum(own, 0, keepdims=True), small)
    slots = gb_ref.shape[1]
    block = lax.broadcasted_iota(jnp.int32, (16, slots), 1) - 96 * (
        lax.broadcasted_iota(jnp.int32, (16, slots), 0) - 7
    )
    hidden_rows = jnp.where((block >= 0) & (block < 96), gb_ref[...], 0.0).astype(BF16)
    small = small + dot(hidden_rows, spot_ref[...])
    small = jnp.where(index == 5, two_ref[0:1, :], small)
    small = jnp.where(index == 6, two_ref[1:2, :], small)
    small = jnp.where(index == 7 + slots // 96, two_ref[2:3, :], small)
    small = jnp.where(index == 2, head_q, small)
    small = jnp.where(index == 3, head_v, small).astype(BF16)
    row = lax.broadcasted_iota(jnp.int32, (16, 256), 0)
    lane = lax.broadcasted_iota(jnp.int32, (16, 256), 1)
    spread = (lane == row + group).astype(F32).astype(BF16)
    g_all[...] = dot(n1_ref[...], d_ref[:, 2 * group :], TN) + dot(small, spread, TN)
    if pieces == 0:
        outs[0][...] = g_all[...].astype(BF16)
        outs[1][...] = gp_all[...].astype(BF16)
        return
    split_halves(
        lambda where, j: g_all[where, :], outs[0], outs[1], half, lambda k, j: k * 4 + j, 256
    )

    def chunk(where, j):
        start = j * group
        block = gp_all[where, start // 128 * 128 : start // 128 * 128 + 256]
        if start % 128:
            block = pltpu.roll(block, 256 - start % 128, 1)
        return block[:, :group]

    split_halves(chunk, outs[0], outs[1], half, lambda k, j: k * 4 + me, group, 256)


def call(kernel, outs, scratch, flops, *args):
    whole = pl.BlockSpec(memory_space=pltpu.VMEM)
    specs = [pl.BlockSpec(memory_space=pltpu.SMEM)] + [whole] * (len(args) - 1)
    moved = sum(math.prod(a.shape) * a.dtype.itemsize for a in args)
    return pl.pallas_call(
        kernel,
        out_shape=[jax.ShapeDtypeStruct(shape, kind) for shape, kind in outs],
        in_specs=specs,
        out_specs=[whole] * len(outs),
        scratch_shapes=[pltpu.VMEM(shape, kind) for shape, kind in scratch],
        compiler_params=pltpu.CompilerParams(vmem_limit_bytes=VMEM_LIMIT),
        cost_estimate=pl.CostEstimate(flops=flops, bytes_accessed=moved, transcendentals=10**6),
    )(*args)


def shards(
    tokens,
    cotangent,
    qkv_weight,
    proj_weight,
    expand_weight,
    shrink_weight,
    small_params,
    qkv_first,
    proj_first,
    expand_first,
    shrink_first,
    small_first,
    qkv_second,
    proj_second,
    expand_second,
    shrink_second,
    small_second,
):
    rows, width = tokens.shape
    hidden = expand_weight.shape[1]
    own_rows = qkv_weight.shape[0]
    own_hidden = shrink_weight.shape[0]
    dp_count, seq_count, blk_count = (lax.axis_size(a) for a in ALL)
    plane = seq_count * blk_count
    assert (seq_count, blk_count) == (4, 2)
    dp, seq, blk = (lax.axis_index(a) for a in ALL)
    spot = seq * blk_count + blk
    group = width // seq_count
    slots = hidden // plane
    length = plane * rows
    half_length = length // blk_count
    small_rows = small_params.shape[0]
    place = jnp.stack([seq, blk, dp]).astype(jnp.int32)

    w_lanes = 3 * group + small_rows
    parts = qkv_weight.astype(BF16).reshape(own_rows, 3, seq_count, group)
    parts = jnp.transpose(parts, (2, 0, 1, 3)).reshape(seq_count, own_rows, 3 * group)
    small_part = jnp.broadcast_to(
        small_params.T.astype(BF16), (seq_count, own_rows, small_rows)
    )
    parts = jnp.concatenate([parts, small_part], 2)
    pieces = 4 if dp_count == 4 and own_rows % 8 == 0 else 0
    if pieces:
        picked = [lax.dynamic_index_in_dim(parts, seq ^ k, 0, keepdims=False) for k in range(4)]
        near = jnp.stack([picked[0]] + [swap(picked[k], k, 0) for k in range(1, 4)])
        layers = [near] + [shift(near, k) for k in range(1, 4)]
        w_parts = []
        for part in layers:
            w_parts += [part, swap(part, 0, 1)]
    else:
        parts = lax.all_to_all(parts, "seq", split_axis=0, concat_axis=0, tiled=True)
        both = lax.all_gather(parts, ("dp", "blk"), axis=0, tiled=False)
        both = both.reshape(dp_count, blk_count, seq_count, own_rows, w_lanes)
        layers = [parts]
        w_parts = [jnp.transpose(both, (0, 2, 1, 3, 4)).reshape(width, w_lanes)]

    tok_all = lax.all_gather(tokens, PLANE, axis=0, tiled=False)

    expand_parts = after(expand_weight, layers[0]).astype(BF16)
    expand_parts = expand_parts.reshape(own_rows, dp_count, plane, own_hidden)
    expand_parts = jnp.transpose(expand_parts, (2, 0, 1, 3)).reshape(plane, own_rows, slots)
    expand_parts = lax.all_to_all(expand_parts, PLANE, split_axis=0, concat_axis=0, tiled=True)
    proj_low = after(proj_weight, layers[0]).astype(BF16)
    if pieces:
        proj_moved = [proj_low] + [shift(proj_low, k) for k in range(1, 4)]
    else:
        proj_moved = [proj_low]
    expand_parts = after(expand_parts, *layers, *proj_moved, w_parts[min(1, pieces)], tok_all)
    expand_parts = expand_parts.reshape(2, own_hidden, slots)
    ff_own = jnp.concatenate(
        [
            shrink_weight.astype(BF16),
            jnp.concatenate([expand_parts[0], expand_parts[1]], 1),
        ],
        0,
    )
    ff_all = lax.all_gather(ff_own, "dp", axis=0, tiled=False)

    cot_near = gather_steps(after(cotangent, layers[-1]))
    cot_a, cot_b = cot_near, swap(cot_near, 1, 0)

    if pieces:
        p_near = gather_steps(jnp.stack(proj_moved))
        hidden_weights = (p_near, swap(p_near, 1, 0), ff_all)
    else:
        w_shrink = ff_all[:, :own_hidden].reshape(slots, width)
        w_expand = jnp.stack([ff_all[:, own_hidden:, :slots], ff_all[:, own_hidden:, slots:]], 1)
        proj_whole = lax.all_gather(proj_low, ALL, axis=0, tiled=True)
        hidden_weights = (proj_whole, w_expand.reshape(width, slots), w_shrink)

    w_parts[0] = after(w_parts[0], ff_own)

    unit_at = jnp.arange(slots) % (width // plane)
    unit_at = unit_at // own_hidden * (plane * own_hidden) + spot * own_hidden + unit_at % own_hidden
    spot_table = (unit_at[:, None] == jnp.arange(width)[None]).astype(BF16)

    wide = 640
    qkv, n1, att, lse, w_qkv, small_full = call(
        partial(forward_kernel, pieces),
        [
            ((length, wide), BF16),
            ((length, width), BF16),
            ((group, half_length), BF16),
            ((4, 3 * rows, 1), F32),
            ((width, wide), BF16),
            ((small_rows, width), F32),
        ],
        [((width, wide), F32)],
        2 * 10**9,
        place, *w_parts, tok_all,
    )
    extra = hidden // width
    zero = jnp.zeros((width,), F32)
    bias_expand = small_full[7 : 7 + extra].reshape(dp_count, plane, own_hidden)
    bias_expand = lax.dynamic_index_in_dim(bias_expand, spot, 1, keepdims=False).reshape(1, slots)
    bias_shrink = small_full[7 + extra]
    att_a = after(gather_near(att), bias_expand)
    att_b = swap(att_a, 1, 0)

    big = ((4, rows, width), BF16)
    if pieces:
        hidden_grads = [((dp_count, 2 * own_hidden, width), BF16)]
    else:
        hidden_grads = [((width, slots), BF16), ((slots, width), BF16)]
    out_a, out_b, dn_a, dn_b, mixed, unit, inverse, sums_two, gb_expand, own_proj, *ff_grad = call(
        partial(hidden_kernel, pieces),
        [
            big, big, big, big,
            ((rows, width), F32),
            ((rows, width), F32),
            ((rows, 1), F32),
            ((3, width), F32),
            ((1, slots), F32),
            ((256, width), BF16),
            *hidden_grads,
        ],
        [
            ((width, length), BF16),
            ((slots, width), F32),
            ((width, slots), F32),
            ((width, width), F32),
            ((width, width), BF16),
            ((width, slots), BF16),
            ((slots, width), BF16),
            ((length, slots), BF16),
            ((length, slots), BF16),
            ((length, width), BF16),
            ((length, width), BF16),
        ],
        6 * 10**9,
        place, tok_all, cot_a, cot_b, att_a, att_b, small_full, bias_expand, *hidden_weights,
    )

    dn_both = add_low(dn_a, swap(dn_b, 1, 0))

    cot_wide = cotangent.astype(F32)
    if pieces:
        ff_grad = ff_grad[0]
    else:
        ge = ff_grad[0].reshape(dp_count, 2, own_hidden, slots)
        ff_grad = jnp.concatenate(
            [
                ff_grad[1].reshape(dp_count, own_hidden, width),
                jnp.concatenate([ge[:, 0], ge[:, 1]], 2),
            ],
            1,
        )
    ff_sum = lax.psum_scatter(
        ff_grad.reshape(-1, width), "dp", scatter_dimension=0, tiled=True
    )
    out_both = add_low(out_a, swap(after(out_b, dn_both), 1, 0))

    dn_parts = lax.optimization_barrier((*spread_near(dn_both), out_both))
    d_normed_two = add_all(dn_parts[:4])
    out_both = dn_parts[4]
    d_mixed = cot_wide + norm_pull(unit, inverse, small_full[5], d_normed_two)
    d_branch = d_mixed.astype(BF16)
    db_near = swap(d_branch, 1, 0)
    db_far = swap(d_branch, 2, 0)
    db_cross = swap(db_far, 1, 0)
    out_half = swap(after(out_both[1::2], d_branch), 0, 1)

    if pieces:
        first = ((4, 4, own_rows, 2 * group), BF16)
        second = ((4, 4, own_rows, 256 + group), BF16)
        first, second = [first] * 2, [second] * 2
    else:
        first = [((width, 2 * group), BF16)]
        second = [((width, 256), BF16), ((width, width), BF16)]
    d_low, db_all, *grads = call(
        partial(attention_back_kernel, pieces),
        [((length, wide), BF16), ((half_length, width), BF16), *first],
        [((length, wide), F32), ((width, 2 * group), F32)],
        10 * 10**9,
        place, d_branch, db_far, db_near, db_cross, qkv, lse, n1, own_proj,
    )
    grads = list(lax.optimization_barrier((*grads, out_half)))[:-1]

    def halves(table, lanes):
        table = table.reshape(dp_count, -1, blk_count, own_rows, lanes)
        keep = lax.dynamic_index_in_dim(table, blk, 2, keepdims=False)
        return keep, lax.dynamic_index_in_dim(table, 1 - blk, 2, keepdims=False)

    keep, send = grads if pieces else halves(grads[0], 2 * group)
    g_first = add_low(keep, swap(send, 0, 1))
    out_two = add_low(after(out_both, d_low)[0::2], out_half)
    out_last = swap(out_two[1], 2, 0)

    dn_a, dn_b, *grads = call(
        partial(norm_back_kernel, pieces),
        [big, big, *second],
        [((width, 256), F32), ((width, width), F32)],
        6 * 10**9,
        place, after(d_low, out_two), db_all, n1, tok_all, att_a, att_b, w_qkv,
        sums_two, gb_expand, spot_table,
    )
    if pieces:
        keep, send = grads
    else:
        v_keep, v_send = halves(grads[0], 256)
        gp = grads[1].reshape(dp_count, seq_count, blk_count, own_rows, seq_count, group)
        gp = lax.dynamic_index_in_dim(gp, seq, 1, keepdims=False)
        gp = jnp.transpose(gp, (0, 3, 1, 2, 4))
        p_keep, p_send = halves(gp, group)
        keep = jnp.concatenate([v_keep, p_keep], -1)
        send = jnp.concatenate([v_send, p_send], -1)
    g_first, keep, send, dn_a, dn_b, out_last = together(g_first, keep, send, dn_a, dn_b, out_last)
    first_parts = spread_dp(g_first)
    g_got = swap(send, 0, 1)
    dn_got = swap(dn_b, 1, 0)
    *first_parts, keep, g_got, dn_a, dn_got = together(*first_parts, keep, g_got, dn_a, dn_got)

    rest_parts = spread_dp(add_low(keep, g_got))
    dn_parts = spread_near(add_low(dn_a, dn_got))
    g_first = add_all(first_parts)
    *rest_parts, dn_0, dn_1, dn_2, dn_3 = together(*rest_parts, *dn_parts)
    g_rest = add_all(rest_parts)

    ff_sum = after(ff_sum, dn_0)
    sum_shrink = ff_sum[:own_hidden].astype(F32)
    sum_expand = ff_sum[own_hidden:]
    sum_expand = jnp.stack([sum_expand[:, :slots], sum_expand[:, slots:]])
    sum_expand = sum_expand.reshape(plane, own_rows, slots)
    sum_expand = lax.all_to_all(sum_expand, PLANE, split_axis=0, concat_axis=0, tiled=True)
    block_out = mixed + (out_two[0].astype(F32) + out_last.astype(F32)) + bias_shrink

    g_all = jnp.concatenate([g_first, g_rest[:, :, : group + small_rows]], -1).astype(BF16)
    g_all = lax.all_to_all(g_all, "seq", split_axis=0, concat_axis=0, tiled=True).astype(F32)
    sum_proj = jnp.transpose(g_rest[:, :, 256:], (1, 0, 2)).reshape(own_rows, width)
    sum_small = jnp.sum(g_all[:, :, 3 * group :], 0).T
    sum_qkv = jnp.transpose(
        g_all[:, :, : 3 * group].reshape(seq_count, own_rows, 3, group), (1, 2, 0, 3)
    ).reshape(own_rows, 3 * width)
    sum_expand = jnp.transpose(
        sum_expand.reshape(plane, own_rows, dp_count, own_hidden), (1, 2, 0, 3)
    ).reshape(own_rows, hidden).astype(F32)

    d_normed_one = add_all((dn_0, dn_1, dn_2, dn_3))
    unit, inverse = norm_parts(tokens.astype(F32))
    token_grad = d_mixed + norm_pull(unit, inverse, small_full[0], d_normed_one)

    qkv_out = adam_update(
        qkv_weight, qkv_first, qkv_second, sum_qkv, matrix_rate, matrix_decay
    )
    proj_out = adam_update(
        proj_weight, proj_first, proj_second, sum_proj, matrix_rate, matrix_decay
    )
    expand_out = adam_update(
        expand_weight, expand_first, expand_second, sum_expand, matrix_rate, matrix_decay
    )
    shrink_out = adam_update(
        shrink_weight, shrink_first, shrink_second, sum_shrink, matrix_rate, matrix_decay
    )
    small_out = adam_update(
        small_params, small_first, small_second, sum_small, small_rate, 0.0
    )
    return (block_out, token_grad, *qkv_out, *proj_out, *expand_out, *shrink_out, *small_out)


def solution(mesh):
    by_rows = P(ALL, None)
    by_columns = P(None, ALL)
    state = (by_rows,) * 4 + (by_columns,)
    return jax.shard_map(
        shards,
        mesh=mesh,
        in_specs=(by_rows, by_rows) + state * 3,
        out_specs=(by_rows,) * 14 + (by_columns,) * 3,
        check_vma=False,
    )
```

```python
from functools import partial
import math

import jax
import jax.numpy as jnp
from jax import lax
from jax.experimental import pallas as pl
from jax.experimental.pallas import tpu as pltpu
from jax.sharding import PartitionSpec as P

HEAD = 64
STEP = 10

norm_eps = 1e-05
beta_one = 0.9
beta_two = 0.95
adam_eps = 1e-08
matrix_rate = 0.05
matrix_decay = 0.1
small_rate = 0.5
masked_score = -1e30
score_scale = 1.0 / math.sqrt(HEAD)

F32 = jnp.float32
BF16 = jnp.bfloat16
ALL = ("dp", "seq", "blk")
PLANE = ("seq", "blk")
VMEM_LIMIT = 56 * 1024 * 1024
NT = (((1,), (1,)), ((), ()))
TN = (((0,), (0,)), ((), ()))


def dot(a, b, dims=None):
    if dims is None:
        return jnp.dot(a, b, preferred_element_type=F32)
    return lax.dot_general(a, b, dims, preferred_element_type=F32)


def adam_update(weight, first_state, second, gradient, step_rate, decay_rate):
    moment = beta_one * first_state + (1.0 - beta_one) * gradient
    variance = beta_two * second + (1.0 - beta_two) * gradient * gradient
    mean_fixed = moment / (1.0 - beta_one**STEP)
    var_fixed = variance / (1.0 - beta_two**STEP)
    updated = weight - step_rate * (
        mean_fixed / (jnp.sqrt(var_fixed) + adam_eps) + decay_rate * weight
    )
    return (moment, variance, updated)


def norm_parts(values):
    center = jnp.mean(values, -1, keepdims=True)
    spread = values - center
    inverse = lax.rsqrt(jnp.mean(spread * spread, -1, keepdims=True) + norm_eps)
    return spread * inverse, inverse


def norm_pull(unit, inverse, gain, grad):
    scaled = grad * gain
    first = jnp.mean(scaled, -1, keepdims=True)
    second = jnp.mean(scaled * unit, -1, keepdims=True)
    return inverse * (scaled - first - unit * second)


def swap(value, seq_bits, blk_bits):
    seq_count, blk_count = lax.axis_size("seq"), lax.axis_size("blk")
    pairs = [
        (i * blk_count + j, (i ^ seq_bits) * blk_count + (j ^ blk_bits))
        for i in range(seq_count)
        for j in range(blk_count)
    ]
    return lax.ppermute(value, PLANE, pairs)


def shift(value, step):
    count = lax.axis_size("dp")
    return lax.ppermute(value, "dp", [(i, (i + step) % count) for i in range(count)])


def gather_near(value):
    return jnp.stack([value, swap(value, 0, 1), swap(value, 2, 0), swap(value, 2, 1)])


def after(value, *others):
    return lax.optimization_barrier((value, *others))[0]


def together(*values):
    return lax.optimization_barrier(values)


def gather_steps(value):
    two = jnp.stack([value, swap(value, 0, 1)])
    return jnp.concatenate([two, swap(two, 2, 0)], 0)


def add_low(a, b):
    return (a.astype(F32) + b.astype(F32)).astype(BF16)


def spread_near(both):
    return both[0], swap(both[1], 0, 1), swap(both[2], 2, 0), swap(both[3], 2, 1)


def add_all(parts):
    total = parts[0].astype(F32)
    for part in parts[1:]:
        total = total + part.astype(F32)
    return total


def spread_dp(value):
    count = lax.axis_size("dp")
    if count != 4:
        return [lax.psum_scatter(value, "dp", scatter_dimension=0, tiled=False)]
    me = lax.axis_index("dp")
    parts = [lax.dynamic_index_in_dim(value, me, 0, keepdims=False)]
    for k in range(1, count):
        chunk = lax.dynamic_index_in_dim(value, (me + k) % count, 0, keepdims=False)
        parts.append(shift(chunk, k))
    return parts


def head_masks(first, group):
    lane = lax.broadcasted_iota(jnp.int32, (1, 256), 1) - first
    return [(lane >= h * HEAD) & (lane < (h + 1) * HEAD) for h in range(group // HEAD)]


def turned(block):
    return pltpu.roll(block.astype(F32), 64, 1).astype(BF16)


def spread_heads(block, masks):
    return jnp.concatenate([jnp.where(m, block, jnp.zeros_like(block)) for m in masks], 0)


def join_heads(stacked, masks):
    rows = stacked.shape[0] // len(masks)
    out = jnp.where(masks[0], stacked[:rows], 0.0)
    for h in range(1, len(masks)):
        out = out + jnp.where(masks[h], stacked[h * rows : (h + 1) * rows], 0.0)
    return out


def visible(heads, rows, keys, first_row):
    row = lax.broadcasted_iota(jnp.int32, (heads, rows, keys), 1).reshape(heads * rows, keys)
    key = lax.broadcasted_iota(jnp.int32, (heads * rows, keys), 1)
    return key <= row + first_row


def both_rows(tok_all, at, half):
    rows = [tok_all[2 * at + half], tok_all[2 * at + 1 - half]]
    return jnp.concatenate(rows, 0).astype(F32)


def forward_kernel(pieces, place, *refs):
    me, half, layer = place[0], place[1], place[2]
    w_parts, refs = refs[: max(1, 2 * pieces)], refs[max(1, 2 * pieces) :]
    tok_all, qkv_ref, n1_ref, att_ref, lse_ref, w_ref, small_ref, w32 = refs
    rows = tok_all.shape[1]
    group = att_ref.shape[0]
    wide = w32.shape[1]
    tail = wide - 128
    w32[:, tail:wide] = jnp.zeros((w32.shape[0], 128), F32)
    if pieces == 0:
        w32[:, : w_parts[0].shape[1]] = w_parts[0][...].astype(F32)
    for k in range(pieces):
        own_layer = lax.rem(layer + (pieces - k), pieces)
        for other in range(2):
            part = w_parts[2 * k + other]
            for j in range(4):
                owner = (own_layer * 4 + (me ^ j)) * 2 + (half ^ other)
                count = part.shape[1]
                where = pl.ds(pl.multiple_of(owner * count, 8), count)
                w32[where, : part.shape[2]] = part[j].astype(F32)
    w_low = w32[...].astype(BF16)
    w_ref[...] = w_low
    first = 3 * group - tail
    small = w32[:, tail:wide].T
    small_ref[...] = small[first : first + small_ref.shape[0]]
    width = small_ref.shape[1]
    turned_small = pltpu.roll(small[first : first + 8], width - me * group, 1)
    bias = jnp.concatenate(
        [
            turned_small[2:3, :group],
            jnp.zeros((1, group), F32),
            turned_small[3:4, :group],
            jnp.zeros((1, wide - 3 * group), F32),
        ],
        1,
    )
    gain, lift = small_ref[0:1, :], small_ref[1:2, :]
    for bit in range(2):
        for far in range(2):
            at = me ^ (2 * far + bit)
            unit, _ = norm_parts(both_rows(tok_all, at, half))
            n1 = (unit * gain + lift).astype(BF16)
            out = (dot(n1, w_low) + bias).astype(BF16)
            for other in range(2):
                where = pl.ds(pl.multiple_of((2 * at + (half ^ other)) * rows, rows), rows)
                n1_ref[where, :] = n1[other * rows : (other + 1) * rows]
                qkv_ref[where, :] = out[other * rows : (other + 1) * rows]
    shifted, plain = head_masks(64, group), head_masks(0, group)
    heads = len(plain)
    for i in range(4):
        keys = 2 * rows * (i + 1)
        where = pl.ds(pl.multiple_of((2 * i + half) * rows, rows), rows)
        queries = spread_heads(turned(qkv_ref[where, 0:256]), shifted)
        scores = dot(queries, qkv_ref[0:keys, 128:384], NT) * score_scale
        seen = visible(heads, rows, keys, (2 * i + half) * rows)
        scores = jnp.where(seen, scores, masked_score)
        top = jnp.max(scores, -1, keepdims=True)
        raised = jnp.exp(scores - top)
        total = jnp.sum(raised, -1, keepdims=True)
        probs = (raised / total).astype(BF16)
        result = join_heads(dot(probs, qkv_ref[0:keys, 384:640]), plain)
        att_ref[:, i * rows : (i + 1) * rows] = result.T[:group].astype(BF16)
        lse_ref[i] = top + jnp.log(total)


def hidden_kernel(
    pieces, place, tok_all, cot_a, cot_b, att_a, att_b, vec_ref, be_ref, *refs
):
    given, refs = refs[:3], refs[3:]
    out_a, out_b, dn_a, dn_b, mixed_ref, unit_ref, inverse_ref, sums_ref, gb_ref, own_ref = refs[:10]
    g_outs, refs = refs[10:-11], refs[-11:]
    att_all, gs_sum, ge_sum, p32, proj_ref, we_ref, ws_ref, act_all, pre_all, n2_all, cot_all = refs
    me, half, layer = place[0], place[1], place[2]
    if pieces == 0:
        p32[...] = given[0][...].astype(F32)
        we_ref[...] = given[1][...]
        ws_ref[...] = given[2][...]
    else:
        p_parts, ff_ref = given[:2], given[2]
        slots, part = ws_ref.shape[0], ws_ref.shape[0] // pieces
        for k in range(pieces):
            ws_ref[k * part : (k + 1) * part, :] = ff_ref[k, 0:part, :]
            for side in range(2):
                we_ref[(2 * k + side) * part : (2 * k + side + 1) * part, :] = ff_ref[
                    k, part:, side * slots : (side + 1) * slots
                ]
        for bit in range(2):
            for j in range(4):
                for k in range(pieces):
                    own_layer = lax.rem(layer + (pieces - k), pieces)
                    owner = (own_layer * 4 + (me ^ ((j & 2) + bit))) * 2 + (half ^ (j & 1))
                    count = p_parts[bit].shape[2]
                    where = pl.ds(pl.multiple_of(owner * count, 8), count)
                    p32[where, :] = p_parts[bit][j, k].astype(F32)
    proj_ref[...] = p32[...].astype(BF16)
    rows = tok_all.shape[1]
    span = 4 * rows
    group = att_a.shape[1]
    for bit in range(2):
        att = (att_a, att_b)[bit]
        for far in range(2):
            at = me ^ (2 * far + bit)
            where = pl.ds(pl.multiple_of(at * group, 64), group)
            if bit == 0 and far == 0:
                own_ref[0:group, :] = p32[where, :].astype(BF16)
                own_ref[group:, :] = jnp.zeros((own_ref.shape[0] - group, own_ref.shape[1]), BF16)
            for other in range(2):
                att_all[where, other * span : (other + 1) * span] = att[2 * far + other]
    bias_proj, gain, lift = vec_ref[4:5, :], vec_ref[5:6, :], vec_ref[6:7, :]
    sums = [jnp.zeros((1, gain.shape[1]), F32)] * 2
    gb = jnp.zeros((1, gb_ref.shape[1]), F32)
    sums_ref[2:3, :] = jnp.sum(cot_a[0].astype(F32), 0, keepdims=True)
    for bit in range(2):
        cot, out, dn = (cot_a, cot_b)[bit], (out_a, out_b)[bit], (dn_a, dn_b)[bit]
        for far in range(2):
            start = pl.multiple_of((me ^ (2 * far + bit)) * rows, rows)
            att = jnp.concatenate(
                [
                    att_all[:, pl.ds(start, rows)],
                    att_all[:, pl.ds(pl.multiple_of(span + start, rows), rows)],
                ],
                1,
            )
            two = both_rows(tok_all, me ^ (2 * far + bit), half)
            mixed = two + (dot(att, proj_ref[...], TN) + bias_proj)
            if bit == 0 and far == 0:
                mixed_ref[...] = mixed[:rows]
            unit, inverse = norm_parts(mixed)
            if bit == 0 and far == 0:
                unit_ref[...] = unit[:rows]
                inverse_ref[...] = inverse[:rows]
            n2 = (unit * gain + lift).astype(BF16)
            pre = dot(n2, we_ref[...]) + be_ref[...]
            cots = cot[2 * far : 2 * far + 2].reshape(2 * rows, -1)
            factor = math.sqrt(2.0 / math.pi)
            square = pre * pre
            bent = jnp.tanh(factor * pre * (1.0 + 0.044715 * square))
            act = (0.5 * pre * (1.0 + bent)).astype(BF16)
            slope = 0.5 * (1.0 + bent) + 0.5 * pre * (1.0 - bent * bent) * (
                factor * (1.0 + 3.0 * 0.044715 * square)
            )
            d_act = dot(cots, ws_ref[...], NT)
            d_pre32 = d_act * slope
            d_pre = d_pre32.astype(BF16)
            d_n2 = dot(d_pre, we_ref[...], NT)
            dn[2 * far : 2 * far + 2] = d_n2.astype(BF16).reshape(2, rows, -1)
            out[2 * far : 2 * far + 2] = dot(act, ws_ref[...]).astype(BF16).reshape(2, rows, -1)
            step = pl.ds((2 * bit + far) * 2 * rows, 2 * rows)
            act_all[step, :] = act
            pre_all[step, :] = d_pre
            n2_all[step, :] = n2
            cot_all[step, :] = cots
            sums[0] = sums[0] + jnp.sum(d_n2 * unit, 0, keepdims=True)
            sums[1] = sums[1] + jnp.sum(d_n2, 0, keepdims=True)
            gb = gb + jnp.sum(d_pre.astype(F32), 0, keepdims=True)
    gs_sum[...] = dot(act_all[...], cot_all[...], TN)
    ge_sum[...] = dot(n2_all[...], pre_all[...], TN)
    sums_ref[0:1, :] = sums[0]
    sums_ref[1:2, :] = sums[1]
    gb_ref[...] = gb
    if pieces == 0:
        g_outs[0][...] = ge_sum[...].astype(BF16)
        g_outs[1][...] = gs_sum[...].astype(BF16)
        return
    pack = g_outs[0]
    for k in range(pieces):
        pack[k, 0:part, :] = gs_sum[k * part : (k + 1) * part, :].astype(BF16)
        for side in range(2):
            pack[k, part:, side * slots : (side + 1) * slots] = ge_sum[
                (2 * k + side) * part : (2 * k + side + 1) * part, :
            ].astype(BF16)


def split_halves(table, keep, send, half, row_of, lanes, at=0):
    layers, four, count, _ = keep.shape
    for k in range(layers):
        for j in range(four):
            base = row_of(k, j) * 2
            for out, owner in ((keep, base + half), (send, base + 1 - half)):
                where = pl.ds(pl.multiple_of(owner * count, 8), count)
                out[k, j, :, at : at + lanes] = table(where, j).astype(BF16)


def attention_back_kernel(
    pieces, place, db_own, db_far, db_near, db_cross, qkv_ref, lse_ref, n1_ref, own_proj, *refs
):
    d_ref, db_all, outs, (d_all, g_all) = refs[0], refs[1], refs[2:-2], refs[-2:]
    me, half = place[0], place[1]
    rows = db_own.shape[0]
    group = 3 * HEAD
    shifted, plain = head_masks(64, group), head_masks(0, group)
    heads = len(plain)
    for bits, db in ((0, db_own), (2, db_far), (1, db_near), (3, db_cross)):
        db_all[pl.ds(pl.multiple_of((me ^ bits) * rows, rows), rows), :] = db[...]
    d_all[...] = jnp.zeros_like(d_all)
    for i in range(4):
        keys = 2 * rows * (i + 1)
        where = pl.ds(pl.multiple_of((2 * i + half) * rows, rows), rows)
        queries = spread_heads(turned(qkv_ref[where, 0:256]), shifted)
        d_att = dot(db_all[i * rows : (i + 1) * rows, :], own_proj[...], NT).astype(BF16)
        grads = spread_heads(d_att, plain)
        key_rows, values = qkv_ref[0:keys, 128:384], qkv_ref[0:keys, 384:640]
        scores = dot(queries, key_rows, NT) * score_scale
        seen = visible(heads, rows, keys, (2 * i + half) * rows)
        probs = jnp.where(seen, jnp.exp(scores - lse_ref[i]), 0.0)
        weighed = probs * dot(grads, values, NT)
        d_scores = (weighed - probs * jnp.sum(weighed, -1, keepdims=True)).astype(BF16)
        dq = join_heads(dot(d_scores, key_rows), shifted) * score_scale
        d_all[where, 0:256] += pltpu.roll(dq, 192, 1)
        d_all[0:keys, 128:384] += dot(d_scores, queries, TN) * score_scale
        d_all[0:keys, 384:640] += dot(probs.astype(BF16), grads, TN)
    d_ref[...] = d_all[...].astype(BF16)
    g_all[...] = dot(n1_ref[...], d_ref[:, 0 : 2 * group], TN)
    if pieces == 0:
        outs[0][...] = g_all[...].astype(BF16)
    else:
        split_halves(
            lambda where, j: g_all[where, :], outs[0], outs[1], half, lambda k, j: k * 4 + j, 2 * group
        )


def norm_back_kernel(
    pieces, place, d_ref, db_all, n1_ref, tok_all, att_a, att_b, w_ref, two_ref, gb_ref, spot_ref,
    dn_a, dn_b, *refs
):
    outs, (g_all, gp_all) = refs[:-2], refs[-2:]
    me, half = place[0], place[1]
    rows = tok_all.shape[1]
    group = att_a.shape[1]
    wide, width = d_ref.shape[1], n1_ref.shape[1]
    sums = [jnp.zeros((1, width), F32)] * 2
    for bit in range(2):
        dn = (dn_a, dn_b)[bit]
        for far in range(2):
            at = me ^ (2 * far + bit)
            gp_all[pl.ds(pl.multiple_of(at * group, 64), group), :] = dot(
                (att_a, att_b)[bit][2 * far], db_all[...]
            )
            for other in range(2):
                where = pl.ds(pl.multiple_of((2 * at + (half ^ other)) * rows, rows), rows)
                d_n1 = dot(d_ref[where, :], w_ref[...], NT)
                unit, _ = norm_parts(tok_all[2 * at + (half ^ other)].astype(F32))
                dn[2 * far + other] = d_n1.astype(BF16)
                sums[0] = sums[0] + jnp.sum(d_n1 * unit, 0, keepdims=True)
                sums[1] = sums[1] + jnp.sum(d_n1, 0, keepdims=True)
    heads_sum = jnp.sum(d_ref[...].astype(F32), 0, keepdims=True)

    def at_heads(row):
        row = jnp.concatenate([row, jnp.zeros((1, width - group), F32)], 1)
        return pltpu.roll(jnp.broadcast_to(row, (8, width)), me * group, 1)[0:1]

    head_q, head_v = at_heads(heads_sum[:, :group]), at_heads(heads_sum[:, 2 * group : 3 * group])
    index = lax.broadcasted_iota(jnp.int32, (16, width), 0)
    small = jnp.where(index == 0, sums[0], 0.0)
    small = jnp.where(index == 1, sums[1], small)
    own = db_all[pl.ds(pl.multiple_of(me * rows, rows), rows), :].astype(F32)
    small = jnp.where(index == 4, jnp.sum(own, 0, keepdims=True), small)
    slots = gb_ref.shape[1]
    block = lax.broadcasted_iota(jnp.int32, (16, slots), 1) - 96 * (
        lax.broadcasted_iota(jnp.int32, (16, slots), 0) - 7
    )
    hidden_rows = jnp.where((block >= 0) & (block < 96), gb_ref[...], 0.0).astype(BF16)
    small = small + dot(hidden_rows, spot_ref[...])
    small = jnp.where(index == 5, two_ref[0:1, :], small)
    small = jnp.where(index == 6, two_ref[1:2, :], small)
    small = jnp.where(index == 7 + slots // 96, two_ref[2:3, :], small)
    small = jnp.where(index == 2, head_q, small)
    small = jnp.where(index == 3, head_v, small).astype(BF16)
    row = lax.broadcasted_iota(jnp.int32, (16, 256), 0)
    lane = lax.broadcasted_iota(jnp.int32, (16, 256), 1)
    spread = (lane == row + group).astype(F32).astype(BF16)
    g_all[...] = dot(n1_ref[...], d_ref[:, 2 * group :], TN) + dot(small, spread, TN)
    if pieces == 0:
        outs[0][...] = g_all[...].astype(BF16)
        outs[1][...] = gp_all[...].astype(BF16)
        return
    split_halves(
        lambda where, j: g_all[where, :], outs[0], outs[1], half, lambda k, j: k * 4 + j, 256
    )

    def chunk(where, j):
        start = j * group
        block = gp_all[where, start // 128 * 128 : start // 128 * 128 + 256]
        if start % 128:
            block = pltpu.roll(block, 256 - start % 128, 1)
        return block[:, :group]

    split_halves(chunk, outs[0], outs[1], half, lambda k, j: k * 4 + me, group, 256)


def call(kernel, outs, scratch, flops, *args):
    whole = pl.BlockSpec(memory_space=pltpu.VMEM)
    specs = [pl.BlockSpec(memory_space=pltpu.SMEM)] + [whole] * (len(args) - 1)
    moved = sum(math.prod(a.shape) * a.dtype.itemsize for a in args)
    return pl.pallas_call(
        kernel,
        out_shape=[jax.ShapeDtypeStruct(shape, kind) for shape, kind in outs],
        in_specs=specs,
        out_specs=[whole] * len(outs),
        scratch_shapes=[pltpu.VMEM(shape, kind) for shape, kind in scratch],
        compiler_params=pltpu.CompilerParams(vmem_limit_bytes=VMEM_LIMIT),
        cost_estimate=pl.CostEstimate(flops=flops, bytes_accessed=moved, transcendentals=10**6),
    )(*args)


def shards(
    tokens,
    cotangent,
    qkv_weight,
    proj_weight,
    expand_weight,
    shrink_weight,
    small_params,
    qkv_first,
    proj_first,
    expand_first,
    shrink_first,
    small_first,
    qkv_second,
    proj_second,
    expand_second,
    shrink_second,
    small_second,
):
    rows, width = tokens.shape
    hidden = expand_weight.shape[1]
    own_rows = qkv_weight.shape[0]
    own_hidden = shrink_weight.shape[0]
    dp_count, seq_count, blk_count = (lax.axis_size(a) for a in ALL)
    plane = seq_count * blk_count
    assert (seq_count, blk_count) == (4, 2)
    dp, seq, blk = (lax.axis_index(a) for a in ALL)
    spot = seq * blk_count + blk
    group = width // seq_count
    slots = hidden // plane
    length = plane * rows
    half_length = length // blk_count
    small_rows = small_params.shape[0]
    place = jnp.stack([seq, blk, dp]).astype(jnp.int32)

    w_lanes = 3 * group + small_rows
    parts = qkv_weight.astype(BF16).reshape(own_rows, 3, seq_count, group)
    parts = jnp.transpose(parts, (2, 0, 1, 3)).reshape(seq_count, own_rows, 3 * group)
    small_part = jnp.broadcast_to(
        small_params.T.astype(BF16), (seq_count, own_rows, small_rows)
    )
    parts = jnp.concatenate([parts, small_part], 2)
    pieces = 4 if dp_count == 4 and own_rows % 8 == 0 else 0
    if pieces:
        picked = [lax.dynamic_index_in_dim(parts, seq ^ k, 0, keepdims=False) for k in range(4)]
        near = jnp.stack([picked[0]] + [swap(picked[k], k, 0) for k in range(1, 4)])
        layers = [near] + [shift(near, k) for k in range(1, 4)]
        w_parts = []
        for part in layers:
            w_parts += [part, swap(part, 0, 1)]
    else:
        parts = lax.all_to_all(parts, "seq", split_axis=0, concat_axis=0, tiled=True)
        both = lax.all_gather(parts, ("dp", "blk"), axis=0, tiled=False)
        both = both.reshape(dp_count, blk_count, seq_count, own_rows, w_lanes)
        layers = [parts]
        w_parts = [jnp.transpose(both, (0, 2, 1, 3, 4)).reshape(width, w_lanes)]

    tok_all = lax.all_gather(tokens, PLANE, axis=0, tiled=False)

    expand_parts = after(expand_weight, layers[0]).astype(BF16)
    expand_parts = expand_parts.reshape(own_rows, dp_count, plane, own_hidden)
    expand_parts = jnp.transpose(expand_parts, (2, 0, 1, 3)).reshape(plane, own_rows, slots)
    expand_parts = lax.all_to_all(expand_parts, PLANE, split_axis=0, concat_axis=0, tiled=True)
    proj_low = after(proj_weight, expand_parts).astype(BF16)
    if pieces:
        proj_moved = [proj_low] + [shift(proj_low, k) for k in range(1, 4)]
    else:
        proj_moved = [proj_low]
    expand_parts = after(expand_parts, *layers, *proj_moved, w_parts[min(1, pieces)], tok_all)
    expand_parts = expand_parts.reshape(2, own_hidden, slots)
    ff_own = jnp.concatenate(
        [
            shrink_weight.astype(BF16),
            jnp.concatenate([expand_parts[0], expand_parts[1]], 1),
        ],
        0,
    )
    ff_all = lax.all_gather(ff_own, "dp", axis=0, tiled=False)

    gate = w_parts[3 * (pieces > 0)]
    cot_low = after(cotangent, layers[-1])
    cot_two = after(jnp.stack([cot_low, swap(cot_low, 0, 1)]), gate)
    cot_far = swap(cot_two, 2, 0)

    if pieces:
        p_near = gather_steps(after(jnp.stack(proj_moved), gate))
        hidden_weights = (p_near, swap(p_near, 1, 0), ff_all)
    else:
        w_shrink = ff_all[:, :own_hidden].reshape(slots, width)
        w_expand = jnp.stack([ff_all[:, own_hidden:, :slots], ff_all[:, own_hidden:, slots:]], 1)
        proj_whole = lax.all_gather(proj_low, ALL, axis=0, tiled=True)
        hidden_weights = (proj_whole, w_expand.reshape(width, slots), w_shrink)

    w_parts[0] = after(w_parts[0], ff_own)

    unit_at = jnp.arange(slots) % (width // plane)
    unit_at = unit_at // own_hidden * (plane * own_hidden) + spot * own_hidden + unit_at % own_hidden
    spot_table = (unit_at[:, None] == jnp.arange(width)[None]).astype(BF16)

    wide = 640
    qkv, n1, att, lse, w_qkv, small_full = call(
        partial(forward_kernel, pieces),
        [
            ((length, wide), BF16),
            ((length, width), BF16),
            ((group, half_length), BF16),
            ((4, 3 * rows, 1), F32),
            ((width, wide), BF16),
            ((small_rows, width), F32),
        ],
        [((width, wide), F32)],
        2 * 10**9,
        place, *w_parts, tok_all,
    )
    extra = hidden // width
    zero = jnp.zeros((width,), F32)
    bias_expand = small_full[7 : 7 + extra].reshape(dp_count, plane, own_hidden)
    bias_expand = lax.dynamic_index_in_dim(bias_expand, spot, 1, keepdims=False).reshape(1, slots)
    bias_shrink = small_full[7 + extra]
    att, cot_two, cot_far = together(att, cot_two, cot_far)
    cot_a = jnp.concatenate([cot_two, cot_far], 0)
    cot_b = swap(cot_a, 1, 0)
    gain_one, gain_two = small_full[0], small_full[5]
    att_a, bias_expand, bias_shrink, gain_one, gain_two, spot_table = together(
        gather_near(att), bias_expand, bias_shrink, gain_one, gain_two, spot_table
    )
    att_b = swap(att_a, 1, 0)

    big = ((4, rows, width), BF16)
    if pieces:
        hidden_grads = [((dp_count, 2 * own_hidden, width), BF16)]
    else:
        hidden_grads = [((width, slots), BF16), ((slots, width), BF16)]
    out_a, out_b, dn_a, dn_b, mixed, unit, inverse, sums_two, gb_expand, own_proj, *ff_grad = call(
        partial(hidden_kernel, pieces),
        [
            big, big, big, big,
            ((rows, width), F32),
            ((rows, width), F32),
            ((rows, 1), F32),
            ((3, width), F32),
            ((1, slots), F32),
            ((256, width), BF16),
            *hidden_grads,
        ],
        [
            ((width, length), BF16),
            ((slots, width), F32),
            ((width, slots), F32),
            ((width, width), F32),
            ((width, width), BF16),
            ((width, slots), BF16),
            ((slots, width), BF16),
            ((length, slots), BF16),
            ((length, slots), BF16),
            ((length, width), BF16),
            ((length, width), BF16),
        ],
        6 * 10**9,
        place, tok_all, cot_a, cot_b, att_a, att_b, small_full, bias_expand, *hidden_weights,
    )

    dn_both = add_low(dn_a, swap(dn_b, 1, 0))

    cot_wide = cotangent.astype(F32)
    if pieces:
        ff_grad = ff_grad[0]
    else:
        ge = ff_grad[0].reshape(dp_count, 2, own_hidden, slots)
        ff_grad = jnp.concatenate(
            [
                ff_grad[1].reshape(dp_count, own_hidden, width),
                jnp.concatenate([ge[:, 0], ge[:, 1]], 2),
            ],
            1,
        )
    ff_sum = lax.psum_scatter(
        ff_grad.reshape(-1, width), "dp", scatter_dimension=0, tiled=True
    )
    out_both = add_low(out_a, swap(after(out_b, dn_both), 1, 0))

    dn_parts = lax.optimization_barrier((*spread_near(dn_both), out_both))
    d_normed_two = add_all(dn_parts[:4])
    out_both = dn_parts[4]
    d_mixed = cot_wide + norm_pull(unit, inverse, gain_two, d_normed_two)
    d_branch = d_mixed.astype(BF16)
    db_near = swap(d_branch, 1, 0)
    db_far = swap(d_branch, 2, 0)
    db_cross = swap(db_far, 1, 0)
    out_half = swap(after(out_both[1::2], d_branch), 0, 1)

    if pieces:
        first = ((4, 4, own_rows, 2 * group), BF16)
        second = ((4, 4, own_rows, 256 + group), BF16)
        first, second = [first] * 2, [second] * 2
    else:
        first = [((width, 2 * group), BF16)]
        second = [((width, 256), BF16), ((width, width), BF16)]
    d_low, db_all, *grads = call(
        partial(attention_back_kernel, pieces),
        [((length, wide), BF16), ((half_length, width), BF16), *first],
        [((length, wide), F32), ((width, 2 * group), F32)],
        10 * 10**9,
        place, d_branch, db_far, db_near, db_cross, qkv, lse, n1, own_proj,
    )
    grads = list(lax.optimization_barrier((*grads, out_half)))[:-1]

    def halves(table, lanes):
        table = table.reshape(dp_count, -1, blk_count, own_rows, lanes)
        keep = lax.dynamic_index_in_dim(table, blk, 2, keepdims=False)
        return keep, lax.dynamic_index_in_dim(table, 1 - blk, 2, keepdims=False)

    keep, send = grads if pieces else halves(grads[0], 2 * group)
    g_first = add_low(keep, swap(send, 0, 1))
    out_two = add_low(after(out_both, d_low)[0::2], out_half)
    out_last = swap(out_two[1], 2, 0)

    dn_a, dn_b, *grads = call(
        partial(norm_back_kernel, pieces),
        [big, big, *second],
        [((width, 256), F32), ((width, width), F32)],
        6 * 10**9,
        place, after(d_low, out_two), db_all, n1, tok_all, att_a, att_b, w_qkv,
        sums_two, gb_expand, spot_table,
    )
    if pieces:
        keep, send = grads
    else:
        v_keep, v_send = halves(grads[0], 256)
        gp = grads[1].reshape(dp_count, seq_count, blk_count, own_rows, seq_count, group)
        gp = lax.dynamic_index_in_dim(gp, seq, 1, keepdims=False)
        gp = jnp.transpose(gp, (0, 3, 1, 2, 4))
        p_keep, p_send = halves(gp, group)
        keep = jnp.concatenate([v_keep, p_keep], -1)
        send = jnp.concatenate([v_send, p_send], -1)
    g_first, keep, send, dn_a, dn_b, out_last = together(g_first, keep, send, dn_a, dn_b, out_last)
    first_parts = spread_dp(g_first)
    g_got = swap(send, 0, 1)
    dn_got = swap(dn_b, 1, 0)
    *first_parts, keep, g_got, dn_a, dn_got = together(*first_parts, keep, g_got, dn_a, dn_got)

    rest_parts = spread_dp(add_low(keep, g_got))
    dn_parts = spread_near(add_low(dn_a, dn_got))
    g_first = add_all(first_parts)
    *rest_parts, dn_0, dn_1, dn_2, dn_3 = together(*rest_parts, *dn_parts)
    g_rest = add_all(rest_parts)

    ff_sum = after(ff_sum, dn_0)
    sum_shrink = ff_sum[:own_hidden].astype(F32)
    sum_expand = ff_sum[own_hidden:]
    sum_expand = jnp.stack([sum_expand[:, :slots], sum_expand[:, slots:]])
    sum_expand = sum_expand.reshape(plane, own_rows, slots)
    sum_expand = lax.all_to_all(sum_expand, PLANE, split_axis=0, concat_axis=0, tiled=True)
    block_out = mixed + (out_two[0].astype(F32) + out_last.astype(F32)) + bias_shrink

    g_all = jnp.concatenate([g_first, g_rest[:, :, : group + small_rows]], -1).astype(BF16)
    picked = [lax.dynamic_index_in_dim(g_all, seq ^ k, 0, keepdims=False) for k in range(4)]
    picked = jnp.stack([picked[0]] + [swap(picked[k], k, 0) for k in range(1, 4)]).astype(F32)
    g_all = [lax.dynamic_index_in_dim(picked, seq ^ k, 0, keepdims=False) for k in range(4)]
    g_all = jnp.stack(g_all)
    sum_proj = jnp.transpose(g_rest[:, :, 256:], (1, 0, 2)).reshape(own_rows, width)
    sum_small = jnp.sum(picked[:, :, 3 * group :], 0).T
    sum_qkv = jnp.transpose(
        g_all[:, :, : 3 * group].reshape(seq_count, own_rows, 3, group), (1, 2, 0, 3)
    ).reshape(own_rows, 3 * width)
    sum_expand = jnp.transpose(
        sum_expand.reshape(plane, own_rows, dp_count, own_hidden), (1, 2, 0, 3)
    ).reshape(own_rows, hidden).astype(F32)

    d_normed_one = add_all((dn_0, dn_1, dn_2, dn_3))
    unit, inverse = norm_parts(tokens.astype(F32))
    token_grad = d_mixed + norm_pull(unit, inverse, gain_one, d_normed_one)

    qkv_out = adam_update(
        qkv_weight, qkv_first, qkv_second, sum_qkv, matrix_rate, matrix_decay
    )
    proj_out = adam_update(
        proj_weight, proj_first, proj_second, sum_proj, matrix_rate, matrix_decay
    )
    expand_out = adam_update(
        expand_weight, expand_first, expand_second, sum_expand, matrix_rate, matrix_decay
    )
    shrink_out = adam_update(
        shrink_weight, shrink_first, shrink_second, sum_shrink, matrix_rate, matrix_decay
    )
    small_out = adam_update(
        small_params, small_first, small_second, sum_small, small_rate, 0.0
    )
    return (block_out, token_grad, *qkv_out, *proj_out, *expand_out, *shrink_out, *small_out)


def solution(mesh):
    by_rows = P(ALL, None)
    by_columns = P(None, ALL)
    state = (by_rows,) * 4 + (by_columns,)
    return jax.shard_map(
        shards,
        mesh=mesh,
        in_specs=(by_rows, by_rows) + state * 3,
        out_specs=(by_rows,) * 14 + (by_columns,) * 3,
        check_vma=False,
    )
```

```python
from functools import partial
import math

import jax
import jax.numpy as jnp
from jax import lax
from jax.experimental import pallas as pl
from jax.experimental.pallas import tpu as pltpu
from jax.sharding import PartitionSpec as P

HEAD = 64
STEP = 10

norm_eps = 1e-05
beta_one = 0.9
beta_two = 0.95
adam_eps = 1e-08
matrix_rate = 0.05
matrix_decay = 0.1
small_rate = 0.5
masked_score = -1e30
score_scale = 1.0 / math.sqrt(HEAD)

F32 = jnp.float32
BF16 = jnp.bfloat16
ALL = ("dp", "seq", "blk")
PLANE = ("seq", "blk")
VMEM_LIMIT = 56 * 1024 * 1024
NT = (((1,), (1,)), ((), ()))
TN = (((0,), (0,)), ((), ()))


def dot(a, b, dims=None):
    if dims is None:
        return jnp.dot(a, b, preferred_element_type=F32)
    return lax.dot_general(a, b, dims, preferred_element_type=F32)


def adam_update(weight, first_state, second, gradient, step_rate, decay_rate):
    moment = beta_one * first_state + (1.0 - beta_one) * gradient
    variance = beta_two * second + (1.0 - beta_two) * gradient * gradient
    mean_fixed = moment / (1.0 - beta_one**STEP)
    var_fixed = variance / (1.0 - beta_two**STEP)
    updated = weight - step_rate * (
        mean_fixed / (jnp.sqrt(var_fixed) + adam_eps) + decay_rate * weight
    )
    return (moment, variance, updated)


def norm_parts(values):
    center = jnp.mean(values, -1, keepdims=True)
    spread = values - center
    inverse = lax.rsqrt(jnp.mean(spread * spread, -1, keepdims=True) + norm_eps)
    return spread * inverse, inverse


def norm_pull(unit, inverse, gain, grad):
    scaled = grad * gain
    first = jnp.mean(scaled, -1, keepdims=True)
    second = jnp.mean(scaled * unit, -1, keepdims=True)
    return inverse * (scaled - first - unit * second)


def swap(value, seq_bits, blk_bits):
    seq_count, blk_count = lax.axis_size("seq"), lax.axis_size("blk")
    pairs = [
        (i * blk_count + j, (i ^ seq_bits) * blk_count + (j ^ blk_bits))
        for i in range(seq_count)
        for j in range(blk_count)
    ]
    return lax.ppermute(value, PLANE, pairs)


def shift(value, step):
    count = lax.axis_size("dp")
    return lax.ppermute(value, "dp", [(i, (i + step) % count) for i in range(count)])


def gather_near(value):
    return jnp.stack([value, swap(value, 0, 1), swap(value, 2, 0), swap(value, 2, 1)])


def after(value, *others):
    return lax.optimization_barrier((value, *others))[0]


def together(*values):
    return lax.optimization_barrier(values)


def gather_steps(value):
    two = jnp.stack([value, swap(value, 0, 1)])
    return jnp.concatenate([two, swap(two, 2, 0)], 0)


def add_low(a, b):
    return (a.astype(F32) + b.astype(F32)).astype(BF16)


def spread_near(both):
    return both[0], swap(both[1], 0, 1), swap(both[2], 2, 0), swap(both[3], 2, 1)


def add_all(parts):
    total = parts[0].astype(F32)
    for part in parts[1:]:
        total = total + part.astype(F32)
    return total


def spread_dp(value):
    count = lax.axis_size("dp")
    if count != 4:
        return [lax.psum_scatter(value, "dp", scatter_dimension=0, tiled=False)]
    me = lax.axis_index("dp")
    parts = [lax.dynamic_index_in_dim(value, me, 0, keepdims=False)]
    for k in range(1, count):
        chunk = lax.dynamic_index_in_dim(value, (me + k) % count, 0, keepdims=False)
        parts.append(shift(chunk, k))
    return parts


def head_masks(first, group):
    lane = lax.broadcasted_iota(jnp.int32, (1, 256), 1) - first
    return [(lane >= h * HEAD) & (lane < (h + 1) * HEAD) for h in range(group // HEAD)]


def turned(block):
    return pltpu.roll(block.astype(F32), 64, 1).astype(BF16)


def spread_heads(block, masks):
    return jnp.concatenate([jnp.where(m, block, jnp.zeros_like(block)) for m in masks], 0)


def join_heads(stacked, masks):
    rows = stacked.shape[0] // len(masks)
    out = jnp.where(masks[0], stacked[:rows], 0.0)
    for h in range(1, len(masks)):
        out = out + jnp.where(masks[h], stacked[h * rows : (h + 1) * rows], 0.0)
    return out


def visible(heads, rows, keys, first_row):
    row = lax.broadcasted_iota(jnp.int32, (heads, rows, keys), 1).reshape(heads * rows, keys)
    key = lax.broadcasted_iota(jnp.int32, (heads * rows, keys), 1)
    return key <= row + first_row


def both_rows(tok_all, at, half):
    rows = [tok_all[2 * at + half], tok_all[2 * at + 1 - half]]
    return jnp.concatenate(rows, 0).astype(F32)


def forward_kernel(pieces, place, *refs):
    me, half, layer = place[0], place[1], place[2]
    w_parts, refs = refs[: max(1, 2 * pieces)], refs[max(1, 2 * pieces) :]
    tok_all, qkv_ref, n1_ref, att_ref, lse_ref, w_ref, small_ref, w32 = refs
    rows = tok_all.shape[1]
    group = att_ref.shape[0]
    wide = w32.shape[1]
    tail = wide - 128
    w32[:, tail:wide] = jnp.zeros((w32.shape[0], 128), F32)
    if pieces == 0:
        w32[:, : w_parts[0].shape[1]] = w_parts[0][...].astype(F32)
    for k in range(pieces):
        own_layer = lax.rem(layer + (pieces - k), pieces)
        for other in range(2):
            part = w_parts[2 * k + other]
            for j in range(4):
                owner = (own_layer * 4 + (me ^ j)) * 2 + (half ^ other)
                count = part.shape[1]
                where = pl.ds(pl.multiple_of(owner * count, 8), count)
                w32[where, : part.shape[2]] = part[j].astype(F32)
    w_low = w32[...].astype(BF16)
    w_ref[...] = w_low
    first = 3 * group - tail
    small = w32[:, tail:wide].T
    small_ref[...] = small[first : first + small_ref.shape[0]]
    width = small_ref.shape[1]
    turned_small = pltpu.roll(small[first : first + 8], width - me * group, 1)
    bias = jnp.concatenate(
        [
            turned_small[2:3, :group],
            jnp.zeros((1, group), F32),
            turned_small[3:4, :group],
            jnp.zeros((1, wide - 3 * group), F32),
        ],
        1,
    )
    gain, lift = small_ref[0:1, :], small_ref[1:2, :]
    for bit in range(2):
        for far in range(2):
            at = me ^ (2 * far + bit)
            unit, _ = norm_parts(both_rows(tok_all, at, half))
            n1 = (unit * gain + lift).astype(BF16)
            out = (dot(n1, w_low) + bias).astype(BF16)
            for other in range(2):
                where = pl.ds(pl.multiple_of((2 * at + (half ^ other)) * rows, rows), rows)
                n1_ref[where, :] = n1[other * rows : (other + 1) * rows]
                qkv_ref[where, :] = out[other * rows : (other + 1) * rows]
    shifted, plain = head_masks(64, group), head_masks(0, group)
    heads = len(plain)
    for i in range(4):
        keys = 2 * rows * (i + 1)
        where = pl.ds(pl.multiple_of((2 * i + half) * rows, rows), rows)
        queries = spread_heads(turned(qkv_ref[where, 0:256]), shifted)
        scores = dot(queries, qkv_ref[0:keys, 128:384], NT) * score_scale
        seen = visible(heads, rows, keys, (2 * i + half) * rows)
        scores = jnp.where(seen, scores, masked_score)
        top = jnp.max(scores, -1, keepdims=True)
        raised = jnp.exp(scores - top)
        total = jnp.sum(raised, -1, keepdims=True)
        probs = (raised / total).astype(BF16)
        result = join_heads(dot(probs, qkv_ref[0:keys, 384:640]), plain)
        att_ref[:, i * rows : (i + 1) * rows] = result.T[:group].astype(BF16)
        lse_ref[i] = top + jnp.log(total)


def hidden_kernel(
    pieces, place, tok_all, cot_a, cot_b, att_a, att_b, vec_ref, be_ref, *refs
):
    given, refs = refs[:3], refs[3:]
    out_a, out_b, dn_a, dn_b, mixed_ref, unit_ref, inverse_ref, sums_ref, gb_ref, own_ref = refs[:10]
    g_outs, refs = refs[10:-11], refs[-11:]
    att_all, gs_sum, ge_sum, p32, proj_ref, we_ref, ws_ref, act_all, pre_all, n2_all, cot_all = refs
    me, half, layer = place[0], place[1], place[2]
    if pieces == 0:
        p32[...] = given[0][...].astype(F32)
        we_ref[...] = given[1][...]
        ws_ref[...] = given[2][...]
    else:
        p_parts, ff_ref = given[:2], given[2]
        slots, part = ws_ref.shape[0], ws_ref.shape[0] // pieces
        for k in range(pieces):
            ws_ref[k * part : (k + 1) * part, :] = ff_ref[k, 0:part, :]
            for side in range(2):
                we_ref[(2 * k + side) * part : (2 * k + side + 1) * part, :] = ff_ref[
                    k, part:, side * slots : (side + 1) * slots
                ]
        for bit in range(2):
            for j in range(4):
                for k in range(pieces):
                    own_layer = lax.rem(layer + (pieces - k), pieces)
                    owner = (own_layer * 4 + (me ^ ((j & 2) + bit))) * 2 + (half ^ (j & 1))
                    count = p_parts[bit].shape[2]
                    where = pl.ds(pl.multiple_of(owner * count, 8), count)
                    p32[where, :] = p_parts[bit][j, k].astype(F32)
    proj_ref[...] = p32[...].astype(BF16)
    rows = tok_all.shape[1]
    span = 4 * rows
    group = att_a.shape[1]
    for bit in range(2):
        att = (att_a, att_b)[bit]
        for far in range(2):
            at = me ^ (2 * far + bit)
            where = pl.ds(pl.multiple_of(at * group, 64), group)
            if bit == 0 and far == 0:
                own_ref[0:group, :] = p32[where, :].astype(BF16)
                own_ref[group:, :] = jnp.zeros((own_ref.shape[0] - group, own_ref.shape[1]), BF16)
            for other in range(2):
                att_all[where, other * span : (other + 1) * span] = att[2 * far + other]
    bias_proj, gain, lift = vec_ref[4:5, :], vec_ref[5:6, :], vec_ref[6:7, :]
    sums = [jnp.zeros((1, gain.shape[1]), F32)] * 2
    gb = jnp.zeros((1, gb_ref.shape[1]), F32)
    sums_ref[2:3, :] = jnp.sum(cot_a[0].astype(F32), 0, keepdims=True)
    for bit in range(2):
        cot, out, dn = (cot_a, cot_b)[bit], (out_a, out_b)[bit], (dn_a, dn_b)[bit]
        for far in range(2):
            start = pl.multiple_of((me ^ (2 * far + bit)) * rows, rows)
            att = jnp.concatenate(
                [
                    att_all[:, pl.ds(start, rows)],
                    att_all[:, pl.ds(pl.multiple_of(span + start, rows), rows)],
                ],
                1,
            )
            two = both_rows(tok_all, me ^ (2 * far + bit), half)
            mixed = two + (dot(att, proj_ref[...], TN) + bias_proj)
            if bit == 0 and far == 0:
                mixed_ref[...] = mixed[:rows]
            unit, inverse = norm_parts(mixed)
            if bit == 0 and far == 0:
                unit_ref[...] = unit[:rows]
                inverse_ref[...] = inverse[:rows]
            n2 = (unit * gain + lift).astype(BF16)
            pre = dot(n2, we_ref[...]) + be_ref[...]
            cots = cot[2 * far : 2 * far + 2].reshape(2 * rows, -1)
            factor = math.sqrt(2.0 / math.pi)
            square = pre * pre
            bent = jnp.tanh(factor * pre * (1.0 + 0.044715 * square))
            act = (0.5 * pre * (1.0 + bent)).astype(BF16)
            slope = 0.5 * (1.0 + bent) + 0.5 * pre * (1.0 - bent * bent) * (
                factor * (1.0 + 3.0 * 0.044715 * square)
            )
            d_act = dot(cots, ws_ref[...], NT)
            d_pre32 = d_act * slope
            d_pre = d_pre32.astype(BF16)
            d_n2 = dot(d_pre, we_ref[...], NT)
            dn[2 * far : 2 * far + 2] = d_n2.astype(BF16).reshape(2, rows, -1)
            out[2 * far : 2 * far + 2] = dot(act, ws_ref[...]).astype(BF16).reshape(2, rows, -1)
            step = pl.ds((2 * bit + far) * 2 * rows, 2 * rows)
            act_all[step, :] = act
            pre_all[step, :] = d_pre
            n2_all[step, :] = n2
            cot_all[step, :] = cots
            sums[0] = sums[0] + jnp.sum(d_n2 * unit, 0, keepdims=True)
            sums[1] = sums[1] + jnp.sum(d_n2, 0, keepdims=True)
            gb = gb + jnp.sum(d_pre.astype(F32), 0, keepdims=True)
    gs_sum[...] = dot(act_all[...], cot_all[...], TN)
    ge_sum[...] = dot(n2_all[...], pre_all[...], TN)
    sums_ref[0:1, :] = sums[0]
    sums_ref[1:2, :] = sums[1]
    gb_ref[...] = gb
    if pieces == 0:
        g_outs[0][...] = ge_sum[...].astype(BF16)
        g_outs[1][...] = gs_sum[...].astype(BF16)
        return
    pack = g_outs[0]
    for k in range(pieces):
        pack[k, 0:part, :] = gs_sum[k * part : (k + 1) * part, :].astype(BF16)
        for side in range(2):
            pack[k, part:, side * slots : (side + 1) * slots] = ge_sum[
                (2 * k + side) * part : (2 * k + side + 1) * part, :
            ].astype(BF16)


def split_halves(table, keep, send, half, row_of, lanes, at=0):
    layers, four, count, _ = keep.shape
    for k in range(layers):
        for j in range(four):
            base = row_of(k, j) * 2
            for out, owner in ((keep, base + half), (send, base + 1 - half)):
                where = pl.ds(pl.multiple_of(owner * count, 8), count)
                out[k, j, :, at : at + lanes] = table(where, j).astype(BF16)


def attention_back_kernel(
    pieces, place, db_own, db_far, db_near, db_cross, qkv_ref, lse_ref, n1_ref, own_proj, *refs
):
    d_ref, db_all, outs, (d_all, g_all) = refs[0], refs[1], refs[2:-2], refs[-2:]
    me, half = place[0], place[1]
    rows = db_own.shape[0]
    group = 3 * HEAD
    shifted, plain = head_masks(64, group), head_masks(0, group)
    heads = len(plain)
    for bits, db in ((0, db_own), (2, db_far), (1, db_near), (3, db_cross)):
        db_all[pl.ds(pl.multiple_of((me ^ bits) * rows, rows), rows), :] = db[...]
    d_all[...] = jnp.zeros_like(d_all)
    for i in range(4):
        keys = 2 * rows * (i + 1)
        where = pl.ds(pl.multiple_of((2 * i + half) * rows, rows), rows)
        queries = spread_heads(turned(qkv_ref[where, 0:256]), shifted)
        d_att = dot(db_all[i * rows : (i + 1) * rows, :], own_proj[...], NT).astype(BF16)
        grads = spread_heads(d_att, plain)
        key_rows, values = qkv_ref[0:keys, 128:384], qkv_ref[0:keys, 384:640]
        scores = dot(queries, key_rows, NT) * score_scale
        seen = visible(heads, rows, keys, (2 * i + half) * rows)
        probs = jnp.where(seen, jnp.exp(scores - lse_ref[i]), 0.0)
        weighed = probs * dot(grads, values, NT)
        d_scores = (weighed - probs * jnp.sum(weighed, -1, keepdims=True)).astype(BF16)
        dq = join_heads(dot(d_scores, key_rows), shifted) * score_scale
        d_all[where, 0:256] += pltpu.roll(dq, 192, 1)
        d_all[0:keys, 128:384] += dot(d_scores, queries, TN) * score_scale
        d_all[0:keys, 384:640] += dot(probs.astype(BF16), grads, TN)
    d_ref[...] = d_all[...].astype(BF16)
    g_all[...] = dot(n1_ref[...], d_ref[:, 0 : 2 * group], TN)
    if pieces == 0:
        outs[0][...] = g_all[...].astype(BF16)
    else:
        split_halves(
            lambda where, j: g_all[where, :], outs[0], outs[1], half, lambda k, j: k * 4 + j, 2 * group
        )


def norm_back_kernel(
    pieces, place, d_ref, db_all, n1_ref, tok_all, att_a, att_b, w_ref, two_ref, gb_ref, spot_ref,
    dn_a, dn_b, *refs
):
    outs, (g_all, gp_all) = refs[:-2], refs[-2:]
    me, half = place[0], place[1]
    rows = tok_all.shape[1]
    group = att_a.shape[1]
    wide, width = d_ref.shape[1], n1_ref.shape[1]
    sums = [jnp.zeros((1, width), F32)] * 2
    for bit in range(2):
        dn = (dn_a, dn_b)[bit]
        for far in range(2):
            at = me ^ (2 * far + bit)
            gp_all[pl.ds(pl.multiple_of(at * group, 64), group), :] = dot(
                (att_a, att_b)[bit][2 * far], db_all[...]
            )
            for other in range(2):
                where = pl.ds(pl.multiple_of((2 * at + (half ^ other)) * rows, rows), rows)
                d_n1 = dot(d_ref[where, :], w_ref[...], NT)
                unit, _ = norm_parts(tok_all[2 * at + (half ^ other)].astype(F32))
                dn[2 * far + other] = d_n1.astype(BF16)
                sums[0] = sums[0] + jnp.sum(d_n1 * unit, 0, keepdims=True)
                sums[1] = sums[1] + jnp.sum(d_n1, 0, keepdims=True)
    heads_sum = jnp.sum(d_ref[...].astype(F32), 0, keepdims=True)

    def at_heads(row):
        row = jnp.concatenate([row, jnp.zeros((1, width - group), F32)], 1)
        return pltpu.roll(jnp.broadcast_to(row, (8, width)), me * group, 1)[0:1]

    head_q, head_v = at_heads(heads_sum[:, :group]), at_heads(heads_sum[:, 2 * group : 3 * group])
    index = lax.broadcasted_iota(jnp.int32, (16, width), 0)
    small = jnp.where(index == 0, sums[0], 0.0)
    small = jnp.where(index == 1, sums[1], small)
    own = db_all[pl.ds(pl.multiple_of(me * rows, rows), rows), :].astype(F32)
    small = jnp.where(index == 4, jnp.sum(own, 0, keepdims=True), small)
    slots = gb_ref.shape[1]
    block = lax.broadcasted_iota(jnp.int32, (16, slots), 1) - 96 * (
        lax.broadcasted_iota(jnp.int32, (16, slots), 0) - 7
    )
    hidden_rows = jnp.where((block >= 0) & (block < 96), gb_ref[...], 0.0).astype(BF16)
    small = small + dot(hidden_rows, spot_ref[...])
    small = jnp.where(index == 5, two_ref[0:1, :], small)
    small = jnp.where(index == 6, two_ref[1:2, :], small)
    small = jnp.where(index == 7 + slots // 96, two_ref[2:3, :], small)
    small = jnp.where(index == 2, head_q, small)
    small = jnp.where(index == 3, head_v, small).astype(BF16)
    row = lax.broadcasted_iota(jnp.int32, (16, 256), 0)
    lane = lax.broadcasted_iota(jnp.int32, (16, 256), 1)
    spread = (lane == row + group).astype(F32).astype(BF16)
    g_all[...] = dot(n1_ref[...], d_ref[:, 2 * group :], TN) + dot(small, spread, TN)
    if pieces == 0:
        outs[0][...] = g_all[...].astype(BF16)
        outs[1][...] = gp_all[...].astype(BF16)
        return
    split_halves(
        lambda where, j: g_all[where, :], outs[0], outs[1], half, lambda k, j: k * 4 + j, 256
    )

    def chunk(where, j):
        start = j * group
        block = gp_all[where, start // 128 * 128 : start // 128 * 128 + 256]
        if start % 128:
            block = pltpu.roll(block, 256 - start % 128, 1)
        return block[:, :group]

    split_halves(chunk, outs[0], outs[1], half, lambda k, j: k * 4 + me, group, 256)


def call(kernel, outs, scratch, flops, *args):
    whole = pl.BlockSpec(memory_space=pltpu.VMEM)
    specs = [pl.BlockSpec(memory_space=pltpu.SMEM)] + [whole] * (len(args) - 1)
    moved = sum(math.prod(a.shape) * a.dtype.itemsize for a in args)
    return pl.pallas_call(
        kernel,
        out_shape=[jax.ShapeDtypeStruct(shape, kind) for shape, kind in outs],
        in_specs=specs,
        out_specs=[whole] * len(outs),
        scratch_shapes=[pltpu.VMEM(shape, kind) for shape, kind in scratch],
        compiler_params=pltpu.CompilerParams(vmem_limit_bytes=VMEM_LIMIT),
        cost_estimate=pl.CostEstimate(flops=flops, bytes_accessed=moved, transcendentals=10**6),
    )(*args)


def shards(
    tokens,
    cotangent,
    qkv_weight,
    proj_weight,
    expand_weight,
    shrink_weight,
    small_params,
    qkv_first,
    proj_first,
    expand_first,
    shrink_first,
    small_first,
    qkv_second,
    proj_second,
    expand_second,
    shrink_second,
    small_second,
):
    rows, width = tokens.shape
    hidden = expand_weight.shape[1]
    own_rows = qkv_weight.shape[0]
    own_hidden = shrink_weight.shape[0]
    dp_count, seq_count, blk_count = (lax.axis_size(a) for a in ALL)
    plane = seq_count * blk_count
    assert (seq_count, blk_count) == (4, 2)
    dp, seq, blk = (lax.axis_index(a) for a in ALL)
    spot = seq * blk_count + blk
    group = width // seq_count
    slots = hidden // plane
    length = plane * rows
    half_length = length // blk_count
    small_rows = small_params.shape[0]
    place = jnp.stack([seq, blk, dp]).astype(jnp.int32)

    w_lanes = 3 * group + small_rows
    parts = qkv_weight.astype(BF16).reshape(own_rows, 3, seq_count, group)
    parts = jnp.transpose(parts, (2, 0, 1, 3)).reshape(seq_count, own_rows, 3 * group)
    small_part = jnp.broadcast_to(
        small_params.T.astype(BF16), (seq_count, own_rows, small_rows)
    )
    parts = jnp.concatenate([parts, small_part], 2)
    pieces = 4 if dp_count == 4 and own_rows % 8 == 0 else 0
    if pieces:
        picked = [lax.dynamic_index_in_dim(parts, seq ^ k, 0, keepdims=False) for k in range(4)]
        near = jnp.stack([picked[0]] + [swap(picked[k], k, 0) for k in range(1, 4)])
        layers = [near] + [shift(near, k) for k in range(1, 4)]
        w_parts = []
        for part in layers:
            w_parts += [part, swap(part, 0, 1)]
    else:
        parts = lax.all_to_all(parts, "seq", split_axis=0, concat_axis=0, tiled=True)
        both = lax.all_gather(parts, ("dp", "blk"), axis=0, tiled=False)
        both = both.reshape(dp_count, blk_count, seq_count, own_rows, w_lanes)
        layers = [parts]
        w_parts = [jnp.transpose(both, (0, 2, 1, 3, 4)).reshape(width, w_lanes)]

    tok_all = lax.all_gather(tokens, PLANE, axis=0, tiled=False)

    expand_parts = after(expand_weight, layers[0]).astype(BF16)
    expand_parts = expand_parts.reshape(own_rows, dp_count, plane, own_hidden)
    expand_parts = jnp.transpose(expand_parts, (2, 0, 1, 3)).reshape(plane, own_rows, slots)
    expand_parts = lax.all_to_all(expand_parts, PLANE, split_axis=0, concat_axis=0, tiled=True)
    proj_low = after(proj_weight, expand_parts).astype(BF16)
    if pieces:
        proj_moved = [proj_low] + [shift(proj_low, k) for k in range(1, 4)]
    else:
        proj_moved = [proj_low]
    expand_parts = after(expand_parts, *layers, *proj_moved, w_parts[min(1, pieces)], tok_all)
    expand_parts = expand_parts.reshape(2, own_hidden, slots)
    ff_own = jnp.concatenate(
        [
            shrink_weight.astype(BF16),
            jnp.concatenate([expand_parts[0], expand_parts[1]], 1),
        ],
        0,
    )
    ff_all = lax.all_gather(ff_own, "dp", axis=0, tiled=False)

    gate = w_parts[3 * (pieces > 0)]
    cot_low = after(cotangent, layers[-1])
    cot_two = after(jnp.stack([cot_low, swap(cot_low, 0, 1)]), gate)
    cot_far = swap(cot_two, 2, 0)

    if pieces:
        p_near = gather_steps(after(jnp.stack(proj_moved), gate))
        hidden_weights = (p_near, swap(p_near, 1, 0), ff_all)
    else:
        w_shrink = ff_all[:, :own_hidden].reshape(slots, width)
        w_expand = jnp.stack([ff_all[:, own_hidden:, :slots], ff_all[:, own_hidden:, slots:]], 1)
        proj_whole = lax.all_gather(proj_low, ALL, axis=0, tiled=True)
        hidden_weights = (proj_whole, w_expand.reshape(width, slots), w_shrink)

    w_parts[0] = after(w_parts[0], ff_own)

    unit_at = jnp.arange(slots) % (width // plane)
    unit_at = unit_at // own_hidden * (plane * own_hidden) + spot * own_hidden + unit_at % own_hidden
    spot_table = (unit_at[:, None] == jnp.arange(width)[None]).astype(BF16)

    wide = 640
    qkv, n1, att, lse, w_qkv, small_full = call(
        partial(forward_kernel, pieces),
        [
            ((length, wide), BF16),
            ((length, width), BF16),
            ((group, half_length), BF16),
            ((4, 3 * rows, 1), F32),
            ((width, wide), BF16),
            ((small_rows, width), F32),
        ],
        [((width, wide), F32)],
        2 * 10**9,
        place, *w_parts, tok_all,
    )
    extra = hidden // width
    zero = jnp.zeros((width,), F32)
    bias_expand = small_full[7 : 7 + extra].reshape(dp_count, plane, own_hidden)
    bias_expand = lax.dynamic_index_in_dim(bias_expand, spot, 1, keepdims=False).reshape(1, slots)
    bias_shrink = small_full[7 + extra]
    att, cot_two, cot_far = together(att, cot_two, cot_far)
    cot_a = jnp.concatenate([cot_two, cot_far], 0)
    cot_b = swap(cot_a, 1, 0)
    gain_one, gain_two = small_full[0], small_full[5]
    att_a, bias_expand, bias_shrink, gain_one, gain_two, spot_table = together(
        gather_near(att), bias_expand, bias_shrink, gain_one, gain_two, spot_table
    )
    att_b = swap(att_a, 1, 0)

    big = ((4, rows, width), BF16)
    if pieces:
        hidden_grads = [((dp_count, 2 * own_hidden, width), BF16)]
    else:
        hidden_grads = [((width, slots), BF16), ((slots, width), BF16)]
    out_a, out_b, dn_a, dn_b, mixed, unit, inverse, sums_two, gb_expand, own_proj, *ff_grad = call(
        partial(hidden_kernel, pieces),
        [
            big, big, big, big,
            ((rows, width), F32),
            ((rows, width), F32),
            ((rows, 1), F32),
            ((3, width), F32),
            ((1, slots), F32),
            ((256, width), BF16),
            *hidden_grads,
        ],
        [
            ((width, length), BF16),
            ((slots, width), F32),
            ((width, slots), F32),
            ((width, width), F32),
            ((width, width), BF16),
            ((width, slots), BF16),
            ((slots, width), BF16),
            ((length, slots), BF16),
            ((length, slots), BF16),
            ((length, width), BF16),
            ((length, width), BF16),
        ],
        6 * 10**9,
        place, tok_all, cot_a, cot_b, att_a, att_b, small_full, bias_expand, *hidden_weights,
    )

    dn_both = add_low(dn_a, swap(dn_b, 1, 0))

    cot_wide = cotangent.astype(F32)
    if pieces:
        ff_grad = ff_grad[0]
    else:
        ge = ff_grad[0].reshape(dp_count, 2, own_hidden, slots)
        ff_grad = jnp.concatenate(
            [
                ff_grad[1].reshape(dp_count, own_hidden, width),
                jnp.concatenate([ge[:, 0], ge[:, 1]], 2),
            ],
            1,
        )
    ff_sum = lax.psum_scatter(
        ff_grad.reshape(-1, width), "dp", scatter_dimension=0, tiled=True
    )
    out_both = add_low(out_a, swap(after(out_b, dn_both), 1, 0))

    dn_parts = lax.optimization_barrier((*spread_near(dn_both), out_both))
    d_normed_two = add_all(dn_parts[:4])
    out_both = dn_parts[4]
    d_mixed = cot_wide + norm_pull(unit, inverse, gain_two, d_normed_two)
    d_branch = d_mixed.astype(BF16)
    db_near = swap(d_branch, 1, 0)
    db_far = swap(d_branch, 2, 0)
    db_cross = swap(db_far, 1, 0)
    out_half = swap(after(out_both[1::2], d_branch), 0, 1)

    if pieces:
        first = ((4, 4, own_rows, 2 * group), BF16)
        second = ((4, 4, own_rows, 256 + group), BF16)
        first, second = [first] * 2, [second] * 2
    else:
        first = [((width, 2 * group), BF16)]
        second = [((width, 256), BF16), ((width, width), BF16)]
    d_low, db_all, *grads = call(
        partial(attention_back_kernel, pieces),
        [((length, wide), BF16), ((half_length, width), BF16), *first],
        [((length, wide), F32), ((width, 2 * group), F32)],
        10 * 10**9,
        place, d_branch, db_far, db_near, db_cross, qkv, lse, n1, own_proj,
    )
    grads = list(lax.optimization_barrier((*grads, out_half)))[:-1]

    def halves(table, lanes):
        table = table.reshape(dp_count, -1, blk_count, own_rows, lanes)
        keep = lax.dynamic_index_in_dim(table, blk, 2, keepdims=False)
        return keep, lax.dynamic_index_in_dim(table, 1 - blk, 2, keepdims=False)

    keep, send = grads if pieces else halves(grads[0], 2 * group)
    g_first = add_low(keep, swap(send, 0, 1))
    out_two = add_low(after(out_both, d_low)[0::2], out_half)

    dn_a, dn_b, *grads = call(
        partial(norm_back_kernel, pieces),
        [big, big, *second],
        [((width, 256), F32), ((width, width), F32)],
        6 * 10**9,
        place, after(d_low, out_two), db_all, n1, tok_all, att_a, att_b, w_qkv,
        sums_two, gb_expand, spot_table,
    )
    if pieces:
        keep, send = grads
    else:
        v_keep, v_send = halves(grads[0], 256)
        gp = grads[1].reshape(dp_count, seq_count, blk_count, own_rows, seq_count, group)
        gp = lax.dynamic_index_in_dim(gp, seq, 1, keepdims=False)
        gp = jnp.transpose(gp, (0, 3, 1, 2, 4))
        p_keep, p_send = halves(gp, group)
        keep = jnp.concatenate([v_keep, p_keep], -1)
        send = jnp.concatenate([v_send, p_send], -1)
    g_first, keep, send, dn_a, dn_b = together(g_first, keep, send, dn_a, dn_b)
    first_parts = spread_dp(g_first)
    g_got = swap(send, 0, 1)
    dn_got = swap(dn_b, 1, 0)
    out_last = swap(after(out_two[1], g_first), 2, 0)
    *first_parts, keep, g_got, dn_a, dn_got, out_last = together(
        *first_parts, keep, g_got, dn_a, dn_got, out_last
    )

    rest_parts = spread_dp(add_low(keep, g_got))
    dn_parts = spread_near(add_low(dn_a, dn_got))
    g_first = add_all(first_parts)
    ff_sum = after(ff_sum, g_got)
    sum_expand = ff_sum[own_hidden:]
    sum_expand = jnp.stack([sum_expand[:, :slots], sum_expand[:, slots:]])
    expand_send = sum_expand.reshape(plane, own_rows, slots)
    shrink_out = adam_update(
        shrink_weight,
        shrink_first,
        shrink_second,
        ff_sum[:own_hidden].astype(F32),
        matrix_rate,
        matrix_decay,
    )
    *rest_parts, dn_0, dn_1, dn_2, dn_3, expand_send, shrink_0, shrink_1, shrink_2 = together(
        *rest_parts, *dn_parts, expand_send, *shrink_out
    )
    shrink_out = (shrink_0, shrink_1, shrink_2)
    g_rest = add_all(rest_parts)

    sum_expand = lax.all_to_all(expand_send, PLANE, split_axis=0, concat_axis=0, tiled=True)
    block_out = mixed + (out_two[0].astype(F32) + out_last.astype(F32)) + bias_shrink

    g_all = jnp.concatenate([g_first, g_rest[:, :, : group + small_rows]], -1).astype(BF16)
    picked = [lax.dynamic_index_in_dim(g_all, seq ^ k, 0, keepdims=False) for k in range(4)]
    picked = jnp.stack([picked[0]] + [swap(picked[k], k, 0) for k in range(1, 4)]).astype(F32)
    g_all = [lax.dynamic_index_in_dim(picked, seq ^ k, 0, keepdims=False) for k in range(4)]
    g_all = jnp.stack(g_all)
    sum_proj = jnp.transpose(g_rest[:, :, 256:], (1, 0, 2)).reshape(own_rows, width)
    sum_small = jnp.sum(picked[:, :, 3 * group :], 0).T
    sum_qkv = jnp.transpose(
        g_all[:, :, : 3 * group].reshape(seq_count, own_rows, 3, group), (1, 2, 0, 3)
    ).reshape(own_rows, 3 * width)
    sum_expand = jnp.transpose(
        sum_expand.reshape(plane, own_rows, dp_count, own_hidden), (1, 2, 0, 3)
    ).reshape(own_rows, hidden).astype(F32)

    d_normed_one = add_all((dn_0, dn_1, dn_2, dn_3))
    unit, inverse = norm_parts(tokens.astype(F32))
    token_grad = d_mixed + norm_pull(unit, inverse, gain_one, d_normed_one)

    qkv_out = adam_update(
        qkv_weight, qkv_first, qkv_second, sum_qkv, matrix_rate, matrix_decay
    )
    proj_out = adam_update(
        proj_weight, proj_first, proj_second, sum_proj, matrix_rate, matrix_decay
    )
    expand_out = adam_update(
        expand_weight, expand_first, expand_second, sum_expand, matrix_rate, matrix_decay
    )
    small_out = adam_update(
        small_params, small_first, small_second, sum_small, small_rate, 0.0
    )
    return (block_out, token_grad, *qkv_out, *proj_out, *expand_out, *shrink_out, *small_out)


def solution(mesh):
    by_rows = P(ALL, None)
    by_columns = P(None, ALL)
    state = (by_rows,) * 4 + (by_columns,)
    return jax.shard_map(
        shards,
        mesh=mesh,
        in_specs=(by_rows, by_rows) + state * 3,
        out_specs=(by_rows,) * 14 + (by_columns,) * 3,
        check_vma=False,
    )
```

```python
from functools import partial
import math

import jax
import jax.numpy as jnp
from jax import lax
from jax.experimental import pallas as pl
from jax.experimental.pallas import tpu as pltpu
from jax.sharding import PartitionSpec as P

HEAD = 64
STEP = 10

norm_eps = 1e-05
beta_one = 0.9
beta_two = 0.95
adam_eps = 1e-08
matrix_rate = 0.05
matrix_decay = 0.1
small_rate = 0.5
masked_score = -1e30
score_scale = 1.0 / math.sqrt(HEAD)

F32 = jnp.float32
BF16 = jnp.bfloat16
ALL = ("dp", "seq", "blk")
PLANE = ("seq", "blk")
VMEM_LIMIT = 56 * 1024 * 1024
NT = (((1,), (1,)), ((), ()))
TN = (((0,), (0,)), ((), ()))


def dot(a, b, dims=None):
    if dims is None:
        return jnp.dot(a, b, preferred_element_type=F32)
    return lax.dot_general(a, b, dims, preferred_element_type=F32)


def adam_update(weight, first_state, second, gradient, step_rate, decay_rate):
    moment = beta_one * first_state + (1.0 - beta_one) * gradient
    variance = beta_two * second + (1.0 - beta_two) * gradient * gradient
    mean_fixed = moment / (1.0 - beta_one**STEP)
    var_fixed = variance / (1.0 - beta_two**STEP)
    updated = weight - step_rate * (
        mean_fixed / (jnp.sqrt(var_fixed) + adam_eps) + decay_rate * weight
    )
    return (moment, variance, updated)


def norm_parts(values):
    center = jnp.mean(values, -1, keepdims=True)
    spread = values - center
    inverse = lax.rsqrt(jnp.mean(spread * spread, -1, keepdims=True) + norm_eps)
    return spread * inverse, inverse


def norm_pull(unit, inverse, gain, grad):
    scaled = grad * gain
    first = jnp.mean(scaled, -1, keepdims=True)
    second = jnp.mean(scaled * unit, -1, keepdims=True)
    return inverse * (scaled - first - unit * second)


def swap(value, seq_bits, blk_bits):
    seq_count, blk_count = lax.axis_size("seq"), lax.axis_size("blk")
    pairs = [
        (i * blk_count + j, (i ^ seq_bits) * blk_count + (j ^ blk_bits))
        for i in range(seq_count)
        for j in range(blk_count)
    ]
    return lax.ppermute(value, PLANE, pairs)


def shift(value, step):
    count = lax.axis_size("dp")
    return lax.ppermute(value, "dp", [(i, (i + step) % count) for i in range(count)])


def gather_near(value):
    return jnp.stack([value, swap(value, 0, 1), swap(value, 2, 0), swap(value, 2, 1)])


def after(value, *others):
    return lax.optimization_barrier((value, *others))[0]


def together(*values):
    return lax.optimization_barrier(values)


def gather_steps(value):
    two = jnp.stack([value, swap(value, 0, 1)])
    return jnp.concatenate([two, swap(two, 2, 0)], 0)


def add_low(a, b):
    return (a.astype(F32) + b.astype(F32)).astype(BF16)


def spread_near(both):
    return both[0], swap(both[1], 0, 1), swap(both[2], 2, 0), swap(both[3], 2, 1)


def add_all(parts):
    total = parts[0].astype(F32)
    for part in parts[1:]:
        total = total + part.astype(F32)
    return total


def spread_dp(value):
    count = lax.axis_size("dp")
    if count != 4:
        return [lax.psum_scatter(value, "dp", scatter_dimension=0, tiled=False)]
    me = lax.axis_index("dp")
    parts = [lax.dynamic_index_in_dim(value, me, 0, keepdims=False)]
    for k in range(1, count):
        chunk = lax.dynamic_index_in_dim(value, (me + k) % count, 0, keepdims=False)
        parts.append(shift(chunk, k))
    return parts


def head_masks(first, group):
    lane = lax.broadcasted_iota(jnp.int32, (1, 256), 1) - first
    return [(lane >= h * HEAD) & (lane < (h + 1) * HEAD) for h in range(group // HEAD)]


def turned(block):
    return pltpu.roll(block.astype(F32), 64, 1).astype(BF16)


def spread_heads(block, masks):
    return jnp.concatenate([jnp.where(m, block, jnp.zeros_like(block)) for m in masks], 0)


def join_heads(stacked, masks):
    rows = stacked.shape[0] // len(masks)
    out = jnp.where(masks[0], stacked[:rows], 0.0)
    for h in range(1, len(masks)):
        out = out + jnp.where(masks[h], stacked[h * rows : (h + 1) * rows], 0.0)
    return out


def visible(heads, rows, keys, first_row):
    row = lax.broadcasted_iota(jnp.int32, (heads, rows, keys), 1).reshape(heads * rows, keys)
    key = lax.broadcasted_iota(jnp.int32, (heads * rows, keys), 1)
    return key <= row + first_row


def both_rows(tok_all, at, half):
    rows = [tok_all[2 * at + half], tok_all[2 * at + 1 - half]]
    return jnp.concatenate(rows, 0).astype(F32)


def forward_kernel(pieces, place, *refs):
    me, half, layer = place[0], place[1], place[2]
    w_parts, refs = refs[: max(1, 2 * pieces)], refs[max(1, 2 * pieces) :]
    tok_all, qkv_ref, n1_ref, att_ref, lse_ref, w_ref, small_ref, w32 = refs
    rows = tok_all.shape[1]
    group = att_ref.shape[0]
    wide = w32.shape[1]
    tail = wide - 128
    w32[:, tail:wide] = jnp.zeros((w32.shape[0], 128), F32)
    if pieces == 0:
        w32[:, : w_parts[0].shape[1]] = w_parts[0][...].astype(F32)
    for k in range(pieces):
        own_layer = lax.rem(layer + (pieces - k), pieces)
        for other in range(2):
            part = w_parts[2 * k + other]
            for j in range(4):
                owner = (own_layer * 4 + (me ^ j)) * 2 + (half ^ other)
                count = part.shape[1]
                where = pl.ds(pl.multiple_of(owner * count, 8), count)
                w32[where, : part.shape[2]] = part[j].astype(F32)
    w_low = w32[...].astype(BF16)
    w_ref[...] = w_low
    first = 3 * group - tail
    small = w32[:, tail:wide].T
    small_ref[...] = small[first : first + small_ref.shape[0]]
    width = small_ref.shape[1]
    turned_small = pltpu.roll(small[first : first + 8], width - me * group, 1)
    bias = jnp.concatenate(
        [
            turned_small[2:3, :group],
            jnp.zeros((1, group), F32),
            turned_small[3:4, :group],
            jnp.zeros((1, wide - 3 * group), F32),
        ],
        1,
    )
    gain, lift = small_ref[0:1, :], small_ref[1:2, :]
    for bit in range(2):
        for far in range(2):
            at = me ^ (2 * far + bit)
            unit, _ = norm_parts(both_rows(tok_all, at, half))
            n1 = (unit * gain + lift).astype(BF16)
            out = (dot(n1, w_low) + bias).astype(BF16)
            for other in range(2):
                where = pl.ds(pl.multiple_of((2 * at + (half ^ other)) * rows, rows), rows)
                n1_ref[where, :] = n1[other * rows : (other + 1) * rows]
                qkv_ref[where, :] = out[other * rows : (other + 1) * rows]
    shifted, plain = head_masks(64, group), head_masks(0, group)
    heads = len(plain)
    for i in range(4):
        keys = 2 * rows * (i + 1)
        where = pl.ds(pl.multiple_of((2 * i + half) * rows, rows), rows)
        queries = spread_heads(turned(qkv_ref[where, 0:256]), shifted)
        scores = dot(queries, qkv_ref[0:keys, 128:384], NT) * score_scale
        seen = visible(heads, rows, keys, (2 * i + half) * rows)
        scores = jnp.where(seen, scores, masked_score)
        top = jnp.max(scores, -1, keepdims=True)
        raised = jnp.exp(scores - top)
        total = jnp.sum(raised, -1, keepdims=True)
        probs = (raised / total).astype(BF16)
        result = join_heads(dot(probs, qkv_ref[0:keys, 384:640]), plain)
        att_ref[:, i * rows : (i + 1) * rows] = result.T[:group].astype(BF16)
        lse_ref[i] = top + jnp.log(total)


def hidden_kernel(
    pieces, place, tok_all, cot_a, cot_b, att_a, att_b, vec_ref, be_ref, *refs
):
    given, refs = refs[:3], refs[3:]
    out_a, out_b, dn_a, dn_b, mixed_ref, unit_ref, inverse_ref, sums_ref, gb_ref, own_ref = refs[:10]
    g_outs, refs = refs[10:-11], refs[-11:]
    att_all, gs_sum, ge_sum, p32, proj_ref, we_ref, ws_ref, act_all, pre_all, n2_all, cot_all = refs
    me, half, layer = place[0], place[1], place[2]
    if pieces == 0:
        p32[...] = given[0][...].astype(F32)
        we_ref[...] = given[1][...]
        ws_ref[...] = given[2][...]
    else:
        p_parts, ff_ref = given[:2], given[2]
        slots, part = ws_ref.shape[0], ws_ref.shape[0] // pieces
        for k in range(pieces):
            ws_ref[k * part : (k + 1) * part, :] = ff_ref[k, 0:part, :]
            for side in range(2):
                we_ref[(2 * k + side) * part : (2 * k + side + 1) * part, :] = ff_ref[
                    k, part:, side * slots : (side + 1) * slots
                ]
        for bit in range(2):
            for j in range(4):
                for k in range(pieces):
                    own_layer = lax.rem(layer + (pieces - k), pieces)
                    owner = (own_layer * 4 + (me ^ ((j & 2) + bit))) * 2 + (half ^ (j & 1))
                    count = p_parts[bit].shape[2]
                    where = pl.ds(pl.multiple_of(owner * count, 8), count)
                    p32[where, :] = p_parts[bit][j, k].astype(F32)
    proj_ref[...] = p32[...].astype(BF16)
    rows = tok_all.shape[1]
    span = 4 * rows
    group = att_a.shape[1]
    for bit in range(2):
        att = (att_a, att_b)[bit]
        for far in range(2):
            at = me ^ (2 * far + bit)
            where = pl.ds(pl.multiple_of(at * group, 64), group)
            if bit == 0 and far == 0:
                own_ref[0:group, :] = p32[where, :].astype(BF16)
                own_ref[group:, :] = jnp.zeros((own_ref.shape[0] - group, own_ref.shape[1]), BF16)
            for other in range(2):
                att_all[where, other * span : (other + 1) * span] = att[2 * far + other]
    bias_proj, gain, lift = vec_ref[4:5, :], vec_ref[5:6, :], vec_ref[6:7, :]
    sums = [jnp.zeros((1, gain.shape[1]), F32)] * 2
    gb = jnp.zeros((1, gb_ref.shape[1]), F32)
    sums_ref[2:3, :] = jnp.sum(cot_a[0].astype(F32), 0, keepdims=True)
    for bit in range(2):
        cot, out, dn = (cot_a, cot_b)[bit], (out_a, out_b)[bit], (dn_a, dn_b)[bit]
        for far in range(2):
            start = pl.multiple_of((me ^ (2 * far + bit)) * rows, rows)
            att = jnp.concatenate(
                [
                    att_all[:, pl.ds(start, rows)],
                    att_all[:, pl.ds(pl.multiple_of(span + start, rows), rows)],
                ],
                1,
            )
            two = both_rows(tok_all, me ^ (2 * far + bit), half)
            mixed = two + (dot(att, proj_ref[...], TN) + bias_proj)
            if bit == 0 and far == 0:
                mixed_ref[...] = mixed[:rows]
            unit, inverse = norm_parts(mixed)
            if bit == 0 and far == 0:
                unit_ref[...] = unit[:rows]
                inverse_ref[...] = inverse[:rows]
            n2 = (unit * gain + lift).astype(BF16)
            pre = dot(n2, we_ref[...]) + be_ref[...]
            cots = cot[2 * far : 2 * far + 2].reshape(2 * rows, -1)
            factor = math.sqrt(2.0 / math.pi)
            square = pre * pre
            bent = jnp.tanh(factor * pre * (1.0 + 0.044715 * square))
            act = (0.5 * pre * (1.0 + bent)).astype(BF16)
            slope = 0.5 * (1.0 + bent) + 0.5 * pre * (1.0 - bent * bent) * (
                factor * (1.0 + 3.0 * 0.044715 * square)
            )
            d_act = dot(cots, ws_ref[...], NT)
            d_pre32 = d_act * slope
            d_pre = d_pre32.astype(BF16)
            d_n2 = dot(d_pre, we_ref[...], NT)
            dn[2 * far : 2 * far + 2] = d_n2.astype(BF16).reshape(2, rows, -1)
            out[2 * far : 2 * far + 2] = dot(act, ws_ref[...]).astype(BF16).reshape(2, rows, -1)
            step = pl.ds((2 * bit + far) * 2 * rows, 2 * rows)
            act_all[step, :] = act
            pre_all[step, :] = d_pre
            n2_all[step, :] = n2
            cot_all[step, :] = cots
            sums[0] = sums[0] + jnp.sum(d_n2 * unit, 0, keepdims=True)
            sums[1] = sums[1] + jnp.sum(d_n2, 0, keepdims=True)
            gb = gb + jnp.sum(d_pre.astype(F32), 0, keepdims=True)
    gs_sum[...] = dot(act_all[...], cot_all[...], TN)
    ge_sum[...] = dot(n2_all[...], pre_all[...], TN)
    sums_ref[0:1, :] = sums[0]
    sums_ref[1:2, :] = sums[1]
    gb_ref[...] = gb
    if pieces == 0:
        g_outs[0][...] = ge_sum[...].astype(BF16)
        g_outs[1][...] = gs_sum[...].astype(BF16)
        return
    pack = g_outs[0]
    for k in range(pieces):
        pack[k, 0:part, :] = gs_sum[k * part : (k + 1) * part, :].astype(BF16)
        for side in range(2):
            pack[k, part:, side * slots : (side + 1) * slots] = ge_sum[
                (2 * k + side) * part : (2 * k + side + 1) * part, :
            ].astype(BF16)


def split_halves(table, keep, send, half, row_of, lanes, at=0):
    layers, four, count, _ = keep.shape
    for k in range(layers):
        for j in range(four):
            base = row_of(k, j) * 2
            for out, owner in ((keep, base + half), (send, base + 1 - half)):
                where = pl.ds(pl.multiple_of(owner * count, 8), count)
                out[k, j, :, at : at + lanes] = table(where, j).astype(BF16)


def attention_back_kernel(
    pieces, place, db_own, db_far, db_near, db_cross, qkv_ref, lse_ref, n1_ref, own_proj, *refs
):
    d_ref, db_all, outs, (d_all, g_all) = refs[0], refs[1], refs[2:-2], refs[-2:]
    me, half = place[0], place[1]
    rows = db_own.shape[0]
    group = 3 * HEAD
    shifted, plain = head_masks(64, group), head_masks(0, group)
    heads = len(plain)
    for bits, db in ((0, db_own), (2, db_far), (1, db_near), (3, db_cross)):
        db_all[pl.ds(pl.multiple_of((me ^ bits) * rows, rows), rows), :] = db[...]
    d_all[...] = jnp.zeros_like(d_all)
    for i in range(4):
        keys = 2 * rows * (i + 1)
        where = pl.ds(pl.multiple_of((2 * i + half) * rows, rows), rows)
        queries = spread_heads(turned(qkv_ref[where, 0:256]), shifted)
        d_att = dot(db_all[i * rows : (i + 1) * rows, :], own_proj[...], NT).astype(BF16)
        grads = spread_heads(d_att, plain)
        key_rows, values = qkv_ref[0:keys, 128:384], qkv_ref[0:keys, 384:640]
        scores = dot(queries, key_rows, NT) * score_scale
        seen = visible(heads, rows, keys, (2 * i + half) * rows)
        probs = jnp.where(seen, jnp.exp(scores - lse_ref[i]), 0.0)
        weighed = probs * dot(grads, values, NT)
        d_scores = (weighed - probs * jnp.sum(weighed, -1, keepdims=True)).astype(BF16)
        dq = join_heads(dot(d_scores, key_rows), shifted) * score_scale
        d_all[where, 0:256] += pltpu.roll(dq, 192, 1)
        d_all[0:keys, 128:384] += dot(d_scores, queries, TN) * score_scale
        d_all[0:keys, 384:640] += dot(probs.astype(BF16), grads, TN)
    d_ref[...] = d_all[...].astype(BF16)
    g_all[...] = dot(n1_ref[...], d_ref[:, 0 : 2 * group], TN)
    if pieces == 0:
        outs[0][...] = g_all[...].astype(BF16)
    else:
        split_halves(
            lambda where, j: g_all[where, :], outs[0], outs[1], half, lambda k, j: k * 4 + j, 2 * group
        )


def norm_back_kernel(
    pieces, place, d_ref, db_all, n1_ref, tok_all, att_a, att_b, w_ref, two_ref, gb_ref, spot_ref,
    dn_a, dn_b, *refs
):
    outs, (g_all, gp_all) = refs[:-2], refs[-2:]
    me, half = place[0], place[1]
    rows = tok_all.shape[1]
    group = att_a.shape[1]
    wide, width = d_ref.shape[1], n1_ref.shape[1]
    sums = [jnp.zeros((1, width), F32)] * 2
    for bit in range(2):
        dn = (dn_a, dn_b)[bit]
        for far in range(2):
            at = me ^ (2 * far + bit)
            gp_all[pl.ds(pl.multiple_of(at * group, 64), group), :] = dot(
                (att_a, att_b)[bit][2 * far], db_all[...]
            )
            for other in range(2):
                where = pl.ds(pl.multiple_of((2 * at + (half ^ other)) * rows, rows), rows)
                d_n1 = dot(d_ref[where, :], w_ref[...], NT)
                unit, _ = norm_parts(tok_all[2 * at + (half ^ other)].astype(F32))
                dn[2 * far + other] = d_n1.astype(BF16)
                sums[0] = sums[0] + jnp.sum(d_n1 * unit, 0, keepdims=True)
                sums[1] = sums[1] + jnp.sum(d_n1, 0, keepdims=True)
    heads_sum = jnp.sum(d_ref[...].astype(F32), 0, keepdims=True)

    def at_heads(row):
        row = jnp.concatenate([row, jnp.zeros((1, width - group), F32)], 1)
        return pltpu.roll(jnp.broadcast_to(row, (8, width)), me * group, 1)[0:1]

    head_q, head_v = at_heads(heads_sum[:, :group]), at_heads(heads_sum[:, 2 * group : 3 * group])
    index = lax.broadcasted_iota(jnp.int32, (16, width), 0)
    small = jnp.where(index == 0, sums[0], 0.0)
    small = jnp.where(index == 1, sums[1], small)
    own = db_all[pl.ds(pl.multiple_of(me * rows, rows), rows), :].astype(F32)
    small = jnp.where(index == 4, jnp.sum(own, 0, keepdims=True), small)
    slots = gb_ref.shape[1]
    block = lax.broadcasted_iota(jnp.int32, (16, slots), 1) - 96 * (
        lax.broadcasted_iota(jnp.int32, (16, slots), 0) - 7
    )
    hidden_rows = jnp.where((block >= 0) & (block < 96), gb_ref[...], 0.0).astype(BF16)
    small = small + dot(hidden_rows, spot_ref[...])
    small = jnp.where(index == 5, two_ref[0:1, :], small)
    small = jnp.where(index == 6, two_ref[1:2, :], small)
    small = jnp.where(index == 7 + slots // 96, two_ref[2:3, :], small)
    small = jnp.where(index == 2, head_q, small)
    small = jnp.where(index == 3, head_v, small).astype(BF16)
    row = lax.broadcasted_iota(jnp.int32, (16, 256), 0)
    lane = lax.broadcasted_iota(jnp.int32, (16, 256), 1)
    spread = (lane == row + group).astype(F32).astype(BF16)
    g_all[...] = dot(n1_ref[...], d_ref[:, 2 * group :], TN) + dot(small, spread, TN)
    if pieces == 0:
        outs[0][...] = g_all[...].astype(BF16)
        outs[1][...] = gp_all[...].astype(BF16)
        return
    split_halves(
        lambda where, j: g_all[where, :], outs[0], outs[1], half, lambda k, j: k * 4 + j, 256
    )

    def chunk(where, j):
        start = j * group
        block = gp_all[where, start // 128 * 128 : start // 128 * 128 + 256]
        if start % 128:
            block = pltpu.roll(block, 256 - start % 128, 1)
        return block[:, :group]

    split_halves(chunk, outs[0], outs[1], half, lambda k, j: k * 4 + me, group, 256)


def call(kernel, outs, scratch, flops, *args, limit=VMEM_LIMIT):
    whole = pl.BlockSpec(memory_space=pltpu.VMEM)
    specs = [pl.BlockSpec(memory_space=pltpu.SMEM)] + [whole] * (len(args) - 1)
    moved = sum(math.prod(a.shape) * a.dtype.itemsize for a in args)
    return pl.pallas_call(
        kernel,
        out_shape=[jax.ShapeDtypeStruct(shape, kind) for shape, kind in outs],
        in_specs=specs,
        out_specs=[whole] * len(outs),
        scratch_shapes=[pltpu.VMEM(shape, kind) for shape, kind in scratch],
        compiler_params=pltpu.CompilerParams(vmem_limit_bytes=limit),
        cost_estimate=pl.CostEstimate(flops=flops, bytes_accessed=moved, transcendentals=10**6),
    )(*args)


def shards(
    tokens,
    cotangent,
    qkv_weight,
    proj_weight,
    expand_weight,
    shrink_weight,
    small_params,
    qkv_first,
    proj_first,
    expand_first,
    shrink_first,
    small_first,
    qkv_second,
    proj_second,
    expand_second,
    shrink_second,
    small_second,
):
    rows, width = tokens.shape
    hidden = expand_weight.shape[1]
    own_rows = qkv_weight.shape[0]
    own_hidden = shrink_weight.shape[0]
    dp_count, seq_count, blk_count = (lax.axis_size(a) for a in ALL)
    plane = seq_count * blk_count
    assert (seq_count, blk_count) == (4, 2)
    dp, seq, blk = (lax.axis_index(a) for a in ALL)
    spot = seq * blk_count + blk
    group = width // seq_count
    slots = hidden // plane
    length = plane * rows
    half_length = length // blk_count
    small_rows = small_params.shape[0]
    place = jnp.stack([seq, blk, dp]).astype(jnp.int32)

    w_lanes = 3 * group + small_rows
    parts = qkv_weight.astype(BF16).reshape(own_rows, 3, seq_count, group)
    parts = jnp.transpose(parts, (2, 0, 1, 3)).reshape(seq_count, own_rows, 3 * group)
    small_part = jnp.broadcast_to(
        small_params.T.astype(BF16), (seq_count, own_rows, small_rows)
    )
    parts = jnp.concatenate([parts, small_part], 2)
    pieces = 4 if dp_count == 4 and own_rows % 8 == 0 else 0
    if pieces:
        picked = [lax.dynamic_index_in_dim(parts, seq ^ k, 0, keepdims=False) for k in range(4)]
        near = jnp.stack([picked[0]] + [swap(picked[k], k, 0) for k in range(1, 4)])
        layers = [near] + [shift(near, k) for k in range(1, 4)]
        w_parts = []
        for part in layers:
            w_parts += [part, swap(part, 0, 1)]
    else:
        parts = lax.all_to_all(parts, "seq", split_axis=0, concat_axis=0, tiled=True)
        both = lax.all_gather(parts, ("dp", "blk"), axis=0, tiled=False)
        both = both.reshape(dp_count, blk_count, seq_count, own_rows, w_lanes)
        layers = [parts]
        w_parts = [jnp.transpose(both, (0, 2, 1, 3, 4)).reshape(width, w_lanes)]

    tok_all = lax.all_gather(tokens, PLANE, axis=0, tiled=False)

    expand_parts = after(expand_weight, layers[0]).astype(BF16)
    expand_parts = expand_parts.reshape(own_rows, dp_count, plane, own_hidden)
    expand_parts = jnp.transpose(expand_parts, (2, 0, 1, 3)).reshape(plane, own_rows, slots)
    expand_parts = lax.all_to_all(expand_parts, PLANE, split_axis=0, concat_axis=0, tiled=True)
    proj_low = after(proj_weight, expand_parts).astype(BF16)
    if pieces:
        proj_moved = [proj_low] + [shift(proj_low, k) for k in range(1, 4)]
    else:
        proj_moved = [proj_low]
    expand_parts = after(expand_parts, *layers, *proj_moved, w_parts[min(1, pieces)], tok_all)
    expand_parts = expand_parts.reshape(2, own_hidden, slots)
    ff_own = jnp.concatenate(
        [
            shrink_weight.astype(BF16),
            jnp.concatenate([expand_parts[0], expand_parts[1]], 1),
        ],
        0,
    )
    ff_all = lax.all_gather(ff_own, "dp", axis=0, tiled=False)

    gate = w_parts[3 * (pieces > 0)]
    cot_low = after(cotangent, layers[-1])
    cot_two = after(jnp.stack([cot_low, swap(cot_low, 0, 1)]), gate)
    cot_far = swap(cot_two, 2, 0)

    if pieces:
        p_near = gather_steps(after(jnp.stack(proj_moved), gate))
        hidden_weights = (p_near, swap(p_near, 1, 0), ff_all)
    else:
        w_shrink = ff_all[:, :own_hidden].reshape(slots, width)
        w_expand = jnp.stack([ff_all[:, own_hidden:, :slots], ff_all[:, own_hidden:, slots:]], 1)
        proj_whole = lax.all_gather(proj_low, ALL, axis=0, tiled=True)
        hidden_weights = (proj_whole, w_expand.reshape(width, slots), w_shrink)

    w_parts[0] = after(w_parts[0], ff_own)

    unit_at = jnp.arange(slots) % (width // plane)
    unit_at = unit_at // own_hidden * (plane * own_hidden) + spot * own_hidden + unit_at % own_hidden
    spot_table = (unit_at[:, None] == jnp.arange(width)[None]).astype(BF16)

    wide = 640
    qkv, n1, att, lse, w_qkv, small_full = call(
        partial(forward_kernel, pieces),
        [
            ((length, wide), BF16),
            ((length, width), BF16),
            ((group, half_length), BF16),
            ((4, 3 * rows, 1), F32),
            ((width, wide), BF16),
            ((small_rows, width), F32),
        ],
        [((width, wide), F32)],
        2 * 10**9,
        place, *w_parts, tok_all,
    )
    extra = hidden // width
    zero = jnp.zeros((width,), F32)
    bias_expand = small_full[7 : 7 + extra].reshape(dp_count, plane, own_hidden)
    bias_expand = lax.dynamic_index_in_dim(bias_expand, spot, 1, keepdims=False).reshape(1, slots)
    bias_shrink = small_full[7 + extra]
    att, cot_two, cot_far = together(att, cot_two, cot_far)
    cot_a = jnp.concatenate([cot_two, cot_far], 0)
    cot_b = swap(cot_a, 1, 0)
    gain_one, gain_two = small_full[0], small_full[5]
    att_a, bias_expand, bias_shrink, gain_one, gain_two, spot_table = together(
        gather_near(att), bias_expand, bias_shrink, gain_one, gain_two, spot_table
    )
    att_b = swap(att_a, 1, 0)

    big = ((4, rows, width), BF16)
    if pieces:
        hidden_grads = [((dp_count, 2 * own_hidden, width), BF16)]
    else:
        hidden_grads = [((width, slots), BF16), ((slots, width), BF16)]
    out_a, out_b, dn_a, dn_b, mixed, unit, inverse, sums_two, gb_expand, own_proj, *ff_grad = call(
        partial(hidden_kernel, pieces),
        [
            big, big, big, big,
            ((rows, width), F32),
            ((rows, width), F32),
            ((rows, 1), F32),
            ((3, width), F32),
            ((1, slots), F32),
            ((256, width), BF16),
            *hidden_grads,
        ],
        [
            ((width, length), BF16),
            ((slots, width), F32),
            ((width, slots), F32),
            ((width, width), F32),
            ((width, width), BF16),
            ((width, slots), BF16),
            ((slots, width), BF16),
            ((length, slots), BF16),
            ((length, slots), BF16),
            ((length, width), BF16),
            ((length, width), BF16),
        ],
        6 * 10**9,
        place, tok_all, cot_a, cot_b, att_a, att_b, small_full, bias_expand, *hidden_weights,
    )

    dn_both = add_low(dn_a, swap(dn_b, 1, 0))

    cot_wide = cotangent.astype(F32)
    if pieces:
        ff_grad = ff_grad[0]
    else:
        ge = ff_grad[0].reshape(dp_count, 2, own_hidden, slots)
        ff_grad = jnp.concatenate(
            [
                ff_grad[1].reshape(dp_count, own_hidden, width),
                jnp.concatenate([ge[:, 0], ge[:, 1]], 2),
            ],
            1,
        )
    ff_sum = lax.psum_scatter(
        ff_grad.reshape(-1, width), "dp", scatter_dimension=0, tiled=True
    )
    out_both = add_low(out_a, swap(after(out_b, dn_both), 1, 0))

    dn_parts = lax.optimization_barrier((*spread_near(dn_both), out_both))
    d_normed_two = add_all(dn_parts[:4])
    out_both = dn_parts[4]
    d_mixed = cot_wide + norm_pull(unit, inverse, gain_two, d_normed_two)
    d_branch = d_mixed.astype(BF16)
    db_near = swap(d_branch, 1, 0)
    db_far = swap(d_branch, 2, 0)
    db_cross = swap(db_far, 1, 0)
    out_half = swap(after(out_both[1::2], d_branch), 0, 1)

    if pieces:
        first = ((4, 4, own_rows, 2 * group), BF16)
        second = ((4, 4, own_rows, 256 + group), BF16)
        first, second = [first] * 2, [second] * 2
    else:
        first = [((width, 2 * group), BF16)]
        second = [((width, 256), BF16), ((width, width), BF16)]
    d_low, db_all, *grads = call(
        partial(attention_back_kernel, pieces),
        [((length, wide), BF16), ((half_length, width), BF16), *first],
        [((length, wide), F32), ((width, 2 * group), F32)],
        10 * 10**9,
        place, d_branch, db_far, db_near, db_cross, qkv, lse, n1, own_proj,
    )
    grads = list(lax.optimization_barrier((*grads, out_half)))[:-1]

    def halves(table, lanes):
        table = table.reshape(dp_count, -1, blk_count, own_rows, lanes)
        keep = lax.dynamic_index_in_dim(table, blk, 2, keepdims=False)
        return keep, lax.dynamic_index_in_dim(table, 1 - blk, 2, keepdims=False)

    keep, send = grads if pieces else halves(grads[0], 2 * group)
    g_first = add_low(keep, swap(send, 0, 1))
    out_two = add_low(after(out_both, d_low)[0::2], out_half)

    dn_a, dn_b, *grads = call(
        partial(norm_back_kernel, pieces),
        [big, big, *second],
        [((width, 256), F32), ((width, width), F32)],
        6 * 10**9,
        place, after(d_low, out_two), db_all, n1, tok_all, att_a, att_b, w_qkv,
        sums_two, gb_expand, spot_table,
        limit=36 * 1024 * 1024,
    )
    if pieces:
        keep, send = grads
    else:
        v_keep, v_send = halves(grads[0], 256)
        gp = grads[1].reshape(dp_count, seq_count, blk_count, own_rows, seq_count, group)
        gp = lax.dynamic_index_in_dim(gp, seq, 1, keepdims=False)
        gp = jnp.transpose(gp, (0, 3, 1, 2, 4))
        p_keep, p_send = halves(gp, group)
        keep = jnp.concatenate([v_keep, p_keep], -1)
        send = jnp.concatenate([v_send, p_send], -1)
    g_first, keep, send, dn_a, dn_b = together(g_first, keep, send, dn_a, dn_b)
    first_parts = spread_dp(g_first)
    g_got = swap(send, 0, 1)
    dn_got = swap(dn_b, 1, 0)
    out_last = swap(after(out_two[1], g_first), 2, 0)
    *first_parts, keep, g_got, dn_a, dn_got, out_last = together(
        *first_parts, keep, g_got, dn_a, dn_got, out_last
    )

    rest_parts = spread_dp(add_low(keep, g_got))
    dn_parts = spread_near(add_low(dn_a, dn_got))
    g_first = add_all(first_parts)
    ff_sum = after(ff_sum, g_got)
    sum_expand = ff_sum[own_hidden:]
    sum_expand = jnp.stack([sum_expand[:, :slots], sum_expand[:, slots:]])
    expand_send = sum_expand.reshape(plane, own_rows, slots)
    shrink_out = adam_update(
        shrink_weight,
        shrink_first,
        shrink_second,
        ff_sum[:own_hidden].astype(F32),
        matrix_rate,
        matrix_decay,
    )
    *rest_parts, dn_0, dn_1, dn_2, dn_3, expand_send, shrink_0, shrink_1, shrink_2 = together(
        *rest_parts, *dn_parts, expand_send, *shrink_out
    )
    shrink_out = (shrink_0, shrink_1, shrink_2)
    g_rest = add_all(rest_parts)

    sum_expand = lax.all_to_all(expand_send, PLANE, split_axis=0, concat_axis=0, tiled=True)
    block_out = mixed + (out_two[0].astype(F32) + out_last.astype(F32)) + bias_shrink

    g_all = jnp.concatenate([g_first, g_rest[:, :, : group + small_rows]], -1).astype(BF16)
    picked = [lax.dynamic_index_in_dim(g_all, seq ^ k, 0, keepdims=False) for k in range(4)]
    picked = jnp.stack([picked[0]] + [swap(picked[k], k, 0) for k in range(1, 4)]).astype(F32)
    g_all = [lax.dynamic_index_in_dim(picked, seq ^ k, 0, keepdims=False) for k in range(4)]
    g_all = jnp.stack(g_all)
    sum_proj = jnp.transpose(g_rest[:, :, 256:], (1, 0, 2)).reshape(own_rows, width)
    sum_small = jnp.sum(picked[:, :, 3 * group :], 0).T
    sum_qkv = jnp.transpose(
        g_all[:, :, : 3 * group].reshape(seq_count, own_rows, 3, group), (1, 2, 0, 3)
    ).reshape(own_rows, 3 * width)
    sum_expand = jnp.transpose(
        sum_expand.reshape(plane, own_rows, dp_count, own_hidden), (1, 2, 0, 3)
    ).reshape(own_rows, hidden).astype(F32)

    d_normed_one = add_all((dn_0, dn_1, dn_2, dn_3))
    unit, inverse = norm_parts(tokens.astype(F32))
    token_grad = d_mixed + norm_pull(unit, inverse, gain_one, d_normed_one)

    qkv_out = adam_update(
        qkv_weight, qkv_first, qkv_second, sum_qkv, matrix_rate, matrix_decay
    )
    proj_out = adam_update(
        proj_weight, proj_first, proj_second, sum_proj, matrix_rate, matrix_decay
    )
    expand_out = adam_update(
        expand_weight, expand_first, expand_second, sum_expand, matrix_rate, matrix_decay
    )
    small_out = adam_update(
        small_params, small_first, small_second, sum_small, small_rate, 0.0
    )
    return (block_out, token_grad, *qkv_out, *proj_out, *expand_out, *shrink_out, *small_out)


def solution(mesh):
    by_rows = P(ALL, None)
    by_columns = P(None, ALL)
    state = (by_rows,) * 4 + (by_columns,)
    return jax.shard_map(
        shards,
        mesh=mesh,
        in_specs=(by_rows, by_rows) + state * 3,
        out_specs=(by_rows,) * 14 + (by_columns,) * 3,
        check_vma=False,
    )
```
